256 devices in a mesh: grp: 32 (over x_hi, z, core), blk: 8 (over y, x_lo).
Axes of the slice: x: 4 (x_hi: 2, x_lo: 2; x = x_hi * 2 + x_lo), y: 4, z: 8, core: 2. Of those that a mesh axis runs over, the one named last changes fastest.
Arguments:
- q_latent: bfloat16 [256, 2, 64, 512], P(('grp', 'blk')), may hold values from -13 to 13
- q_rope: bfloat16 [256, 2, 4096], P(('grp', 'blk')), may hold values from -6 to 6
- prefix_latent: bfloat16 [32, 16384, 512], P('grp', 'blk'), may hold values from -6 to 6
- prefix_rope: bfloat16 [32, 64, 16384], P('grp', None, 'blk'), may hold values from -6 to 6
- suffix_latent: bfloat16 [256, 2048, 512], P(('grp', 'blk')), may hold values from -6 to 6
- suffix_rope: bfloat16 [256, 64, 2048], P(('grp', 'blk')), may hold values from -6 to 6
- prefix_of: int32 [8, 32, 1], P('blk'), may hold values from 0 to 31; in each aligned block of 32 rows (0 to 31, 32 to 63, ..., all dimensions but the last counted through in order) at most 2 rows name the same one
- suffix_len: int32 [256], P(('grp', 'blk')), may hold values from 1 to 2046, 261888 in all
Outputs:
- attended: bfloat16 [256, 2, 64, 512], P(('grp', 'blk'))
The draws below stay inside these ranges and needn't reach their ends.
Inputs may be any that keep to these rules, and one draw needn't show every extreme that they name: `prefix_of`: among the 32 requests of one blk index b, at most 2 name the same holder group.
All inputs are finite; a program needn't handle non-finite values. No bound on the sum of `suffix_len` on one device may be relied on, other than what follows from the above.
Results may differ from the reference program's by a relative error of at most 0.01.
Values may be sent and summed in bfloat16 or wider, within the bound.
No kernel may reach another device: no remote copies, remote signals or barrier semaphores. Data moves between devices by JAX's collectives and lax.ppermute only.
A program may use at most 64 MiB of HBM per device.

```python
import math
import jax
import jax.numpy as jnp
import numpy as np
from jax import lax

LATENT = 512
ROPE = 64
HEADS = 64
QK_DIM = 192
STEPS = 2
MOST = 2
SUF_MAX = 2048
REQUESTS = 256
PREFIX = 16384
N_GRP = 32
N_BLK = 8


def cache_values(key, shape):
    values = jnp.clip(jax.random.normal(key, shape, jnp.float32), -6.0, 6.0)
    return values.astype(jnp.bfloat16)


def draw_prefix_latent(key, part):
    key = jax.random.fold_in(key, 11)
    return cache_values(key, (N_GRP, PREFIX, LATENT))


def draw_suffix_latent(key, part):
    key = jax.random.fold_in(key, 12)
    return cache_values(key, (REQUESTS, SUF_MAX, LATENT))


def draw_q_latent(key, part):
    key = jax.random.fold_in(key, 13)
    shape = (REQUESTS, STEPS, HEADS, LATENT)
    values = jnp.clip(jax.random.normal(key, shape, jnp.float32), -6.0, 6.0)
    return values.astype(jnp.bfloat16)


def block_levels(rng, dims, pieces, low, top_value):
    def one(position, shards_of):
        heights = jax.random.uniform(jax.random.fold_in(jax.random.fold_in(rng, 6), position), (shards_of,), jnp.float32, low / len(pieces), top_value / len(pieces))
        return jnp.repeat(jnp.exp(heights), dims[position] // shards_of).reshape((-1,) + (1,) * (len(dims) - position - 1))

    gain = one(*pieces[0])
    for cut in pieces[1:]:
        gain = gain * one(*cut)
    return gain


def split_up(number_of, total, bound, skew):
    loads = [(1 << 20) // math.isqrt(grade ** skew) + 1 for grade in range(2, number_of + 1)]
    spare, counts = total - bound - (number_of - 1), [1] * (number_of - 1)
    while spare > 0:
        candidates = [i for i in range(number_of - 1) if counts[i] < bound]
        mass, left = sum([loads[i] for i in candidates]), spare
        for i in candidates:
            addition = min(bound - counts[i], max(1, left * loads[i] // mass), spare)
            counts[i] = counts[i] + addition
            spare = spare - addition
    return np.array([bound] + counts)


def ragged_sizes(stream_key, count, total, bound, slope):
    if count == 2:
        one = jax.random.randint(stream_key, (), max(1, total - bound), min(bound, total - 1) + 1)
        return jnp.stack([one, total - one])
    tallies = jnp.asarray(split_up(count, total, bound, slope), jnp.int32)
    couples = (count - 1) // 2
    source_of, sink = tallies[1:1 + 2 * couples:2], tallies[2:2 + 2 * couples:2]
    slack = jnp.minimum(source_of - 1, bound - sink)
    moved = jax.random.randint(jax.random.fold_in(stream_key, 1), (couples,), 0, 1 << 20) % (slack + 1)
    tallies = tallies.at[1:1 + 2 * couples:2].set(source_of - moved).at[2:2 + 2 * couples:2].set(sink + moved)
    return tallies[jax.random.permutation(jax.random.fold_in(stream_key, 2), count)]


def shared_out(own_key, own, number, rows, count, top, bound, skew):
    order = jax.random.permutation(own_key, count)
    heavy_load, ordinary = shares(count, rows * top, bound, skew, True), shares(count, rows * top, bound, skew, False)
    places = jnp.arange(count)

    def named(tallies, rotation):
        used = int((tallies > 0).sum())
        fixed = max(1, used // 4)
        moved = fixed + (places - fixed + rotation * (used - fixed)) % max(1, count - fixed)
        return jnp.zeros((count,), jnp.int32).at[order[jnp.where(places < fixed, places, moved)]].set(jnp.asarray(tallies, jnp.int32))

    tallies = jnp.where(number % 4 == 0, named(heavy_load, number // 4), named(ordinary, number - number // 4 - 1))
    mixed = jax.random.permutation(jax.random.fold_in(own, 3), count)
    giver, receiver = mixed[0:count // 2 * 2:2], mixed[1:count // 2 * 2:2]
    margin = jnp.minimum(tallies[giver] - 1, bound - tallies[receiver]) // 2
    margin = jnp.where((giver == order[0]) | (receiver == order[0]) | (tallies[receiver] == 0), 0, jnp.maximum(margin, 0))
    moved = jax.random.randint(jax.random.fold_in(own, 4), (count // 2,), 0, 1 << 20) % (margin + 1)
    tallies = tallies.at[giver].add(-moved).at[receiver].add(moved)
    labels = jnp.searchsorted(jnp.cumsum(tallies), jnp.arange(rows * top), side="right").astype(jnp.int32)
    table = labels.reshape(top, rows).T
    table = table[jax.random.permutation(jax.random.fold_in(own, 1), rows)]
    rotation = jax.random.randint(jax.random.fold_in(own, 2), (rows, 1), 0, top)
    return jnp.take_along_axis(table, (jnp.arange(top)[None, :] + rotation) % top, axis=1)


def shares(number_of, total, most, skew, full):
    portions = [(1 << 20) // math.isqrt(rank ** skew) + 1 for rank in range(1, number_of + 1)]
    largest = most if full else min(most, max(-(-total // number_of), total * portions[0] // sum(portions)))
    least = 1 if total - largest >= number_of - 1 else 0
    holding, rest = [largest] + [least] * (number_of - 1), total - largest - least * (number_of - 1)
    while rest > 0:
        candidates = [i for i in range(1, number_of) if holding[i] < largest] or [i for i in range(1, number_of) if holding[i] < most]
        whole, budget = sum([portions[i] for i in candidates]), rest
        for i in candidates:
            addition = min(most - holding[i], max(1, budget * portions[i] // whole), rest)
            holding[i] = holding[i] + addition
            rest = rest - addition
    return np.array(holding)


def normal_values(own_key, dims, deviation, most, cuts=(), held_as=jnp.bfloat16):
    entries = jax.random.normal(own_key, dims, jnp.float32) * deviation
    if len(cuts) > 0:
        entries = block_levels(own_key, dims, cuts, -0.22, 0.18) * entries
    return jnp.clip(entries, min=-most, max=most).astype(held_as)


def setup_inputs(seed: int = 0) -> dict:
    key_of = jax.random.split(jax.random.key(seed), 9)
    q_latent = draw_q_latent(jax.random.fold_in(key_of[8], 71), 0)
    q_rope = normal_values(key_of[1], (REQUESTS, STEPS, HEADS * ROPE), 1.0, 6.0, ((0, 256),))
    prefix_latent = draw_prefix_latent(jax.random.fold_in(key_of[8], 71), 0)
    prefix_rope = normal_values(key_of[3], (N_GRP, ROPE, PREFIX), 1.0, 6.0, ((0, 32), (2, 8)))
    suffix_latent = draw_suffix_latent(jax.random.fold_in(key_of[8], 71), 0)
    suffix_rope = normal_values(key_of[5], (REQUESTS, ROPE, SUF_MAX), 1.0, 6.0, ((0, 256),))
    prefix_of_keys = jax.random.split(jax.random.fold_in(key_of[6], 1), N_BLK * N_GRP // N_GRP)
    prefix_of_turns = jax.random.permutation(jax.random.fold_in(key_of[6], 3), N_BLK * N_GRP // N_GRP)
    prefix_of = jax.vmap(lambda own, number: shared_out(jax.random.fold_in(key_of[6], 2), own, number, N_GRP, N_GRP, 1, MOST, 2))(prefix_of_keys, prefix_of_turns).reshape((N_BLK, N_GRP, 1))
    suffix_len = ragged_sizes(key_of[7], REQUESTS, REQUESTS * (SUF_MAX - STEPS) // 2, SUF_MAX - STEPS, 2).astype(jnp.int32)
    return dict(q_latent=q_latent, q_rope=q_rope, prefix_latent=prefix_latent, prefix_rope=prefix_rope, suffix_latent=suffix_latent, suffix_rope=suffix_rope, prefix_of=prefix_of, suffix_len=suffix_len)


def softmax_part(q_lat, q_rot, keys, key_rope, valid):
    scale = QK_DIM ** -0.5
    scores = jnp.dot(q_lat, keys.T, preferred_element_type=jnp.float32)
    scores = (scores + jnp.dot(q_rot, key_rope, preferred_element_type=jnp.float32)) * scale
    scores = jnp.where(valid, scores, -1e30)
    top = jnp.max(scores, axis=1)
    weights = jnp.exp(scores - top[:, None])
    total = jnp.sum(weights, axis=1)
    mixed = jnp.dot(weights.astype(jnp.bfloat16), keys, preferred_element_type=jnp.float32) / total[:, None]
    return mixed, top + jnp.log(total)


def reference(q_latent, q_rope, prefix_latent, prefix_rope, suffix_latent, suffix_rope, prefix_of, suffix_len):
    rows = STEPS * HEADS
    step_of = (jnp.arange(rows, dtype=jnp.int32) // HEADS).astype(jnp.int32)
    token_positions = jnp.arange(SUF_MAX, dtype=jnp.int32)
    every_valid = jnp.ones((1, PREFIX), dtype=bool)

    def one(request):
        holder = prefix_of[request % N_BLK, request // N_BLK, 0]
        q_lat = q_latent[request].reshape(rows, LATENT)
        q_rot = q_rope[request].reshape(rows, ROPE)
        keys = lax.dynamic_index_in_dim(prefix_latent, holder, 0, keepdims=False)
        key_rope = lax.dynamic_index_in_dim(prefix_rope, holder, 0, keepdims=False)
        pre_out, prefix_log_sum_exp = softmax_part(q_lat, q_rot, keys, key_rope, every_valid)
        pre_out = lax.optimization_barrier(pre_out.astype(jnp.bfloat16)).astype(jnp.float32)
        limit = (suffix_len[request] + step_of + 1).astype(jnp.int32)
        valid = token_positions[None, :] < limit[:, None]
        suffix_output, suf_lse = softmax_part(q_lat, q_rot, suffix_latent[request], suffix_rope[request], valid)
        top = jnp.maximum(prefix_log_sum_exp, suf_lse)
        w_pre = jnp.exp(prefix_log_sum_exp - top)
        w_suf = jnp.exp(suf_lse - top)
        mixed = (w_pre[:, None] * pre_out + w_suf[:, None] * suffix_output) / (w_pre + w_suf)[:, None]
        return mixed.astype(jnp.bfloat16).reshape(STEPS, HEADS, LATENT)

    return lax.map(one, jnp.arange(REQUESTS, dtype=jnp.int32))
```

```python
import functools
import math

import jax
import jax.numpy as jnp
from jax import lax
from jax.experimental import pallas as pl
from jax.experimental.pallas import tpu as pltpu
from jax.sharding import Mesh, PartitionSpec as P

QK_DIM = 192
SCALE = QK_DIM**-0.5
LOG2E = math.log2(math.e)
BF = jnp.bfloat16
F32 = jnp.float32
AXES = ("xh", "z", "c", "y", "xl")
NZ, NY = 8, 4
HEADS, LATENT, ROPE = 64, 512, 64
WIDE = 128
COLS = LATENT // WIDE
LAT_ROWS = COLS * HEADS
Q_ROWS = LAT_ROWS + HEADS // 2
PAIR_ROWS = 2 * LAT_ROWS + 16
OUT_ROWS = LAT_ROWS + 16
NT = (((1,), (1,)), ((), ()))

SMEM = pl.BlockSpec(memory_space=pltpu.SMEM)
VMEM = pl.BlockSpec(memory_space=pltpu.VMEM)

T_ROUTE, T_MERGE_C, T_MERGE_X, T_BACK, T_PICK = 0, 8, 12, 16, 24


def call(kernel, outs, ints, arrays, flops=0, bytes_accessed=0, exps=0):
    single = not isinstance(outs, (list, tuple))
    specs = jax.tree.map(lambda _: VMEM, outs)
    return pl.pallas_call(
        kernel,
        out_shape=outs,
        in_specs=[SMEM] * len(ints) + [VMEM] * len(arrays),
        out_specs=VMEM if single else specs,
        compiler_params=pltpu.CompilerParams(vmem_limit_bytes=48 * 1024 * 1024),
        cost_estimate=pl.CostEstimate(
            flops=flops, bytes_accessed=bytes_accessed, transcendentals=exps
        ),
    )(*ints, *arrays)


def shaped(*shape, dtype=BF):
    return jax.ShapeDtypeStruct(shape, dtype)


def along(x, axis, distance):
    n = lax.axis_size(axis)
    return lax.ppermute(x, axis, [(i, (i + distance) % n) for i in range(n)])


def across(x, flip_xh, flip_xl):
    pairs = [
        (2 * i + j, 2 * (i ^ flip_xh) + (j ^ flip_xl)) for i in range(2) for j in range(2)
    ]
    return lax.ppermute(x, ("xh", "xl"), pairs)


def ranks(dest):
    ids = jnp.arange(dest.shape[0], dtype=jnp.int32)
    before = (ids[None, :] < ids[:, None]) & (dest[None, :] == dest[:, None])
    return jnp.sum(before.astype(jnp.int32), axis=1)


def sources(dest, rank, holders, slots):
    ids = jnp.arange(dest.shape[0], dtype=jnp.int32)
    match = (dest[None, :] == holders[:, None]) & (rank[None, :] == slots[:, None])
    return jnp.sum(jnp.where(match, ids[None, :] + 1, 0), axis=1) - 1


def table(dest, other_dest, xh, z, c):
    eight = jnp.arange(8, dtype=jnp.int32)
    cr, xr, slot = eight // 4, (eight // 2) % 2, eight % 2
    rank, other_rank = ranks(dest), ranks(other_dest)
    me = (xh * NZ + z) * 2 + c
    src = sources(dest, rank, ((xh ^ xr) * NZ + z) * 2 + (c ^ cr), slot)
    here = (src >= 0) & (src // (2 * NZ) == xh) & (src % 2 == c)
    route = jnp.where(here, (z - (src // 2) % NZ) % NZ, 0)
    merge_c = (src[:4] % 2 == c).astype(jnp.int32)
    own_x = src[:2] // (2 * NZ) == xh
    other = sources(other_dest, other_rank, jnp.full((2,), me), eight[:2])
    other_x = other // (2 * NZ) == xh
    merge_x = jnp.concatenate([own_x, other_x]).astype(jnp.int32)
    roots = (xh * NZ + (z + eight) % NZ) * 2 + c
    ids = jnp.arange(dest.shape[0], dtype=jnp.int32)
    take = lambda values: jnp.sum(jnp.where(roots[:, None] == ids[None, :], values[None], 0), axis=1)
    h, r = take(dest), take(rank)
    back = jnp.where((h // 2) % NZ == z, ((h % 2) ^ c) * 4 + ((h // (2 * NZ)) ^ xh) * 2 + r, 0)
    pick = jnp.stack([(z - (h[0] // 2) % NZ) % NZ, r[0]])
    return jnp.concatenate([route, merge_c, merge_x, back, pick]).astype(jnp.int32)


def route_kernel(t, *refs):
    units, (keep, send) = refs[:NZ], refs[NZ:]
    for slot in range(8):
        out = (keep if slot < 4 else send).at[slot % 4]
        for d in range(NZ):

            @pl.when(t[T_ROUTE + slot] == d)
            def _():
                out[...] = units[d][...]


def either(flag, out, a, b):
    @pl.when(flag == 1)
    def _():
        out[...] = a[...]

    @pl.when(flag != 1)
    def _():
        out[...] = b[...]


def merge_c_kernel(t, keep, got, near, far):
    for xr in range(2):
        for r in range(2):
            k = 2 * xr + r
            out = (far if xr else near).at[r]
            either(t[T_MERGE_C + k], out, keep.at[k], got.at[k])


def merge_x_kernel(t, near, from_xl, from_xh, from_both, out):
    for r in range(2):
        either(t[T_MERGE_X + r], out.at[r], near.at[r], from_xh.at[r])
        either(t[T_MERGE_X + 2 + r], out.at[2 + r], from_xl.at[r], from_both.at[r])


def queries_of(units):
    lat, rot = [], []
    lanes = lax.broadcasted_iota(jnp.int32, (HEADS // 2, WIDE), 1)
    for u in units:
        lat.append(
            jnp.concatenate([u[HEADS * j : HEADS * (j + 1)] for j in range(COLS)], axis=1)
        )
        pair = u[LAT_ROWS:Q_ROWS]
        zero = jnp.zeros_like(pair)
        rot += [jnp.where(lanes < ROPE, pair, zero), jnp.where(lanes < ROPE, zero, pair)]
    return jnp.concatenate(lat, axis=0), jnp.concatenate(rot, axis=0)


def prefix_kernel(q0, q1, q2, q3, keys, rope, o0, o1, o2, o3, rope2):
    rope2[:ROPE] = rope[...]
    rope2[ROPE:] = rope[...]
    for q, o in ((q0, o0), (q1, o1), (q2, o2), (q3, o3)):
        lat, rot = queries_of([q[u] for u in range(4)])
        s = lax.dot_general(lat, keys[...], NT, preferred_element_type=F32)
        s = s + jnp.dot(rot, rope2[...], preferred_element_type=F32)
        top = jnp.max(s, axis=1, keepdims=True)
        w = jnp.exp2((s - top) * (SCALE * LOG2E))
        total = jnp.sum(w, axis=1, keepdims=True)
        out = jnp.dot(w.astype(BF), keys[...], preferred_element_type=F32)
        out = (out / total).astype(BF)
        lse = top * SCALE + jnp.log(total)
        flat = jnp.transpose(jnp.broadcast_to(lse, (4 * HEADS, WIDE)))
        for u in range(4):
            for j in range(COLS):
                at = (u % 2) * LAT_ROWS + j * HEADS
                o[u // 2, at : at + HEADS] = out[
                    u * HEADS : (u + 1) * HEADS, j * WIDE : (j + 1) * WIDE
                ]
        for t in range(2):
            o[t, 2 * LAT_ROWS :] = in_thirds(flat[0:1, t * WIDE : (t + 1) * WIDE])


def in_thirds(row):
    high = row.astype(BF).astype(F32)
    mid = (row - high).astype(BF).astype(F32)
    low = row - high - mid
    place = lax.broadcasted_iota(jnp.int32, (16, WIDE), 0)
    block = jnp.where(place == 0, high, jnp.where(place == 1, mid, jnp.where(place == 2, low, 0.0)))
    return block.astype(BF)


def from_thirds(block):
    block = block.astype(F32)
    return block[0:1] + block[1:2] + block[2:3]


def down(row):
    return jnp.transpose(jnp.broadcast_to(row, (WIDE, WIDE)))


def merge_parts(parts, out):
    lses = [from_thirds(p[2 * LAT_ROWS :]) for p in parts]
    top = functools.reduce(jnp.maximum, lses)
    shares = [jnp.exp(x - top) for x in lses]
    total = functools.reduce(jnp.add, shares)
    weights = [down(x / total) for x in shares]
    for r in range(2):
        ws = [w[r * HEADS : (r + 1) * HEADS] for w in weights]
        for j in range(COLS):
            at = r * LAT_ROWS + j * HEADS
            mixed = [w * p[at : at + HEADS].astype(F32) for w, p in zip(ws, parts)]
            out[at : at + HEADS] = functools.reduce(jnp.add, mixed).astype(BF)
    out[2 * LAT_ROWS :] = in_thirds(top + jnp.log(total))


def merge_y_kernel(p0, p1, p2, p3, near, far):
    for t, out in ((0, near), (1, far)):
        merge_parts([p.at[t] for p in (p0, p1, p2, p3)], out)


def merge_xl_kernel(near, from_xl, from_xh, from_both, out):
    merge_parts([near, from_xl], out.at[0])
    merge_parts([from_xh, from_both], out.at[1])


def back_kernel(t, own, got, *outs):
    for d in range(NZ):
        for k in range(8):

            @pl.when(t[T_BACK + d] == k)
            def _():
                pair = (got if k // 4 else own).at[(k // 2) % 2]
                at = (k % 2) * LAT_ROWS
                outs[d][:LAT_ROWS] = pair[at : at + LAT_ROWS]
                outs[d][LAT_ROWS:] = pair[2 * LAT_ROWS :]


def suffix_kernel(length, units, keys, rope, out, out_lse, rope2):
    rope2[:ROPE] = rope[...]
    rope2[ROPE:] = rope[...]
    lat, rot = queries_of([units[0], units[1]])
    s = lax.dot_general(lat, keys[...], NT, preferred_element_type=F32)
    s = (s + jnp.dot(rot, rope2[...], preferred_element_type=F32)) * SCALE
    position = lax.broadcasted_iota(jnp.int32, s.shape, 1)
    step = lax.broadcasted_iota(jnp.int32, s.shape, 0) // HEADS
    s = jnp.where(position < length[0] + step + 1, s, -1e30)
    top = jnp.max(s, axis=1, keepdims=True)
    w = jnp.exp(s - top)
    total = jnp.sum(w, axis=1, keepdims=True)
    out[...] = jnp.dot(w.astype(BF), keys[...], preferred_element_type=F32) / total
    out_lse[...] = jnp.broadcast_to(top + jnp.log(total), out_lse.shape)


def final_kernel(step, t, *refs):
    units, (suffix, suffix_lse, out, held) = refs[:NZ], refs[NZ:]
    for d in range(NZ):

        @pl.when(t[T_PICK] == d)
        def _():
            held[...] = units[d][...]

    lses = down(from_thirds(held[LAT_ROWS:]))
    pre = jnp.where(t[T_PICK + 1] == 1, lses[HEADS:], lses[:HEADS])
    rows = slice(step * HEADS, (step + 1) * HEADS)
    suf = suffix_lse[rows]
    top = jnp.maximum(pre, suf)
    w_pre, w_suf = jnp.exp(pre - top), jnp.exp(suf - top)
    total = w_pre + w_suf
    for j in range(COLS):
        got = held[j * HEADS : (j + 1) * HEADS].astype(F32)
        cols = slice(j * WIDE, (j + 1) * WIDE)
        out[:, cols] = ((w_pre * got + w_suf * suffix[rows, cols]) / total).astype(BF)


def body(
    q_latent, q_rope, prefix_latent, prefix_rope, suffix_latent, suffix_rope, prefix_of, suffix_len
):
    steps = q_latent.shape[1]
    xh, z, c = (lax.axis_index(a) for a in ("xh", "z", "c"))
    lat = q_latent[0].reshape(steps, HEADS, COLS, WIDE).transpose(0, 2, 1, 3)
    rot = q_rope[0].reshape(steps, 2, HEADS // 2, ROPE).transpose(0, 2, 1, 3)
    units = jnp.concatenate(
        [lat.reshape(steps, LAT_ROWS, WIDE), rot.reshape(steps, HEADS // 2, WIDE)], axis=1
    )
    dest = prefix_of[0, :, 0]
    t = table(dest, across(dest, 0, 1), xh, z, c)
    keys, rope = prefix_latent[0], prefix_rope[0]
    positions = keys.shape[0]

    rows = steps * HEADS
    suffix, suffix_lse = pl.pallas_call(
        suffix_kernel,
        out_shape=[shaped(rows, LATENT, dtype=F32), shaped(rows, WIDE, dtype=F32)],
        in_specs=[SMEM, VMEM, VMEM, VMEM],
        out_specs=[VMEM, VMEM],
        scratch_shapes=[pltpu.VMEM((2 * ROPE, positions), BF)],
        compiler_params=pltpu.CompilerParams(vmem_limit_bytes=48 * 1024 * 1024),
        cost_estimate=pl.CostEstimate(
            flops=2 * rows * 2048 * 1152, bytes_accessed=3 << 20, transcendentals=rows * 2048
        ),
    )(suffix_len, units, suffix_latent[0], suffix_rope[0])

    def chunk(step):
        own = units[step]
        heard = [own] + [along(own, "z", d) for d in range(1, NZ)]
        quad = shaped(4, Q_ROWS, WIDE)
        pair_q = shaped(2, Q_ROWS, WIDE)
        keep, send = call(route_kernel, [quad, quad], [t], heard, bytes_accessed=1 << 20)
        got = along(send, "c", 1)
        near, far = call(merge_c_kernel, [pair_q, pair_q], [t], [keep, got], bytes_accessed=1 << 20)
        mine = call(
            merge_x_kernel,
            quad,
            [t],
            [near, across(near, 0, 1), across(far, 1, 0), across(far, 1, 1)],
            bytes_accessed=1 << 20,
        )
        asked = [mine] + [along(mine, "y", d) for d in range(1, NY)]
        pairs = shaped(2, PAIR_ROWS, WIDE)
        parts = pl.pallas_call(
            prefix_kernel,
            out_shape=[pairs] * NY,
            in_specs=[VMEM] * (NY + 2),
            out_specs=[VMEM] * NY,
            scratch_shapes=[pltpu.VMEM((2 * ROPE, positions), BF)],
            compiler_params=pltpu.CompilerParams(vmem_limit_bytes=48 * 1024 * 1024),
            cost_estimate=pl.CostEstimate(
                flops=2 * 1024 * 2048 * 1152, bytes_accessed=6 << 20, transcendentals=1024 * 2048
            ),
        )(*asked, keys, rope)
        back = [parts[0]] + [along(parts[d], "y", -d) for d in range(1, NY)]
        pair = shaped(PAIR_ROWS, WIDE)
        p_near, p_far = call(merge_y_kernel, [pair, pair], [], back, bytes_accessed=1 << 20)
        both = call(
            merge_xl_kernel,
            pairs,
            [],
            [p_near, across(p_far, 0, 1), across(p_near, 1, 0), across(p_far, 1, 1)],
            bytes_accessed=1 << 20,
        )
        outs = call(
            back_kernel,
            [shaped(OUT_ROWS, WIDE)] * NZ,
            [t],
            [both, along(both, "c", 1)],
            bytes_accessed=1 << 20,
        )
        arrived = [outs[0]] + [along(outs[d], "z", d) for d in range(1, NZ)]
        return pl.pallas_call(
            functools.partial(final_kernel, step),
            out_shape=shaped(HEADS, LATENT),
            in_specs=[SMEM] + [VMEM] * (NZ + 2),
            out_specs=VMEM,
            scratch_shapes=[pltpu.VMEM((OUT_ROWS, WIDE), BF)],
            compiler_params=pltpu.CompilerParams(vmem_limit_bytes=48 * 1024 * 1024),
        )(t, *arrived, suffix, suffix_lse)

    return jnp.stack([chunk(step) for step in range(steps)])[None]


def solution(mesh):
    fine = Mesh(mesh.devices.reshape(2, NZ, 2, NY, 2), AXES)
    grp, blk = ("xh", "z", "c"), ("y", "xl")
    in_specs = (
        P(AXES, None, None, None),
        P(AXES, None, None),
        P(grp, blk, None),
        P(grp, None, blk),
        P(AXES, None, None),
        P(AXES, None, None),
        P(blk, None, None),
        P(AXES),
    )
    return jax.shard_map(
        body, mesh=fine, in_specs=in_specs, out_specs=P(AXES, None, None, None), check_vma=False
    )
```

```python
import functools
import math

import jax
import jax.numpy as jnp
from jax import lax
from jax.experimental import pallas as pl
from jax.experimental.pallas import tpu as pltpu
from jax.sharding import Mesh, PartitionSpec as P

QK_DIM = 192
SCALE = QK_DIM**-0.5
LOG2E = math.log2(math.e)
BF = jnp.bfloat16
F32 = jnp.float32
AXES = ("xh", "z", "c", "y", "xl")
NZ, NY = 8, 4
HEADS, LATENT, ROPE = 64, 512, 64
WIDE = 128
COLS = LATENT // WIDE
LAT_ROWS = COLS * HEADS
Q_ROWS = LAT_ROWS + HEADS // 2
PAIR_ROWS = 2 * LAT_ROWS + 16
OUT_ROWS = LAT_ROWS + 16
NT = (((1,), (1,)), ((), ()))

SMEM = pl.BlockSpec(memory_space=pltpu.SMEM)
VMEM = pl.BlockSpec(memory_space=pltpu.VMEM)

T_ROUTE, T_BACK, T_PICK = 0, 8, 16


def call(kernel, outs, ints, arrays, flops=0, bytes_accessed=0, exps=0):
    single = not isinstance(outs, (list, tuple))
    specs = jax.tree.map(lambda _: VMEM, outs)
    return pl.pallas_call(
        kernel,
        out_shape=outs,
        in_specs=[SMEM] * len(ints) + [VMEM] * len(arrays),
        out_specs=VMEM if single else specs,
        compiler_params=pltpu.CompilerParams(vmem_limit_bytes=48 * 1024 * 1024),
        cost_estimate=pl.CostEstimate(
            flops=flops, bytes_accessed=bytes_accessed, transcendentals=exps
        ),
    )(*ints, *arrays)


def shaped(*shape, dtype=BF):
    return jax.ShapeDtypeStruct(shape, dtype)


def along(x, axis, distance):
    n = lax.axis_size(axis)
    return lax.ppermute(x, axis, [(i, (i + distance) % n) for i in range(n)])


def across(x, flip_xh, flip_xl):
    pairs = [
        (2 * i + j, 2 * (i ^ flip_xh) + (j ^ flip_xl)) for i in range(2) for j in range(2)
    ]
    return lax.ppermute(x, ("xh", "xl"), pairs)


def ranks(dest):
    ids = jnp.arange(dest.shape[0], dtype=jnp.int32)
    before = (ids[None, :] < ids[:, None]) & (dest[None, :] == dest[:, None])
    return jnp.sum(before.astype(jnp.int32), axis=1)


def table(dest, xh, z, c):
    ids = jnp.arange(dest.shape[0], dtype=jnp.int32)
    eight = jnp.arange(8, dtype=jnp.int32)
    cr, xr, slot = eight // 4, (eight // 2) % 2, eight % 2
    rank = ranks(dest)
    holders = ((xh ^ xr) * NZ + z) * 2 + (c ^ cr)
    in_ring = (ids // (2 * NZ) == xh) & (ids % 2 == c)
    match = (dest[None, :] == holders[:, None]) & (rank[None, :] == slot[:, None]) & in_ring[None, :]
    route = jnp.sum(jnp.where(match, (ids[None, :] // 2) % NZ + 1, 0), axis=1) - 1
    roots = (xh * NZ + eight) * 2 + c
    root = roots[:, None] == ids[None, :]
    h = jnp.sum(jnp.where(root, dest[None], 0), axis=1)
    r = jnp.sum(jnp.where(root, rank[None], 0), axis=1)
    place = ((h % 2) ^ c) * 4 + ((h // (2 * NZ)) ^ xh) * 2 + r
    back = jnp.where((h // 2) % NZ == z, place, -1)
    mine = eight == z
    pick = jnp.stack([jnp.sum(jnp.where(mine, (h // 2) % NZ, 0)), jnp.sum(jnp.where(mine, r, 0))])
    return jnp.concatenate([route, back, pick]).astype(jnp.int32)


def route_kernel(first, t, heard, keep, send):
    for slot in range(8):
        out = (keep if slot < 4 else send).at[slot % 4]
        source = t[T_ROUTE + slot]

        @pl.when(source >= 0)
        def _():
            out[...] = heard[source, first : first + Q_ROWS]

        @pl.when(source < 0)
        def _():
            out[...] = jnp.zeros(out.shape, BF)


def merge_c_kernel(keep, got, near, far):
    for r in range(2):
        near[r] = keep[r] + got[r]
        far[r] = keep[2 + r] + got[2 + r]


def merge_x_kernel(near, from_xl, from_xh, from_both, out):
    for r in range(2):
        out[r] = near[r] + from_xh[r]
        out[2 + r] = from_xl[r] + from_both[r]


def queries_of(units):
    lat, rot = [], []
    lanes = lax.broadcasted_iota(jnp.int32, (HEADS // 2, WIDE), 1)
    for u in units:
        lat.append(
            jnp.concatenate([u[HEADS * j : HEADS * (j + 1)] for j in range(COLS)], axis=1)
        )
        pair = u[LAT_ROWS:Q_ROWS]
        zero = jnp.zeros_like(pair)
        rot += [jnp.where(lanes < ROPE, pair, zero), jnp.where(lanes < ROPE, zero, pair)]
    return jnp.concatenate(lat, axis=0), jnp.concatenate(rot, axis=0)


def prefix_kernel(q0, q1, q2, q3, keys, rope, o0, o1, o2, o3, rope2):
    rope2[:ROPE] = rope[...]
    rope2[ROPE:] = rope[...]
    for q, o in ((q0, o0), (q1, o1), (q2, o2), (q3, o3)):
        lat, rot = queries_of([q[u] for u in range(4)])
        s = lax.dot_general(lat, keys[...], NT, preferred_element_type=F32)
        s = s + jnp.dot(rot, rope2[...], preferred_element_type=F32)
        top = jnp.max(s, axis=1, keepdims=True)
        w = jnp.exp2((s - top) * (SCALE * LOG2E))
        total = jnp.sum(w, axis=1, keepdims=True)
        out = jnp.dot(w.astype(BF), keys[...], preferred_element_type=F32)
        out = (out / total).astype(BF)
        lse = top * SCALE + jnp.log(total)
        flat = jnp.transpose(jnp.broadcast_to(lse, (4 * HEADS, WIDE)))
        for u in range(4):
            for j in range(COLS):
                at = (u % 2) * LAT_ROWS + j * HEADS
                o[u // 2, at : at + HEADS] = out[
                    u * HEADS : (u + 1) * HEADS, j * WIDE : (j + 1) * WIDE
                ]
        for t in range(2):
            o[t, 2 * LAT_ROWS :] = in_thirds(flat[0:1, t * WIDE : (t + 1) * WIDE])


def in_thirds(row):
    high = row.astype(BF).astype(F32)
    mid = (row - high).astype(BF).astype(F32)
    low = row - high - mid
    place = lax.broadcasted_iota(jnp.int32, (16, WIDE), 0)
    block = jnp.where(place == 0, high, jnp.where(place == 1, mid, jnp.where(place == 2, low, 0.0)))
    return block.astype(BF)


def from_thirds(block):
    block = block.astype(F32)
    return block[0:1] + block[1:2] + block[2:3]


def down(row):
    return jnp.transpose(jnp.broadcast_to(row, (WIDE, WIDE)))


def merge_parts(parts, out):
    lses = [from_thirds(p[2 * LAT_ROWS :]) for p in parts]
    top = functools.reduce(jnp.maximum, lses)
    shares = [jnp.exp(x - top) for x in lses]
    total = functools.reduce(jnp.add, shares)
    weights = [down(x / total) for x in shares]
    for r in range(2):
        ws = [w[r * HEADS : (r + 1) * HEADS] for w in weights]
        for j in range(COLS):
            at = r * LAT_ROWS + j * HEADS
            mixed = [w * p[at : at + HEADS].astype(F32) for w, p in zip(ws, parts)]
            out[at : at + HEADS] = functools.reduce(jnp.add, mixed).astype(BF)
    out[2 * LAT_ROWS :] = in_thirds(top + jnp.log(total))


def merge_y_kernel(p0, p1, p2, p3, near, far):
    for t, out in ((0, near), (1, far)):
        merge_parts([p.at[t] for p in (p0, p1, p2, p3)], out)


def merge_xl_kernel(near, from_xl, from_xh, from_both, out):
    merge_parts([near, from_xl], out.at[0])
    merge_parts([from_xh, from_both], out.at[1])


def back_kernel(t, own, got, out):
    for d in range(NZ):
        place = t[T_BACK + d]
        for k in range(8):

            @pl.when(place == k)
            def _():
                pair = (got if k // 4 else own).at[(k // 2) % 2]
                at = (k % 2) * LAT_ROWS
                out[d, :LAT_ROWS] = pair[at : at + LAT_ROWS]
                out[d, LAT_ROWS:] = pair[2 * LAT_ROWS :]

        @pl.when(place < 0)
        def _():
            out[d] = jnp.zeros((OUT_ROWS, WIDE), BF)


def suffix_kernel(length, units, keys, rope, out, out_lse, rope2):
    rope2[:ROPE] = rope[...]
    rope2[ROPE:] = rope[...]
    lat, rot = queries_of([units[0], units[1]])
    s = lax.dot_general(lat, keys[...], NT, preferred_element_type=F32)
    s = (s + jnp.dot(rot, rope2[...], preferred_element_type=F32)) * SCALE
    position = lax.broadcasted_iota(jnp.int32, s.shape, 1)
    step = lax.broadcasted_iota(jnp.int32, s.shape, 0) // HEADS
    s = jnp.where(position < length[0] + step + 1, s, -1e30)
    top = jnp.max(s, axis=1, keepdims=True)
    w = jnp.exp(s - top)
    total = jnp.sum(w, axis=1, keepdims=True)
    out[...] = jnp.dot(w.astype(BF), keys[...], preferred_element_type=F32) / total
    out_lse[...] = jnp.broadcast_to(top + jnp.log(total), out_lse.shape)


def final_kernel(step, t, units, suffix, suffix_lse, out):
    held = units.at[t[T_PICK] if units.shape[0] > 1 else 0]
    lses = down(from_thirds(held[LAT_ROWS:]))
    pre = jnp.where(t[T_PICK + 1] == 1, lses[HEADS:], lses[:HEADS])
    rows = slice(step * HEADS, (step + 1) * HEADS)
    suf = suffix_lse[rows]
    top = jnp.maximum(pre, suf)
    w_pre, w_suf = jnp.exp(pre - top), jnp.exp(suf - top)
    total = w_pre + w_suf
    for j in range(COLS):
        got = held[j * HEADS : (j + 1) * HEADS].astype(F32)
        cols = slice(j * WIDE, (j + 1) * WIDE)
        out[:, cols] = ((w_pre * got + w_suf * suffix[rows, cols]) / total).astype(BF)


def body(
    q_latent, q_rope, prefix_latent, prefix_rope, suffix_latent, suffix_rope, prefix_of, suffix_len
):
    steps = q_latent.shape[1]
    xh, z, c = (lax.axis_index(a) for a in ("xh", "z", "c"))
    lat = q_latent[0].reshape(steps, HEADS, COLS, WIDE).transpose(0, 2, 1, 3)
    rot = q_rope[0].reshape(steps, 2, HEADS // 2, ROPE).transpose(0, 2, 1, 3)
    units = jnp.concatenate(
        [lat.reshape(steps, LAT_ROWS, WIDE), rot.reshape(steps, HEADS // 2, WIDE)], axis=1
    )
    t = table(prefix_of[0, :, 0], xh, z, c)
    keys, rope = prefix_latent[0], prefix_rope[0]
    positions = keys.shape[0]

    rows = steps * HEADS
    suffix, suffix_lse = pl.pallas_call(
        suffix_kernel,
        out_shape=[shaped(rows, LATENT, dtype=F32), shaped(rows, WIDE, dtype=F32)],
        in_specs=[SMEM, VMEM, VMEM, VMEM],
        out_specs=[VMEM, VMEM],
        scratch_shapes=[pltpu.VMEM((2 * ROPE, positions), BF)],
        compiler_params=pltpu.CompilerParams(vmem_limit_bytes=48 * 1024 * 1024),
        cost_estimate=pl.CostEstimate(
            flops=2 * rows * 2048 * 1152, bytes_accessed=3 << 20, transcendentals=rows * 2048
        ),
    )(suffix_len, units, suffix_latent[0], suffix_rope[0])

    heard_all = lax.all_gather(units.reshape(steps * Q_ROWS, WIDE), "z")
    ahead = jnp.broadcast_to(units[0][None], (NZ, Q_ROWS, WIDE))
    heard_first = lax.all_to_all(ahead, "z", 0, 0, tiled=True)

    def chunk(step):
        heard, first = (heard_first, 0) if step == 0 else (heard_all, step * Q_ROWS)
        quad = shaped(4, Q_ROWS, WIDE)
        pair_q = shaped(2, Q_ROWS, WIDE)
        keep, send = call(
            functools.partial(route_kernel, first), [quad, quad], [t], [heard], bytes_accessed=1 << 20
        )
        got = along(send, "c", 1)
        near, far = call(merge_c_kernel, [pair_q, pair_q], [], [keep, got], bytes_accessed=1 << 20)
        mine = call(
            merge_x_kernel,
            quad,
            [],
            [near, across(near, 0, 1), across(far, 1, 0), across(far, 1, 1)],
            bytes_accessed=1 << 20,
        )
        asked = [mine] + [along(mine, "y", d) for d in range(1, NY)]
        pairs = shaped(2, PAIR_ROWS, WIDE)
        parts = pl.pallas_call(
            prefix_kernel,
            out_shape=[pairs] * NY,
            in_specs=[VMEM] * (NY + 2),
            out_specs=[VMEM] * NY,
            scratch_shapes=[pltpu.VMEM((2 * ROPE, positions), BF)],
            compiler_params=pltpu.CompilerParams(vmem_limit_bytes=48 * 1024 * 1024),
            cost_estimate=pl.CostEstimate(
                flops=2 * 1024 * 2048 * 1152, bytes_accessed=6 << 20, transcendentals=1024 * 2048
            ),
        )(*asked, keys, rope)
        back = [parts[0]] + [along(parts[d], "y", -d) for d in range(1, NY)]
        pair = shaped(PAIR_ROWS, WIDE)
        p_near, p_far = call(merge_y_kernel, [pair, pair], [], back, bytes_accessed=1 << 20)
        both = call(
            merge_xl_kernel,
            pairs,
            [],
            [p_near, across(p_far, 0, 1), across(p_near, 1, 0), across(p_far, 1, 1)],
            bytes_accessed=1 << 20,
        )
        out = call(
            back_kernel,
            shaped(NZ, OUT_ROWS, WIDE),
            [t],
            [both, along(both, "c", 1)],
            bytes_accessed=1 << 20,
        )
        if step == 0:
            arrived = lax.psum_scatter(out, "z", scatter_dimension=0, tiled=True)
        else:
            arrived = lax.all_to_all(out, "z", 0, 0, tiled=True)
        return call(
            functools.partial(final_kernel, step),
            shaped(HEADS, LATENT),
            [t],
            [arrived, suffix, suffix_lse],
            bytes_accessed=1 << 20,
        )

    return jnp.stack([chunk(step) for step in range(steps)])[None]


def solution(mesh):
    fine = Mesh(mesh.devices.reshape(2, NZ, 2, NY, 2), AXES)
    grp, blk = ("xh", "z", "c"), ("y", "xl")
    in_specs = (
        P(AXES, None, None, None),
        P(AXES, None, None),
        P(grp, blk, None),
        P(grp, None, blk),
        P(AXES, None, None),
        P(AXES, None, None),
        P(blk, None, None),
        P(AXES),
    )
    return jax.shard_map(
        body, mesh=fine, in_specs=in_specs, out_specs=P(AXES, None, None, None), check_vma=False
    )
```

```python
import functools
import math

import jax
import jax.numpy as jnp
from jax import lax
from jax.experimental import pallas as pl
from jax.experimental.pallas import tpu as pltpu
from jax.sharding import Mesh, PartitionSpec as P

QK_DIM = 192
SCALE = QK_DIM**-0.5
LOG2E = math.log2(math.e)
BF = jnp.bfloat16
F32 = jnp.float32
AXES = ("xh", "z", "c", "y", "xl")
NZ, NY = 8, 4
HEADS, LATENT, ROPE = 64, 512, 64
WIDE = 128
COLS = LATENT // WIDE
ROWS = 2 * HEADS
LAT_ROWS = COLS * ROWS
Q_ROWS = LAT_ROWS + HEADS
HALF = Q_ROWS // 2
OUT_ROWS = LAT_ROWS + 16
NT = (((1,), (1,)), ((), ()))

SMEM = pl.BlockSpec(memory_space=pltpu.SMEM)
VMEM = pl.BlockSpec(memory_space=pltpu.VMEM)

T_ROUTE, T_BACK, T_PICK = 0, 8, 16


def call(kernel, outs, ints, arrays, flops=0, bytes_accessed=0, exps=0):
    single = not isinstance(outs, (list, tuple))
    specs = jax.tree.map(lambda _: VMEM, outs)
    return pl.pallas_call(
        kernel,
        out_shape=outs,
        in_specs=[SMEM] * len(ints) + [VMEM] * len(arrays),
        out_specs=VMEM if single else specs,
        compiler_params=pltpu.CompilerParams(vmem_limit_bytes=48 * 1024 * 1024),
        cost_estimate=pl.CostEstimate(
            flops=flops, bytes_accessed=bytes_accessed, transcendentals=exps
        ),
    )(*ints, *arrays)


def shaped(*shape, dtype=BF):
    return jax.ShapeDtypeStruct(shape, dtype)


def along(x, axis, distance):
    n = lax.axis_size(axis)
    return lax.ppermute(x, axis, [(i, (i + distance) % n) for i in range(n)])


def across(x, flip_xh, flip_xl):
    pairs = [
        (2 * i + j, 2 * (i ^ flip_xh) + (j ^ flip_xl)) for i in range(2) for j in range(2)
    ]
    return lax.ppermute(x, ("xh", "xl"), pairs)


def ranks(dest):
    ids = jnp.arange(dest.shape[0], dtype=jnp.int32)
    before = (ids[None, :] < ids[:, None]) & (dest[None, :] == dest[:, None])
    return jnp.sum(before.astype(jnp.int32), axis=1)


def table(dest, xh, z, c):
    ids = jnp.arange(dest.shape[0], dtype=jnp.int32)
    eight = jnp.arange(8, dtype=jnp.int32)
    cr, xr, slot = eight // 4, (eight // 2) % 2, eight % 2
    rank = ranks(dest)
    holders = ((xh ^ xr) * NZ + z) * 2 + (c ^ cr)
    in_ring = (ids // (2 * NZ) == xh) & (ids % 2 == c)
    match = (dest[None, :] == holders[:, None]) & (rank[None, :] == slot[:, None]) & in_ring[None, :]
    distance = (z - ids // 2) % NZ
    route = jnp.sum(jnp.where(match, distance[None, :] + 1, 0), axis=1) - 1
    roots = (xh * NZ + eight) * 2 + c
    root = roots[:, None] == ids[None, :]
    h = jnp.sum(jnp.where(root, dest[None], 0), axis=1)
    r = jnp.sum(jnp.where(root, rank[None], 0), axis=1)
    place = ((h % 2) ^ c) * 4 + ((h // (2 * NZ)) ^ xh) * 2 + r
    back = jnp.where((h // 2) % NZ == z, place, -1)
    mine = eight == z
    pick = jnp.sum(jnp.where(mine, (h // 2) % NZ, 0))
    return jnp.concatenate([route, back, pick[None]]).astype(jnp.int32)


def old_row(n):
    return (n // 32) % 2 * HEADS + n % 32 * 2 + n // HEADS


def pack_kernel(lat, rot, out):
    shape = (ROWS, ROWS)
    new, old = (lax.broadcasted_iota(jnp.int32, shape, d) for d in (0, 1))
    order = jnp.where(old == old_row(new), 1.0, 0.0).astype(BF)
    rows = jnp.dot(order, lat[...], preferred_element_type=F32).astype(BF)
    for j in range(COLS):
        out[j * ROWS : (j + 1) * ROWS] = rows[:, j * WIDE : (j + 1) * WIDE]
    flat = rot[...].astype(F32)
    pairs = [
        flat[s : s + 1, j * WIDE : (j + 1) * WIDE] for s in range(2) for j in range(HEADS // 2)
    ]
    out[LAT_ROWS:] = jnp.concatenate(pairs, axis=0).astype(BF)


def relay_kernel(one_up, two_up, one_down, two_down, up, down):
    up[:Q_ROWS] = one_up[...]
    up[Q_ROWS:] = two_up[:HALF]
    down[:Q_ROWS] = one_down[...]
    down[Q_ROWS:] = two_down[HALF:]


def route_kernel(t, own, one_up, two_up, one_down, two_down, up, down, keep, send):
    whole = [own, one_up, two_up, up.at[:Q_ROWS], None, down.at[:Q_ROWS], two_down, one_down]
    for slot in range(8):
        out = (keep if slot < 4 else send).at[slot % 4]
        source = t[T_ROUTE + slot]
        for d in range(NZ):

            @pl.when(source == d)
            def _():
                if d == NZ // 2:
                    out[:HALF] = up[Q_ROWS:]
                    out[HALF:] = down[Q_ROWS:]
                else:
                    out[...] = whole[d][...]

        @pl.when(source < 0)
        def _():
            out[...] = jnp.zeros(out.shape, BF)


def merge_c_kernel(keep, got, near, far):
    for r in range(2):
        near[r] = keep[r] + got[r]
        far[r] = keep[2 + r] + got[2 + r]


def merge_x_kernel(near, from_xl, from_xh, from_both, out):
    for r in range(2):
        out[r] = near[r] + from_xh[r]
        out[2 + r] = from_xl[r] + from_both[r]


def queries_of(units):
    lat, rot = [], []
    lanes = lax.broadcasted_iota(jnp.int32, (HEADS, WIDE), 1)
    for u in units:
        lat.append(jnp.concatenate([u[ROWS * j : ROWS * (j + 1)] for j in range(COLS)], axis=1))
        pair = u[LAT_ROWS:]
        zero = jnp.zeros_like(pair)
        rot += [jnp.where(lanes < ROPE, pair, zero), jnp.where(lanes < ROPE, zero, pair)]
    return jnp.concatenate(lat, axis=0), jnp.concatenate(rot, axis=0)


def prefix_kernel(q, keys, rope, o, rope2):
    rope2[:ROPE] = rope[...]
    rope2[ROPE:] = rope[...]
    for first in (0, 2):
        lat, rot = queries_of([q[first], q[first + 1]])
        s = lax.dot_general(lat, keys[...], NT, preferred_element_type=F32)
        s = s + jnp.dot(rot, rope2[...], preferred_element_type=F32)
        top = jnp.max(s, axis=1, keepdims=True)
        w = jnp.exp2((s - top) * (SCALE * LOG2E))
        total = jnp.sum(w, axis=1, keepdims=True)
        out = jnp.dot(w.astype(BF), keys[...], preferred_element_type=F32)
        out = (out / total).astype(BF)
        lse = top * SCALE + jnp.log(total)
        flat = jnp.transpose(jnp.broadcast_to(lse, (2 * ROWS, WIDE)))
        for u in range(2):
            for j in range(COLS):
                o[first + u, j * ROWS : (j + 1) * ROWS] = out[
                    u * ROWS : (u + 1) * ROWS, j * WIDE : (j + 1) * WIDE
                ]
            o[first + u, LAT_ROWS:] = in_thirds(flat[0:1, u * ROWS : (u + 1) * ROWS])


def in_thirds(row):
    high = row.astype(BF).astype(F32)
    mid = (row - high).astype(BF).astype(F32)
    low = row - high - mid
    place = lax.broadcasted_iota(jnp.int32, (16, WIDE), 0)
    block = jnp.where(place == 0, high, jnp.where(place == 1, mid, jnp.where(place == 2, low, 0.0)))
    return block.astype(BF)


def from_thirds(block):
    block = block.astype(F32)
    return block[0:1] + block[1:2] + block[2:3]


def down(row):
    return jnp.transpose(jnp.broadcast_to(row, (WIDE, WIDE)))


def merge_parts(parts, out):
    lses = [from_thirds(p[LAT_ROWS:]) for p in parts]
    top = functools.reduce(jnp.maximum, lses)
    shares = [jnp.exp(x - top) for x in lses]
    total = functools.reduce(jnp.add, shares)
    weights = [down(x / total) for x in shares]
    for j in range(COLS):
        at = slice(j * ROWS, (j + 1) * ROWS)
        mixed = [w * p[at].astype(F32) for w, p in zip(weights, parts)]
        out[at] = functools.reduce(jnp.add, mixed).astype(BF)
    out[LAT_ROWS:] = in_thirds(top + jnp.log(total))


def merge_y_kernel(p0, p1, p2, p3, near, far):
    for k in range(4):
        merge_parts([p.at[k] for p in (p0, p1, p2, p3)], (far if k // 2 else near).at[k % 2])


def merge_xl_kernel(near, from_xl, from_xh, from_both, out):
    for r in range(2):
        merge_parts([near.at[r], from_xl.at[r]], out.at[r])
        merge_parts([from_xh.at[r], from_both.at[r]], out.at[2 + r])


def back_kernel(t, own, got, out):
    for d in range(NZ):
        place = t[T_BACK + d]

        @pl.when((place >= 0) & (place < 4))
        def _():
            out[d] = own[place]

        @pl.when(place >= 4)
        def _():
            out[d] = got[place - 4]

        @pl.when(place < 0)
        def _():
            out[d] = jnp.zeros((OUT_ROWS, WIDE), BF)


def suffix_kernel(length, unit, keys, rope, out, out_lse, rope2):
    rope2[:ROPE] = rope[...]
    rope2[ROPE:] = rope[...]
    lat, rot = queries_of([unit[...]])
    s = lax.dot_general(lat, keys[...], NT, preferred_element_type=F32)
    s = (s + jnp.dot(rot, rope2[...], preferred_element_type=F32)) * SCALE
    position = lax.broadcasted_iota(jnp.int32, s.shape, 1)
    step = lax.broadcasted_iota(jnp.int32, s.shape, 0) // (HEADS // 2) % 2
    s = jnp.where(position < length[0] + step + 1, s, -1e30)
    top = jnp.max(s, axis=1, keepdims=True)
    w = jnp.exp(s - top)
    total = jnp.sum(w, axis=1, keepdims=True)
    out[...] = jnp.dot(w.astype(BF), keys[...], preferred_element_type=F32) / total
    out_lse[...] = jnp.broadcast_to(top + jnp.log(total), out_lse.shape)


def final_kernel(t, units, suffix, suf, out):
    held = units.at[t[T_PICK]]
    pre = down(from_thirds(held[LAT_ROWS:]))
    top = jnp.maximum(pre, suf[...])
    w_pre, w_suf = jnp.exp(pre - top), jnp.exp(suf[...] - top)
    total = w_pre + w_suf
    shape = (ROWS, ROWS)
    old, new = (lax.broadcasted_iota(jnp.int32, shape, d) for d in (0, 1))
    order = jnp.where(old == old_row(new), 1.0, 0.0).astype(BF)
    for j in range(COLS):
        got = held[j * ROWS : (j + 1) * ROWS].astype(F32)
        cols = slice(j * WIDE, (j + 1) * WIDE)
        mixed = ((w_pre * got + w_suf * suffix[:, cols]) / total).astype(BF)
        out[:, cols] = jnp.dot(order, mixed, preferred_element_type=F32).astype(BF)


def body(
    q_latent, q_rope, prefix_latent, prefix_rope, suffix_latent, suffix_rope, prefix_of, suffix_len
):
    rows, latent = q_latent.shape[1] * q_latent.shape[2], q_latent.shape[3]
    xh, z, c = (lax.axis_index(a) for a in ("xh", "z", "c"))
    unit = shaped(Q_ROWS, WIDE)
    own = call(pack_kernel, unit, [], [q_latent[0].reshape(rows, latent), q_rope[0]])

    one_up, one_down = along(own, "z", 1), along(own, "z", -1)
    two_up, two_down = along(own, "z", 2), along(own, "z", -2)
    more = shaped(Q_ROWS + HALF, WIDE)
    up, down_ = call(
        relay_kernel, [more, more], [], [one_up, two_up, one_down, two_down], bytes_accessed=1 << 20
    )
    up, down_ = along(up, "z", 2), along(down_, "z", -2)

    t = table(prefix_of[0, :, 0], xh, z, c)
    keys, rope = prefix_latent[0], prefix_rope[0]
    positions = keys.shape[0]
    attend = functools.partial(
        pl.pallas_call,
        scratch_shapes=[pltpu.VMEM((2 * ROPE, positions), BF)],
        compiler_params=pltpu.CompilerParams(vmem_limit_bytes=48 * 1024 * 1024),
    )
    suffix, suffix_lse = attend(
        suffix_kernel,
        out_shape=[shaped(rows, LATENT, dtype=F32), shaped(rows, WIDE, dtype=F32)],
        in_specs=[SMEM, VMEM, VMEM, VMEM],
        out_specs=[VMEM, VMEM],
        cost_estimate=pl.CostEstimate(
            flops=2 * rows * 2048 * 1152, bytes_accessed=3 << 20, transcendentals=rows * 2048
        ),
    )(suffix_len, own, suffix_latent[0], suffix_rope[0])

    quad, two = shaped(4, Q_ROWS, WIDE), shaped(2, Q_ROWS, WIDE)
    keep, send = call(
        route_kernel,
        [quad, quad],
        [t],
        [own, one_up, two_up, one_down, two_down, up, down_],
        bytes_accessed=1 << 20,
    )
    near, far = call(
        merge_c_kernel, [two, two], [], [keep, along(send, "c", 1)], bytes_accessed=1 << 20
    )
    mine = call(
        merge_x_kernel,
        quad,
        [],
        [near, across(near, 0, 1), across(far, 1, 0), across(far, 1, 1)],
        bytes_accessed=1 << 20,
    )
    asked = {d: along(mine, "y", d) if d else mine for d in (0, 1, 3, 2)}

    outs = shaped(4, OUT_ROWS, WIDE)
    parts = {}
    for d, queries in asked.items():
        if d == 1:
            queries, parts[0] = lax.optimization_barrier((queries, parts[0]))
        part = attend(
            prefix_kernel,
            out_shape=outs,
            in_specs=[VMEM] * 3,
            out_specs=VMEM,
            cost_estimate=pl.CostEstimate(
                flops=2 * 512 * 2048 * 1152, bytes_accessed=4 << 20, transcendentals=512 * 2048
            ),
        )(queries, keys, rope)
        parts[d] = along(part, "y", -d) if d else part
    out2 = shaped(2, OUT_ROWS, WIDE)
    p_near, p_far = call(
        merge_y_kernel, [out2, out2], [], [parts[d] for d in range(NY)], bytes_accessed=1 << 20
    )
    both = call(
        merge_xl_kernel,
        outs,
        [],
        [p_near, across(p_far, 0, 1), across(p_near, 1, 0), across(p_far, 1, 1)],
        bytes_accessed=1 << 20,
    )
    back = call(
        back_kernel,
        shaped(NZ, OUT_ROWS, WIDE),
        [t],
        [both, along(both, "c", 1)],
        bytes_accessed=1 << 20,
    )
    arrived = lax.all_to_all(back, "z", 0, 0, tiled=True)
    out = call(
        final_kernel,
        shaped(rows, LATENT),
        [t],
        [arrived, suffix, suffix_lse],
        bytes_accessed=1 << 20,
    )
    return out.reshape(q_latent.shape)


def solution(mesh):
    fine = Mesh(mesh.devices.reshape(2, NZ, 2, NY, 2), AXES)
    grp, blk = ("xh", "z", "c"), ("y", "xl")
    in_specs = (
        P(AXES, None, None, None),
        P(AXES, None, None),
        P(grp, blk, None),
        P(grp, None, blk),
        P(AXES, None, None),
        P(AXES, None, None),
        P(blk, None, None),
        P(AXES),
    )
    return jax.shard_map(
        body, mesh=fine, in_specs=in_specs, out_specs=P(AXES, None, None, None), check_vma=False
    )
```

```python
import functools
import math

import jax
import jax.numpy as jnp
from jax import lax
from jax.experimental import pallas as pl
from jax.experimental.pallas import tpu as pltpu
from jax.sharding import Mesh, PartitionSpec as P

QK_DIM = 192
SCALE = QK_DIM**-0.5
LOG2E = math.log2(math.e)
BF = jnp.bfloat16
F32 = jnp.float32
AXES = ("xh", "z", "c", "y", "xl")
NZ, NY = 8, 4
HEADS, LATENT, ROPE = 64, 512, 64
WIDE = 128
COLS = LATENT // WIDE
ROWS = 2 * HEADS
LAT_ROWS = COLS * ROWS
Q_ROWS = LAT_ROWS + HEADS
HALF = Q_ROWS // 2
OUT_ROWS = LAT_ROWS + 16
OUT_HALF = 272
NT = (((1,), (1,)), ((), ()))

SMEM = pl.BlockSpec(memory_space=pltpu.SMEM)
VMEM = pl.BlockSpec(memory_space=pltpu.VMEM)

T_ROUTE, T_BACK = 0, 8


def call(kernel, outs, ints, arrays, flops=0, bytes_accessed=0, exps=0):
    single = not isinstance(outs, (list, tuple))
    specs = jax.tree.map(lambda _: VMEM, outs)
    return pl.pallas_call(
        kernel,
        out_shape=outs,
        in_specs=[SMEM] * len(ints) + [VMEM] * len(arrays),
        out_specs=VMEM if single else specs,
        compiler_params=pltpu.CompilerParams(vmem_limit_bytes=48 * 1024 * 1024),
        cost_estimate=pl.CostEstimate(
            flops=flops, bytes_accessed=bytes_accessed, transcendentals=exps
        ),
    )(*ints, *arrays)


def shaped(*shape, dtype=BF):
    return jax.ShapeDtypeStruct(shape, dtype)


def along(x, axis, distance):
    n = lax.axis_size(axis)
    return lax.ppermute(x, axis, [(i, (i + distance) % n) for i in range(n)])


def across(x, flip_xh, flip_xl):
    pairs = [
        (2 * i + j, 2 * (i ^ flip_xh) + (j ^ flip_xl)) for i in range(2) for j in range(2)
    ]
    return lax.ppermute(x, ("xh", "xl"), pairs)


def ranks(dest):
    ids = jnp.arange(dest.shape[0], dtype=jnp.int32)
    before = (ids[None, :] < ids[:, None]) & (dest[None, :] == dest[:, None])
    return jnp.sum(before.astype(jnp.int32), axis=1)


def table(dest, xh, z, c):
    ids = jnp.arange(dest.shape[0], dtype=jnp.int32)
    eight = jnp.arange(8, dtype=jnp.int32)
    cr, xr, slot = eight // 4, (eight // 2) % 2, eight % 2
    rank = ranks(dest)
    holders = ((xh ^ xr) * NZ + z) * 2 + (c ^ cr)
    in_ring = (ids // (2 * NZ) == xh) & (ids % 2 == c)
    match = (dest[None, :] == holders[:, None]) & (rank[None, :] == slot[:, None]) & in_ring[None, :]
    distance = (z - ids // 2) % NZ
    route = jnp.sum(jnp.where(match, distance[None, :] + 1, 0), axis=1) - 1
    roots = (xh * NZ + (z + eight) % NZ) * 2 + c
    root = roots[:, None] == ids[None, :]
    h = jnp.sum(jnp.where(root, dest[None], 0), axis=1)
    r = jnp.sum(jnp.where(root, rank[None], 0), axis=1)
    place = ((h % 2) ^ c) * 4 + ((h // (2 * NZ)) ^ xh) * 2 + r
    back = jnp.where((h // 2) % NZ == z, place, -1)
    return jnp.concatenate([route, back]).astype(jnp.int32)


def old_row(n):
    return (n // 32) % 2 * HEADS + n % 32 * 2 + n // HEADS


def pack_kernel(lat, rot, out):
    shape = (ROWS, ROWS)
    new, old = (lax.broadcasted_iota(jnp.int32, shape, d) for d in (0, 1))
    order = jnp.where(old == old_row(new), 1.0, 0.0).astype(BF)
    rows = jnp.dot(order, lat[...], preferred_element_type=F32).astype(BF)
    for j in range(COLS):
        out[j * ROWS : (j + 1) * ROWS] = rows[:, j * WIDE : (j + 1) * WIDE]
    flat = rot[...].astype(F32)
    pairs = [
        flat[s : s + 1, j * WIDE : (j + 1) * WIDE] for s in range(2) for j in range(HEADS // 2)
    ]
    out[LAT_ROWS:] = jnp.concatenate(pairs, axis=0).astype(BF)


def relay_kernel(one_up, two_up, one_down, two_down, up, down):
    up[:Q_ROWS] = one_up[...]
    up[Q_ROWS:] = two_up[:HALF]
    down[:Q_ROWS] = one_down[...]
    down[Q_ROWS:] = two_down[HALF:]


def route_kernel(t, own, one_up, two_up, one_down, two_down, up, down, keep, send):
    whole = [own, one_up, two_up, up.at[:Q_ROWS], None, down.at[:Q_ROWS], two_down, one_down]
    for slot in range(8):
        out = (keep if slot < 4 else send).at[slot % 4]
        source = t[T_ROUTE + slot]
        for d in range(NZ):

            @pl.when(source == d)
            def _():
                if d == NZ // 2:
                    out[:HALF] = up[Q_ROWS:]
                    out[HALF:] = down[Q_ROWS:]
                else:
                    out[...] = whole[d][...]

        @pl.when(source < 0)
        def _():
            out[...] = jnp.zeros(out.shape, BF)


def merge_c_kernel(keep, got, near, far):
    for r in range(2):
        near[r] = keep[r] + got[r]
        far[r] = keep[2 + r] + got[2 + r]


def add_kernel(a, b, out):
    out[...] = a[...] + b[...]


def queries_of(units):
    lat, rot = [], []
    lanes = lax.broadcasted_iota(jnp.int32, (HEADS, WIDE), 1)
    for u in units:
        lat.append(jnp.concatenate([u[ROWS * j : ROWS * (j + 1)] for j in range(COLS)], axis=1))
        pair = u[LAT_ROWS:]
        zero = jnp.zeros_like(pair)
        rot += [jnp.where(lanes < ROPE, pair, zero), jnp.where(lanes < ROPE, zero, pair)]
    return jnp.concatenate(lat, axis=0), jnp.concatenate(rot, axis=0)


def prefix_kernel(q, keys, rope, o, rope2):
    rope2[:ROPE] = rope[...]
    rope2[ROPE:] = rope[...]
    for first in range(0, q.shape[0], 2):
        lat, rot = queries_of([q[first], q[first + 1]])
        s = lax.dot_general(lat, keys[...], NT, preferred_element_type=F32)
        s = s + jnp.dot(rot, rope2[...], preferred_element_type=F32)
        top = jnp.max(s, axis=1, keepdims=True)
        w = jnp.exp2((s - top) * (SCALE * LOG2E))
        total = jnp.sum(w, axis=1, keepdims=True)
        out = jnp.dot(w.astype(BF), keys[...], preferred_element_type=F32)
        out = (out / total).astype(BF)
        lse = top * SCALE + jnp.log(total)
        flat = jnp.transpose(jnp.broadcast_to(lse, (2 * ROWS, WIDE)))
        for u in range(2):
            for j in range(COLS):
                o[first + u, j * ROWS : (j + 1) * ROWS] = out[
                    u * ROWS : (u + 1) * ROWS, j * WIDE : (j + 1) * WIDE
                ]
            o[first + u, LAT_ROWS:] = in_thirds(flat[0:1, u * ROWS : (u + 1) * ROWS])


def in_thirds(row):
    high = row.astype(BF).astype(F32)
    mid = (row - high).astype(BF).astype(F32)
    low = row - high - mid
    place = lax.broadcasted_iota(jnp.int32, (16, WIDE), 0)
    block = jnp.where(place == 0, high, jnp.where(place == 1, mid, jnp.where(place == 2, low, 0.0)))
    return block.astype(BF)


def from_thirds(block):
    block = block.astype(F32)
    return block[0:1] + block[1:2] + block[2:3]


def down(row):
    return jnp.transpose(jnp.broadcast_to(row, (WIDE, WIDE)))


def merge_parts(parts, out):
    lses = [from_thirds(p[LAT_ROWS:]) for p in parts]
    top = functools.reduce(jnp.maximum, lses)
    shares = [jnp.exp(x - top) for x in lses]
    total = functools.reduce(jnp.add, shares)
    weights = [down(x / total) for x in shares]
    for j in range(COLS):
        at = slice(j * ROWS, (j + 1) * ROWS)
        mixed = [w * p[at].astype(F32) for w, p in zip(weights, parts)]
        out[at] = functools.reduce(jnp.add, mixed).astype(BF)
    out[LAT_ROWS:] = in_thirds(top + jnp.log(total))


def merge_kernel(*refs):
    parts, out = refs[:-1], refs[-1]
    for k in range(out.shape[0]):
        merge_parts([p.at[k] for p in parts], out.at[k])


def merge_xl_kernel(near, from_xl, from_xh, from_both, out):
    for r in range(2):
        merge_parts([near.at[r], from_xl.at[r]], out.at[r])
        merge_parts([from_xh.at[r], from_both.at[r]], out.at[2 + r])


def back_kernel(t, own, got, here, one_up, two_up, two_down, one_down, up, down):
    whole = [here, one_up, two_up, up.at[:OUT_ROWS], None, down.at[:OUT_ROWS], two_down, one_down]
    for d in range(NZ):
        place = t[T_BACK + d]

        def put(unit):
            if d == NZ // 2:
                up[OUT_ROWS:] = unit[:OUT_HALF]
                down[OUT_ROWS:] = unit[OUT_HALF:]
            else:
                whole[d][...] = unit[...]

        @pl.when((place >= 0) & (place < 4))
        def _():
            put(own[place])

        @pl.when(place >= 4)
        def _():
            put(got[place - 4])

        @pl.when(place < 0)
        def _():
            put(jnp.zeros((OUT_ROWS, WIDE), BF))


def relay_back_kernel(one_up, two_up, two_down, one_down, up, down, o1, o2, o6, o7):
    o1[...] = one_up[...] + up[:OUT_ROWS]
    o2[:OUT_HALF] = two_up[:OUT_HALF] + up[OUT_ROWS:]
    o2[OUT_HALF:] = two_up[OUT_HALF:]
    o6[:OUT_HALF] = two_down[:OUT_HALF]
    o6[OUT_HALF:] = two_down[OUT_HALF:] + down[OUT_ROWS:]
    o7[...] = one_down[...] + down[:OUT_ROWS]


def suffix_kernel(length, unit, keys, rope, out, out_lse, rope2):
    rope2[:ROPE] = rope[...]
    rope2[ROPE:] = rope[...]
    lat, rot = queries_of([unit[...]])
    s = lax.dot_general(lat, keys[...], NT, preferred_element_type=F32)
    s = (s + jnp.dot(rot, rope2[...], preferred_element_type=F32)) * SCALE
    position = lax.broadcasted_iota(jnp.int32, s.shape, 1)
    step = lax.broadcasted_iota(jnp.int32, s.shape, 0) // (HEADS // 2) % 2
    s = jnp.where(position < length[0] + step + 1, s, -1e30)
    top = jnp.max(s, axis=1, keepdims=True)
    w = jnp.exp(s - top)
    total = jnp.sum(w, axis=1, keepdims=True)
    out[...] = jnp.dot(w.astype(BF), keys[...], preferred_element_type=F32) / total
    out_lse[...] = jnp.broadcast_to(top + jnp.log(total), out_lse.shape)


def final_kernel(here, from1, from2, from6, from7, suffix, suf, out):
    held = here[...] + from1[...] + from2[...] + from6[...] + from7[...]
    pre = down(from_thirds(held[LAT_ROWS:]))
    top = jnp.maximum(pre, suf[...])
    w_pre, w_suf = jnp.exp(pre - top), jnp.exp(suf[...] - top)
    total = w_pre + w_suf
    shape = (ROWS, ROWS)
    old, new = (lax.broadcasted_iota(jnp.int32, shape, d) for d in (0, 1))
    order = jnp.where(old == old_row(new), 1.0, 0.0).astype(BF)
    for j in range(COLS):
        got = held[j * ROWS : (j + 1) * ROWS].astype(F32)
        cols = slice(j * WIDE, (j + 1) * WIDE)
        mixed = ((w_pre * got + w_suf * suffix[:, cols]) / total).astype(BF)
        out[:, cols] = jnp.dot(order, mixed, preferred_element_type=F32).astype(BF)


def body(
    q_latent, q_rope, prefix_latent, prefix_rope, suffix_latent, suffix_rope, prefix_of, suffix_len
):
    rows, latent = q_latent.shape[1] * q_latent.shape[2], q_latent.shape[3]
    xh, z, c = (lax.axis_index(a) for a in ("xh", "z", "c"))
    unit = shaped(Q_ROWS, WIDE)
    own = call(pack_kernel, unit, [], [q_latent[0].reshape(rows, latent), q_rope[0]])

    one_up, one_down = along(own, "z", 1), along(own, "z", -1)
    two_up, two_down = along(own, "z", 2), along(own, "z", -2)
    more = shaped(Q_ROWS + HALF, WIDE)
    up, down_ = call(
        relay_kernel, [more, more], [], [one_up, two_up, one_down, two_down], bytes_accessed=1 << 20
    )
    up, down_ = along(up, "z", 2), along(down_, "z", -2)

    t = table(prefix_of[0, :, 0], xh, z, c)
    keys, rope = prefix_latent[0], prefix_rope[0]
    positions = keys.shape[0]
    attend = functools.partial(
        pl.pallas_call,
        scratch_shapes=[pltpu.VMEM((2 * ROPE, positions), BF)],
        compiler_params=pltpu.CompilerParams(vmem_limit_bytes=48 * 1024 * 1024),
    )
    suffix, suffix_lse = attend(
        suffix_kernel,
        out_shape=[shaped(rows, LATENT, dtype=F32), shaped(rows, WIDE, dtype=F32)],
        in_specs=[SMEM, VMEM, VMEM, VMEM],
        out_specs=[VMEM, VMEM],
        cost_estimate=pl.CostEstimate(
            flops=2 * rows * 2048 * 1152, bytes_accessed=3 << 20, transcendentals=rows * 2048
        ),
    )(suffix_len, own, suffix_latent[0], suffix_rope[0])

    quad, two = shaped(4, Q_ROWS, WIDE), shaped(2, Q_ROWS, WIDE)
    keep, send = call(
        route_kernel,
        [quad, quad],
        [t],
        [own, one_up, two_up, one_down, two_down, up, down_],
        bytes_accessed=1 << 20,
    )
    near, far = call(
        merge_c_kernel, [two, two], [], [keep, along(send, "c", 1)], bytes_accessed=1 << 20
    )
    q = {}
    q[0, 1] = call(
        add_kernel, two, [], [across(near, 0, 1), across(far, 1, 1)], bytes_accessed=1 << 20
    )
    q[0, 0] = call(add_kernel, two, [], [near, across(far, 1, 0)], bytes_accessed=1 << 20)
    for half in (1, 0):
        q[1, half] = along(q[0, half], "y", 1)
        q[3, half] = along(q[0, half], "y", -1)
    q[2, 1] = along(q[1, 1], "y", 1)
    q[2, 0] = along(q[3, 0], "y", -1)

    out2 = shaped(2, OUT_ROWS, WIDE)

    def attention(queries):
        return attend(
            prefix_kernel,
            out_shape=out2,
            in_specs=[VMEM] * 3,
            out_specs=VMEM,
            cost_estimate=pl.CostEstimate(
                flops=2 * 256 * 2048 * 1152, bytes_accessed=3 << 20, transcendentals=256 * 2048
            ),
        )(queries, keys, rope)

    def merged(*parts):
        return call(merge_kernel, out2, [], parts, bytes_accessed=1 << 20)

    p = {}
    for place in ((0, 1), (0, 0), (1, 1), (3, 1), (1, 0), (3, 0), (2, 1), (2, 0)):
        if place == (1, 1):
            q[place], p[0, 1], p[0, 0] = lax.optimization_barrier((q[place], p[0, 1], p[0, 0]))
        p[place] = attention(q[place])
    plain_far = along(p[3, 1], "y", 1)
    plain_near = along(p[1, 0], "y", -1)
    summed_far = along(merged(p[1, 1], along(p[2, 1], "y", -1)), "y", -1)
    summed_near = along(merged(p[3, 0], along(p[2, 0], "y", 1)), "y", 1)
    p_far = merged(p[0, 1], plain_far, summed_far)
    p_near = merged(p[0, 0], plain_near, summed_near)
    both = call(
        merge_xl_kernel,
        shaped(4, OUT_ROWS, WIDE),
        [],
        [p_near, across(p_far, 0, 1), across(p_near, 1, 0), across(p_far, 1, 1)],
        bytes_accessed=1 << 20,
    )

    one = shaped(OUT_ROWS, WIDE)
    here, o1, o2, o6, o7, up, down_ = call(
        back_kernel,
        [one] * 5 + [shaped(OUT_ROWS + OUT_HALF, WIDE), shaped(2 * OUT_ROWS - OUT_HALF, WIDE)],
        [t],
        [both, along(both, "c", 1)],
        bytes_accessed=1 << 20,
    )
    up, down_ = along(up, "z", 2), along(down_, "z", -2)
    o1, o2, o6, o7 = call(
        relay_back_kernel, [one] * 4, [], [o1, o2, o6, o7, up, down_], bytes_accessed=1 << 20
    )
    arrived = [along(o2, "z", 2), along(o6, "z", -2), along(o1, "z", 1), along(o7, "z", -1)]
    out = call(
        final_kernel,
        shaped(rows, LATENT),
        [],
        [here, *arrived, suffix, suffix_lse],
        bytes_accessed=1 << 20,
    )
    return out.reshape(q_latent.shape)


def solution(mesh):
    fine = Mesh(mesh.devices.reshape(2, NZ, 2, NY, 2), AXES)
    grp, blk = ("xh", "z", "c"), ("y", "xl")
    in_specs = (
        P(AXES, None, None, None),
        P(AXES, None, None),
        P(grp, blk, None),
        P(grp, None, blk),
        P(AXES, None, None),
        P(AXES, None, None),
        P(blk, None, None),
        P(AXES),
    )
    return jax.shard_map(
        body, mesh=fine, in_specs=in_specs, out_specs=P(AXES, None, None, None), check_vma=False
    )
```

```python
import functools
import math

import jax
import jax.numpy as jnp
from jax import lax
from jax.experimental import pallas as pl
from jax.experimental.pallas import tpu as pltpu
from jax.sharding import Mesh, PartitionSpec as P

QK_DIM = 192
SCALE = QK_DIM**-0.5
LOG2E = math.log2(math.e)
BF = jnp.bfloat16
F32 = jnp.float32
AXES = ("xh", "z", "c", "y", "xl")
NZ, NY = 8, 4
HEADS, LATENT, ROPE = 64, 512, 64
WIDE = 128
COLS = LATENT // WIDE
ROWS = 2 * HEADS
LAT_ROWS = COLS * ROWS
Q_ROWS = LAT_ROWS + HEADS
HALF = Q_ROWS // 2
OUT_ROWS = LAT_ROWS + 16
OUT_HALF = 272
NT = (((1,), (1,)), ((), ()))

SMEM = pl.BlockSpec(memory_space=pltpu.SMEM)
VMEM = pl.BlockSpec(memory_space=pltpu.VMEM)

T_ROUTE, T_BACK = 0, 8


def call(kernel, outs, ints, arrays):
    single = not isinstance(outs, (list, tuple))
    specs = jax.tree.map(lambda _: VMEM, outs)
    return pl.pallas_call(
        kernel,
        out_shape=outs,
        in_specs=[SMEM] * len(ints) + [VMEM] * len(arrays),
        out_specs=VMEM if single else specs,
        compiler_params=pltpu.CompilerParams(vmem_limit_bytes=48 * 1024 * 1024),
        cost_estimate=pl.CostEstimate(flops=0, bytes_accessed=0, transcendentals=0),
    )(*ints, *arrays)


def shaped(*shape, dtype=BF):
    return jax.ShapeDtypeStruct(shape, dtype)


def along(x, axis, distance):
    n = lax.axis_size(axis)
    return lax.ppermute(x, axis, [(i, (i + distance) % n) for i in range(n)])


def across(x, flip_xh, flip_xl):
    pairs = [
        (2 * i + j, 2 * (i ^ flip_xh) + (j ^ flip_xl)) for i in range(2) for j in range(2)
    ]
    return lax.ppermute(x, ("xh", "xl"), pairs)


def ranks(dest):
    ids = jnp.arange(dest.shape[0], dtype=jnp.int32)
    before = (ids[None, :] < ids[:, None]) & (dest[None, :] == dest[:, None])
    return jnp.sum(before.astype(jnp.int32), axis=1)


def table(dest, xh, z, c):
    ids = jnp.arange(dest.shape[0], dtype=jnp.int32)
    eight = jnp.arange(8, dtype=jnp.int32)
    cr, xr, slot = eight // 4, (eight // 2) % 2, eight % 2
    rank = ranks(dest)
    holders = ((xh ^ xr) * NZ + z) * 2 + (c ^ cr)
    in_ring = (ids // (2 * NZ) == xh) & (ids % 2 == c)
    match = (dest[None, :] == holders[:, None]) & (rank[None, :] == slot[:, None]) & in_ring[None, :]
    distance = (z - ids // 2) % NZ
    route = jnp.sum(jnp.where(match, distance[None, :] + 1, 0), axis=1) - 1
    roots = (xh * NZ + (z + eight) % NZ) * 2 + c
    root = roots[:, None] == ids[None, :]
    h = jnp.sum(jnp.where(root, dest[None], 0), axis=1)
    r = jnp.sum(jnp.where(root, rank[None], 0), axis=1)
    place = ((h % 2) ^ c) * 4 + ((h // (2 * NZ)) ^ xh) * 2 + r
    back = jnp.where((h // 2) % NZ == z, place, -1)
    return jnp.concatenate([route, back]).astype(jnp.int32)


def old_row(n):
    return (n // 32) % 2 * HEADS + n % 32 * 2 + n // HEADS


def pack_kernel(lat, rot, out):
    shape = (ROWS, ROWS)
    new, old = (lax.broadcasted_iota(jnp.int32, shape, d) for d in (0, 1))
    order = jnp.where(old == old_row(new), 1.0, 0.0).astype(BF)
    rows = jnp.dot(order, lat[...], preferred_element_type=F32).astype(BF)
    for j in range(COLS):
        out[j * ROWS : (j + 1) * ROWS] = rows[:, j * WIDE : (j + 1) * WIDE]
    flat = rot[...].astype(F32)
    pairs = [
        flat[s : s + 1, j * WIDE : (j + 1) * WIDE] for s in range(2) for j in range(HEADS // 2)
    ]
    out[LAT_ROWS:] = jnp.concatenate(pairs, axis=0).astype(BF)


def route_kernel(t, own, two_up, two_down, one_up, one_down, three_up, three_down, four_up, four_down, keep, send):
    whole = [own, one_up, two_up, three_up, None, three_down, two_down, one_down]
    for slot in range(8):
        out = (keep if slot < 4 else send).at[slot % 4]
        source = t[T_ROUTE + slot]
        for d in range(NZ):

            @pl.when(source == d)
            def _():
                if d == NZ // 2:
                    out[:HALF] = four_up[...]
                    out[HALF:] = four_down[...]
                else:
                    out[...] = whole[d][...]

        @pl.when(source < 0)
        def _():
            out[...] = jnp.zeros(out.shape, BF)


def merge_c_kernel(keep, got, near, far):
    for r in range(2):
        near[r] = keep[r] + got[r]
        far[r] = keep[2 + r] + got[2 + r]


def add_kernel(a, b, out):
    out[...] = a[...] + b[...]


def queries_of(units):
    lat, rot = [], []
    lanes = lax.broadcasted_iota(jnp.int32, (HEADS, WIDE), 1)
    for u in units:
        lat.append(jnp.concatenate([u[ROWS * j : ROWS * (j + 1)] for j in range(COLS)], axis=1))
        pair = u[LAT_ROWS:]
        zero = jnp.zeros_like(pair)
        rot += [jnp.where(lanes < ROPE, pair, zero), jnp.where(lanes < ROPE, zero, pair)]
    return jnp.concatenate(lat, axis=0), jnp.concatenate(rot, axis=0)


def prefix_kernel(q, keys, rope, o, rope2):
    rope2[:ROPE] = rope[...]
    rope2[ROPE:] = rope[...]
    for first in range(0, q.shape[0], 2):
        lat, rot = queries_of([q[first], q[first + 1]])
        s = lax.dot_general(lat, keys[...], NT, preferred_element_type=F32)
        s = s + jnp.dot(rot, rope2[...], preferred_element_type=F32)
        top = jnp.max(s, axis=1, keepdims=True)
        w = jnp.exp2((s - top) * (SCALE * LOG2E))
        total = jnp.sum(w, axis=1, keepdims=True)
        out = jnp.dot(w.astype(BF), keys[...], preferred_element_type=F32)
        out = (out / total).astype(BF)
        lse = top * SCALE + jnp.log(total)
        flat = jnp.transpose(jnp.broadcast_to(lse, (2 * ROWS, WIDE)))
        for u in range(2):
            for j in range(COLS):
                o[first + u, j * ROWS : (j + 1) * ROWS] = out[
                    u * ROWS : (u + 1) * ROWS, j * WIDE : (j + 1) * WIDE
                ]
            o[first + u, LAT_ROWS:] = in_thirds(flat[0:1, u * ROWS : (u + 1) * ROWS])


def in_thirds(row):
    high = row.astype(BF).astype(F32)
    mid = (row - high).astype(BF).astype(F32)
    low = row - high - mid
    place = lax.broadcasted_iota(jnp.int32, (16, WIDE), 0)
    block = jnp.where(place == 0, high, jnp.where(place == 1, mid, jnp.where(place == 2, low, 0.0)))
    return block.astype(BF)


def from_thirds(block):
    block = block.astype(F32)
    return block[0:1] + block[1:2] + block[2:3]


def down(row):
    return jnp.transpose(jnp.broadcast_to(row, (WIDE, WIDE)))


def merge_parts(parts, out):
    lses = [from_thirds(p[LAT_ROWS:]) for p in parts]
    top = functools.reduce(jnp.maximum, lses)
    shares = [jnp.exp(x - top) for x in lses]
    total = functools.reduce(jnp.add, shares)
    weights = [down(x / total) for x in shares]
    for j in range(COLS):
        at = slice(j * ROWS, (j + 1) * ROWS)
        mixed = [w * p[at].astype(F32) for w, p in zip(weights, parts)]
        out[at] = functools.reduce(jnp.add, mixed).astype(BF)
    out[LAT_ROWS:] = in_thirds(top + jnp.log(total))


def merge_kernel(*refs):
    parts, out = refs[:-1], refs[-1]
    for k in range(out.shape[0]):
        merge_parts([p.at[k] for p in parts], out.at[k])


def merge_xl_kernel(near, from_xl, from_xh, from_both, out):
    for r in range(2):
        merge_parts([near.at[r], from_xl.at[r]], out.at[r])
        merge_parts([from_xh.at[r], from_both.at[r]], out.at[2 + r])


def back_kernel(t, own, got, here, o1, o2, o3, four_up, four_down, o5, o6, o7):
    whole = [here, o1, o2, o3, None, o5, o6, o7]
    for d in range(NZ):
        place = t[T_BACK + d]

        def put(unit):
            if d == NZ // 2:
                four_up[...] = unit[:OUT_HALF]
                four_down[...] = unit[OUT_HALF:]
            else:
                whole[d][...] = unit[...]

        @pl.when((place >= 0) & (place < 4))
        def _():
            put(own[place])

        @pl.when(place >= 4)
        def _():
            put(got[place - 4])

        @pl.when(place < 0)
        def _():
            put(jnp.zeros((OUT_ROWS, WIDE), BF))


def relay_kernel(o2, o6, r3, r5, four_up, four_down, up, down):
    up[:OUT_HALF] = o2[:OUT_HALF] + r3[:OUT_HALF] + four_up[...]
    up[OUT_HALF:] = o2[OUT_HALF:] + r3[OUT_HALF:]
    down[:OUT_HALF] = o6[:OUT_HALF] + r5[:OUT_HALF]
    down[OUT_HALF:] = o6[OUT_HALF:] + r5[OUT_HALF:] + four_down[...]


def suffix_kernel(length, unit, keys, rope, out, out_lse, rope2):
    rope2[:ROPE] = rope[...]
    rope2[ROPE:] = rope[...]
    lat, rot = queries_of([unit[...]])
    s = lax.dot_general(lat, keys[...], NT, preferred_element_type=F32)
    s = (s + jnp.dot(rot, rope2[...], preferred_element_type=F32)) * SCALE
    position = lax.broadcasted_iota(jnp.int32, s.shape, 1)
    step = lax.broadcasted_iota(jnp.int32, s.shape, 0) // (HEADS // 2) % 2
    s = jnp.where(position < length[0] + step + 1, s, -1e30)
    top = jnp.max(s, axis=1, keepdims=True)
    w = jnp.exp(s - top)
    total = jnp.sum(w, axis=1, keepdims=True)
    out[...] = jnp.dot(w.astype(BF), keys[...], preferred_element_type=F32) / total
    out_lse[...] = jnp.broadcast_to(top + jnp.log(total), out_lse.shape)


def final_kernel(here, from1, from7, from2, from6, suffix, suf, out):
    held = here[...] + from1[...] + from7[...] + from2[...] + from6[...]
    pre = down(from_thirds(held[LAT_ROWS:]))
    top = jnp.maximum(pre, suf[...])
    w_pre, w_suf = jnp.exp(pre - top), jnp.exp(suf[...] - top)
    total = w_pre + w_suf
    shape = (ROWS, ROWS)
    old, new = (lax.broadcasted_iota(jnp.int32, shape, d) for d in (0, 1))
    order = jnp.where(old == old_row(new), 1.0, 0.0).astype(BF)
    for j in range(COLS):
        got = held[j * ROWS : (j + 1) * ROWS].astype(F32)
        cols = slice(j * WIDE, (j + 1) * WIDE)
        mixed = ((w_pre * got + w_suf * suffix[:, cols]) / total).astype(BF)
        out[:, cols] = jnp.dot(order, mixed, preferred_element_type=F32).astype(BF)


def body(
    q_latent, q_rope, prefix_latent, prefix_rope, suffix_latent, suffix_rope, prefix_of, suffix_len
):
    rows, latent = q_latent.shape[1] * q_latent.shape[2], q_latent.shape[3]
    xh, z, c = (lax.axis_index(a) for a in ("xh", "z", "c"))
    unit = shaped(Q_ROWS, WIDE)
    own = pl.pallas_call(pack_kernel, out_shape=unit, out_specs=VMEM)(
        q_latent[0].reshape(rows, latent), q_rope[0]
    )

    two_up, two_down = along(own, "z", 2), along(own, "z", -2)
    one_up, one_down = along(own, "z", 1), along(own, "z", -1)
    three_up, three_down = along(two_up, "z", 1), along(two_down, "z", -1)
    four_up, four_down = along(two_up[:HALF], "z", 2), along(two_down[HALF:], "z", -2)

    t = table(prefix_of[0, :, 0], xh, z, c)
    keys, rope = prefix_latent[0], prefix_rope[0]
    positions = keys.shape[0]
    attend = functools.partial(
        pl.pallas_call,
        scratch_shapes=[pltpu.VMEM((2 * ROPE, positions), BF)],
        compiler_params=pltpu.CompilerParams(vmem_limit_bytes=48 * 1024 * 1024),
    )
    suffix, suffix_lse = attend(
        suffix_kernel,
        out_shape=[shaped(rows, LATENT, dtype=F32), shaped(rows, WIDE, dtype=F32)],
        in_specs=[SMEM, VMEM, VMEM, VMEM],
        out_specs=[VMEM, VMEM],
        cost_estimate=pl.CostEstimate(
            flops=rows * 2048 * 64, bytes_accessed=0, transcendentals=0
        ),
    )(suffix_len, own, suffix_latent[0], suffix_rope[0])

    quad, two = shaped(4, Q_ROWS, WIDE), shaped(2, Q_ROWS, WIDE)
    keep, send = call(
        route_kernel,
        [quad, quad],
        [t],
        [own, two_up, two_down, one_up, one_down, three_up, three_down, four_up, four_down])
    near, far = call(
        merge_c_kernel, [two, two], [], [keep, along(send, "c", 1)])
    out2 = shaped(2, OUT_ROWS, WIDE)

    def attention(queries):
        return attend(
            prefix_kernel,
            out_shape=out2,
            in_specs=[VMEM] * 3,
            out_specs=VMEM,
            cost_estimate=pl.CostEstimate(
                flops=2 * 256 * 2048 * 1152, bytes_accessed=3 << 20, transcendentals=256 * 2048
            ),
        )(queries, keys, rope)

    def merged(*parts):
        return call(merge_kernel, out2, [], parts)

    wait = lax.optimization_barrier
    from_xl, from_both, from_xh = across(near, 0, 1), across(far, 1, 1), across(far, 1, 0)
    q, p = {}, {}
    q[0, 1] = call(add_kernel, two, [], [from_xl, from_both])
    q[1, 1], q[3, 1] = along(q[0, 1], "y", 1), along(q[0, 1], "y", -1)
    p[0, 1] = attention(q[0, 1])
    from_xh, p[0, 1] = wait((from_xh, p[0, 1]))
    q[0, 0] = call(add_kernel, two, [], [near, from_xh])
    q[3, 0], q[1, 0] = along(q[0, 0], "y", -1), along(q[0, 0], "y", 1)
    p[0, 0] = attention(q[0, 0])
    q[1, 1], q[3, 1], p[0, 1] = wait((q[1, 1], q[3, 1], p[0, 1]))
    q[2, 1] = along(q[1, 1], "y", 1)
    q[3, 0], q[1, 0], p[0, 0] = wait((q[3, 0], q[1, 0], p[0, 0]))
    q[2, 0] = along(q[3, 0], "y", -1)
    p[3, 1], p[1, 1] = attention(q[3, 1]), attention(q[1, 1])
    plain_far = along(p[3, 1], "y", 1)
    q[2, 1], p[1, 1], p[3, 1] = wait((q[2, 1], p[1, 1], p[3, 1]))
    p[2, 1] = attention(q[2, 1])
    sum_far = along(p[2, 1], "y", -1)
    p[1, 0], p[3, 0] = attention(q[1, 0]), attention(q[3, 0])
    plain_near = along(p[1, 0], "y", -1)
    q[2, 0], p[1, 0], p[3, 0] = wait((q[2, 0], p[1, 0], p[3, 0]))
    p[2, 0] = attention(q[2, 0])
    sum_near = along(p[2, 0], "y", 1)
    sum_far, plain_far = wait((sum_far, plain_far))
    sum_far = along(merged(p[1, 1], sum_far), "y", -1)
    sum_near, plain_near = wait((sum_near, plain_near))
    sum_near = along(merged(p[3, 0], sum_near), "y", 1)
    p_far = merged(p[0, 1], plain_far, sum_far)
    p_near = merged(p[0, 0], plain_near, sum_near)
    both = call(
        merge_xl_kernel,
        shaped(4, OUT_ROWS, WIDE),
        [],
        [p_near, across(p_far, 0, 1), across(p_near, 1, 0), across(p_far, 1, 1)])

    one = shaped(OUT_ROWS, WIDE)
    four_a, four_b = shaped(OUT_HALF, WIDE), shaped(OUT_ROWS - OUT_HALF, WIDE)
    here, o1, o2, o3, o4a, o4b, o5, o6, o7 = call(
        back_kernel,
        [one] * 4 + [four_a, four_b] + [one] * 3,
        [t],
        [both, along(both, "c", 1)],
    )
    r3, r5 = along(o3, "z", 1), along(o5, "z", -1)
    r4a, r4b = along(o4a, "z", 2), along(o4b, "z", -2)
    from1, from7 = along(o1, "z", 1), along(o7, "z", -1)
    o2, o6 = call(relay_kernel, [one] * 2, [], [o2, o6, r3, r5, r4a, r4b])
    arrived = [from1, from7, along(o2, "z", 2), along(o6, "z", -2)]
    out = call(
        final_kernel,
        shaped(rows, LATENT),
        [],
        [here, *arrived, suffix, suffix_lse])
    return out.reshape(q_latent.shape)


def solution(mesh):
    fine = Mesh(mesh.devices.reshape(2, NZ, 2, NY, 2), AXES)
    grp, blk = ("xh", "z", "c"), ("y", "xl")
    in_specs = (
        P(AXES, None, None, None),
        P(AXES, None, None),
        P(grp, blk, None),
        P(grp, None, blk),
        P(AXES, None, None),
        P(AXES, None, None),
        P(blk, None, None),
        P(AXES),
    )
    return jax.shard_map(
        body, mesh=fine, in_specs=in_specs, out_specs=P(AXES, None, None, None), check_vma=False
    )
```

```python
import functools
import math

import jax
import jax.numpy as jnp
from jax import lax
from jax.experimental import pallas as pl
from jax.experimental.pallas import tpu as pltpu
from jax.sharding import Mesh, PartitionSpec as P

QK_DIM = 192
SCALE = QK_DIM**-0.5
LOG2E = math.log2(math.e)
BF = jnp.bfloat16
F32 = jnp.float32
AXES = ("xh", "z", "c", "y", "xl")
NZ, NY = 8, 4
HEADS, LATENT, ROPE = 64, 512, 64
WIDE = 128
COLS = LATENT // WIDE
ROWS = 2 * HEADS
LAT_ROWS = COLS * ROWS
Q_ROWS = LAT_ROWS + HEADS
HALF = Q_ROWS // 2
OUT_ROWS = LAT_ROWS + 16
OUT_HALF = 272
NT = (((1,), (1,)), ((), ()))

SMEM = pl.BlockSpec(memory_space=pltpu.SMEM)
VMEM = pl.BlockSpec(memory_space=pltpu.VMEM)

T_ROUTE, T_BACK = 0, 8


def call(kernel, outs, ints, arrays):
    single = not isinstance(outs, (list, tuple))
    specs = jax.tree.map(lambda _: VMEM, outs)
    return pl.pallas_call(
        kernel,
        out_shape=outs,
        in_specs=[SMEM] * len(ints) + [VMEM] * len(arrays),
        out_specs=VMEM if single else specs,
        compiler_params=pltpu.CompilerParams(vmem_limit_bytes=48 * 1024 * 1024),
        cost_estimate=pl.CostEstimate(flops=0, bytes_accessed=0, transcendentals=0),
    )(*ints, *arrays)


def shaped(*shape, dtype=BF):
    return jax.ShapeDtypeStruct(shape, dtype)


def along(x, axis, distance):
    n = lax.axis_size(axis)
    return lax.ppermute(x, axis, [(i, (i + distance) % n) for i in range(n)])


def across(x, flip_xh, flip_xl):
    pairs = [
        (2 * i + j, 2 * (i ^ flip_xh) + (j ^ flip_xl)) for i in range(2) for j in range(2)
    ]
    return lax.ppermute(x, ("xh", "xl"), pairs)


def ranks(dest):
    ids = jnp.arange(dest.shape[0], dtype=jnp.int32)
    before = (ids[None, :] < ids[:, None]) & (dest[None, :] == dest[:, None])
    return jnp.sum(before.astype(jnp.int32), axis=1)


def table(dest, xh, z, c):
    ids = jnp.arange(dest.shape[0], dtype=jnp.int32)
    eight = jnp.arange(8, dtype=jnp.int32)
    cr, xr, slot = eight // 4, (eight // 2) % 2, eight % 2
    rank = ranks(dest)
    holders = ((xh ^ xr) * NZ + z) * 2 + (c ^ cr)
    in_ring = (ids // (2 * NZ) == xh) & (ids % 2 == c)
    match = (dest[None, :] == holders[:, None]) & (rank[None, :] == slot[:, None]) & in_ring[None, :]
    distance = (z - ids // 2) % NZ
    route = jnp.sum(jnp.where(match, distance[None, :] + 1, 0), axis=1) - 1
    roots = (xh * NZ + (z + eight) % NZ) * 2 + c
    root = roots[:, None] == ids[None, :]
    h = jnp.sum(jnp.where(root, dest[None], 0), axis=1)
    r = jnp.sum(jnp.where(root, rank[None], 0), axis=1)
    place = ((h % 2) ^ c) * 4 + ((h // (2 * NZ)) ^ xh) * 2 + r
    back = jnp.where((h // 2) % NZ == z, place, -1)
    return jnp.concatenate([route, back]).astype(jnp.int32)


def old_row(n):
    return (n // 32) % 2 * HEADS + n % 32 * 2 + n // HEADS


def pack_kernel(lat, rot, out):
    shape = (ROWS, ROWS)
    new, old = (lax.broadcasted_iota(jnp.int32, shape, d) for d in (0, 1))
    order = jnp.where(old == old_row(new), 1.0, 0.0).astype(BF)
    rows = jnp.dot(order, lat[...], preferred_element_type=F32).astype(BF)
    for j in range(COLS):
        out[j * ROWS : (j + 1) * ROWS] = rows[:, j * WIDE : (j + 1) * WIDE]
    flat = rot[...].astype(F32)
    pairs = [
        flat[s : s + 1, j * WIDE : (j + 1) * WIDE] for s in range(2) for j in range(HEADS // 2)
    ]
    out[LAT_ROWS:] = jnp.concatenate(pairs, axis=0).astype(BF)


def route_kernel(t, own, two_up, two_down, one_up, one_down, three_up, three_down, four_up, four_down, keep, send):
    whole = [own, one_up, two_up, three_up, None, three_down, two_down, one_down]
    for slot in range(8):
        out = (keep if slot < 4 else send).at[slot % 4]
        source = t[T_ROUTE + slot]
        for d in range(NZ):

            @pl.when(source == d)
            def _():
                if d == NZ // 2:
                    out[:HALF] = four_up[...]
                    out[HALF:] = four_down[...]
                else:
                    out[...] = whole[d][...]

        @pl.when(source < 0)
        def _():
            out[...] = jnp.zeros(out.shape, BF)


def merge_c_kernel(keep, got, near, far):
    for r in range(2):
        near[r] = keep[r] + got[r]
        far[r] = keep[2 + r] + got[2 + r]


def add_kernel(a, b, out):
    out[...] = a[...] + b[...]


def queries_of(units):
    lat, rot = [], []
    lanes = lax.broadcasted_iota(jnp.int32, (HEADS, WIDE), 1)
    for u in units:
        lat.append(jnp.concatenate([u[ROWS * j : ROWS * (j + 1)] for j in range(COLS)], axis=1))
        pair = u[LAT_ROWS:]
        zero = jnp.zeros_like(pair)
        rot += [jnp.where(lanes < ROPE, pair, zero), jnp.where(lanes < ROPE, zero, pair)]
    return jnp.concatenate(lat, axis=0), jnp.concatenate(rot, axis=0)


def prefix_kernel(q, keys, rope, o, rope2):
    rope2[:ROPE] = rope[...]
    rope2[ROPE:] = rope[...]
    for first in range(0, q.shape[0], 2):
        lat, rot = queries_of([q[first], q[first + 1]])
        s = lax.dot_general(lat, keys[...], NT, preferred_element_type=F32)
        s = s + jnp.dot(rot, rope2[...], preferred_element_type=F32)
        top = jnp.max(s, axis=1, keepdims=True)
        w = jnp.exp2((s - top) * (SCALE * LOG2E))
        total = jnp.sum(w, axis=1, keepdims=True)
        out = jnp.dot(w.astype(BF), keys[...], preferred_element_type=F32)
        out = (out / total).astype(BF)
        lse = top * SCALE + jnp.log(total)
        flat = jnp.transpose(jnp.broadcast_to(lse, (2 * ROWS, WIDE)))
        for u in range(2):
            for j in range(COLS):
                o[first + u, j * ROWS : (j + 1) * ROWS] = out[
                    u * ROWS : (u + 1) * ROWS, j * WIDE : (j + 1) * WIDE
                ]
            o[first + u, LAT_ROWS:] = in_thirds(flat[0:1, u * ROWS : (u + 1) * ROWS])


def in_thirds(row):
    high = row.astype(BF).astype(F32)
    mid = (row - high).astype(BF).astype(F32)
    low = row - high - mid
    place = lax.broadcasted_iota(jnp.int32, (16, WIDE), 0)
    block = jnp.where(place == 0, high, jnp.where(place == 1, mid, jnp.where(place == 2, low, 0.0)))
    return block.astype(BF)


def from_thirds(block):
    block = block.astype(F32)
    return block[0:1] + block[1:2] + block[2:3]


def down(row):
    return jnp.transpose(jnp.broadcast_to(row, (WIDE, WIDE)))


def merge_parts(parts, out):
    lses = [from_thirds(p[LAT_ROWS:]) for p in parts]
    top = functools.reduce(jnp.maximum, lses)
    shares = [jnp.exp(x - top) for x in lses]
    total = functools.reduce(jnp.add, shares)
    weights = [down(x / total) for x in shares]
    for j in range(COLS):
        at = slice(j * ROWS, (j + 1) * ROWS)
        mixed = [w * p[at].astype(F32) for w, p in zip(weights, parts)]
        out[at] = functools.reduce(jnp.add, mixed).astype(BF)
    out[LAT_ROWS:] = in_thirds(top + jnp.log(total))


def merge_kernel(*refs):
    parts, out = refs[:-1], refs[-1]
    for k in range(out.shape[0]):
        merge_parts([p.at[k] for p in parts], out.at[k])


def merge_xl_kernel(near, from_xl, from_xh, from_both, out):
    for r in range(2):
        merge_parts([near.at[r], from_xl.at[r]], out.at[r])
        merge_parts([from_xh.at[r], from_both.at[r]], out.at[2 + r])


def back_kernel(t, own, got, here, o1, o2, o3, four_up, four_down, o5, o6, o7):
    whole = [here, o1, o2, o3, None, o5, o6, o7]
    for d in range(NZ):
        place = t[T_BACK + d]

        def put(unit):
            if d == NZ // 2:
                four_up[...] = unit[:OUT_HALF]
                four_down[...] = unit[OUT_HALF:]
            else:
                whole[d][...] = unit[...]

        @pl.when((place >= 0) & (place < 4))
        def _():
            put(own[place])

        @pl.when(place >= 4)
        def _():
            put(got[place - 4])

        @pl.when(place < 0)
        def _():
            put(jnp.zeros((OUT_ROWS, WIDE), BF))


def relay_kernel(o2, o6, r3, r5, four_up, four_down, up, down):
    up[:OUT_HALF] = o2[:OUT_HALF] + r3[:OUT_HALF] + four_up[...]
    up[OUT_HALF:] = o2[OUT_HALF:] + r3[OUT_HALF:]
    down[:OUT_HALF] = o6[:OUT_HALF] + r5[:OUT_HALF]
    down[OUT_HALF:] = o6[OUT_HALF:] + r5[OUT_HALF:] + four_down[...]


def suffix_kernel(length, unit, keys, rope, out, out_lse, rope2):
    rope2[:ROPE] = rope[...]
    rope2[ROPE:] = rope[...]
    lat, rot = queries_of([unit[...]])
    s = lax.dot_general(lat, keys[...], NT, preferred_element_type=F32)
    s = (s + jnp.dot(rot, rope2[...], preferred_element_type=F32)) * SCALE
    position = lax.broadcasted_iota(jnp.int32, s.shape, 1)
    step = lax.broadcasted_iota(jnp.int32, s.shape, 0) // (HEADS // 2) % 2
    s = jnp.where(position < length[0] + step + 1, s, -1e30)
    top = jnp.max(s, axis=1, keepdims=True)
    w = jnp.exp(s - top)
    total = jnp.sum(w, axis=1, keepdims=True)
    out[...] = jnp.dot(w.astype(BF), keys[...], preferred_element_type=F32) / total
    out_lse[...] = jnp.broadcast_to(top + jnp.log(total), out_lse.shape)


def final_kernel(here, from1, from7, from2, from6, suffix, suf, out):
    held = here[...] + from1[...] + from7[...] + from2[...] + from6[...]
    pre = down(from_thirds(held[LAT_ROWS:]))
    top = jnp.maximum(pre, suf[...])
    w_pre, w_suf = jnp.exp(pre - top), jnp.exp(suf[...] - top)
    total = w_pre + w_suf
    shape = (ROWS, ROWS)
    old, new = (lax.broadcasted_iota(jnp.int32, shape, d) for d in (0, 1))
    order = jnp.where(old == old_row(new), 1.0, 0.0).astype(BF)
    for j in range(COLS):
        got = held[j * ROWS : (j + 1) * ROWS].astype(F32)
        cols = slice(j * WIDE, (j + 1) * WIDE)
        mixed = ((w_pre * got + w_suf * suffix[:, cols]) / total).astype(BF)
        out[:, cols] = jnp.dot(order, mixed, preferred_element_type=F32).astype(BF)


def body(
    q_latent, q_rope, prefix_latent, prefix_rope, suffix_latent, suffix_rope, prefix_of, suffix_len
):
    rows, latent = q_latent.shape[1] * q_latent.shape[2], q_latent.shape[3]
    xh, z, c = (lax.axis_index(a) for a in ("xh", "z", "c"))
    unit = shaped(Q_ROWS, WIDE)
    own = call(pack_kernel, unit, [], [q_latent[0].reshape(rows, latent), q_rope[0]])

    two_up, two_down = along(own, "z", 2), along(own, "z", -2)
    one_up, one_down = along(own, "z", 1), along(own, "z", -1)
    three_up, three_down = along(two_up, "z", 1), along(two_down, "z", -1)
    four_up, four_down = along(two_up[:HALF], "z", 2), along(two_down[HALF:], "z", -2)

    t = table(prefix_of[0, :, 0], xh, z, c)
    keys, rope = prefix_latent[0], prefix_rope[0]
    positions = keys.shape[0]
    attend = functools.partial(
        pl.pallas_call,
        scratch_shapes=[pltpu.VMEM((2 * ROPE, positions), BF)],
        compiler_params=pltpu.CompilerParams(vmem_limit_bytes=48 * 1024 * 1024),
    )
    suffix, suffix_lse = attend(
        suffix_kernel,
        out_shape=[shaped(rows, LATENT, dtype=F32), shaped(rows, WIDE, dtype=F32)],
        in_specs=[SMEM, VMEM, VMEM, VMEM],
        out_specs=[VMEM, VMEM],
        cost_estimate=pl.CostEstimate(
            flops=rows * 2048 * 64, bytes_accessed=0, transcendentals=0
        ),
    )(suffix_len, own, suffix_latent[0], suffix_rope[0])

    quad, two = shaped(4, Q_ROWS, WIDE), shaped(2, Q_ROWS, WIDE)
    keep, send = call(
        route_kernel,
        [quad, quad],
        [t],
        [own, two_up, two_down, one_up, one_down, three_up, three_down, four_up, four_down])
    near, far = call(
        merge_c_kernel, [two, two], [], [keep, along(send, "c", 1)])
    out2 = shaped(2, OUT_ROWS, WIDE)

    def attention(queries):
        return attend(
            prefix_kernel,
            out_shape=out2,
            in_specs=[VMEM] * 3,
            out_specs=VMEM,
            cost_estimate=pl.CostEstimate(
                flops=2 * 256 * 2048 * 1152, bytes_accessed=3 << 20, transcendentals=256 * 2048
            ),
        )(queries, keys, rope)

    def merged(*parts):
        return call(merge_kernel, out2, [], parts)

    wait = lax.optimization_barrier
    from_xl, from_both = across(near, 0, 1), across(far, 1, 1)
    q, p = {}, {}
    q[0, 1] = call(add_kernel, two, [], [from_xl, from_both])
    q[1, 1], q[3, 1] = along(q[0, 1], "y", 1), along(q[0, 1], "y", -1)
    far, q[0, 1] = wait((far, q[0, 1]))
    from_xh = across(far, 1, 0)
    p[0, 1] = attention(q[0, 1])
    from_xh, p[0, 1] = wait((from_xh, p[0, 1]))
    q[0, 0] = call(add_kernel, two, [], [near, from_xh])
    q[3, 0] = along(q[0, 0], "y", -1)
    p[0, 0] = attention(q[0, 0])
    q[1, 1], q[3, 1], p[0, 1] = wait((q[1, 1], q[3, 1], p[0, 1]))
    q[2, 1] = along(q[1, 1], "y", 1)
    p[3, 1], p[1, 1] = attention(q[3, 1]), attention(q[1, 1])
    plain_far = along(p[1, 1], "y", -1)
    q[3, 0], p[0, 0], p[3, 1], p[1, 1] = wait((q[3, 0], p[0, 0], p[3, 1], p[1, 1]))
    q[2, 0] = along(q[3, 0], "y", -1)
    q[2, 1], q[3, 0], p[0, 0], p[3, 1] = wait((q[2, 1], q[3, 0], p[0, 0], p[3, 1]))
    p[2, 1] = attention(q[2, 1])
    sum_far = along(p[2, 1], "y", 1)
    q[0, 0], q[3, 0], p[2, 1] = wait((q[0, 0], q[3, 0], p[2, 1]))
    q[1, 0] = along(q[0, 0], "y", 1)
    p[3, 0] = attention(q[3, 0])
    plain_near = along(p[3, 0], "y", 1)
    p[1, 0] = attention(q[1, 0])
    q[2, 0], p[1, 0], p[3, 0] = wait((q[2, 0], p[1, 0], p[3, 0]))
    p[2, 0] = attention(q[2, 0])
    sum_near = along(p[2, 0], "y", -1)
    sum_far, plain_far = wait((sum_far, plain_far))
    sum_far = along(merged(p[3, 1], sum_far), "y", 1)
    sum_near, plain_near = wait((sum_near, plain_near))
    sum_near = along(merged(p[1, 0], sum_near), "y", -1)
    p_far = merged(p[0, 1], plain_far, sum_far)
    p_near = merged(p[0, 0], plain_near, sum_near)
    both = call(
        merge_xl_kernel,
        shaped(4, OUT_ROWS, WIDE),
        [],
        [p_near, across(p_far, 0, 1), across(p_near, 1, 0), across(p_far, 1, 1)])

    one = shaped(OUT_ROWS, WIDE)
    four_a, four_b = shaped(OUT_HALF, WIDE), shaped(OUT_ROWS - OUT_HALF, WIDE)
    here, o1, o2, o3, o4a, o4b, o5, o6, o7 = call(
        back_kernel,
        [one] * 4 + [four_a, four_b] + [one] * 3,
        [t],
        [both, along(both, "c", 1)],
    )
    r3, r5 = along(o3, "z", 1), along(o5, "z", -1)
    r4a, r4b = along(o4a, "z", 2), along(o4b, "z", -2)
    from1, from7 = along(o1, "z", 1), along(o7, "z", -1)
    o2, o6 = call(relay_kernel, [one] * 2, [], [o2, o6, r3, r5, r4a, r4b])
    arrived = [from1, from7, along(o2, "z", 2), along(o6, "z", -2)]
    out = call(
        final_kernel,
        shaped(rows, LATENT),
        [],
        [here, *arrived, suffix, suffix_lse])
    return out.reshape(q_latent.shape)


def solution(mesh):
    fine = Mesh(mesh.devices.reshape(2, NZ, 2, NY, 2), AXES)
    grp, blk = ("xh", "z", "c"), ("y", "xl")
    in_specs = (
        P(AXES, None, None, None),
        P(AXES, None, None),
        P(grp, blk, None),
        P(grp, None, blk),
        P(AXES, None, None),
        P(AXES, None, None),
        P(blk, None, None),
        P(AXES),
    )
    return jax.shard_map(
        body, mesh=fine, in_specs=in_specs, out_specs=P(AXES, None, None, None), check_vma=False
    )
```

```python
import functools
import math

import jax
import jax.numpy as jnp
from jax import lax
from jax.experimental import pallas as pl
from jax.experimental.pallas import tpu as pltpu
from jax.sharding import Mesh, PartitionSpec as P

QK_DIM = 192
SCALE = QK_DIM**-0.5
LOG2E = math.log2(math.e)
BF = jnp.bfloat16
F32 = jnp.float32
AXES = ("xh", "z", "c", "y", "xl")
NZ, NY = 8, 4
HEADS, LATENT, ROPE = 64, 512, 64
WIDE = 128
COLS = LATENT // WIDE
ROWS = 2 * HEADS
LAT_ROWS = COLS * ROWS
Q_ROWS = LAT_ROWS + HEADS
OUT_ROWS = LAT_ROWS + 16
NT = (((1,), (1,)), ((), ()))

SMEM = pl.BlockSpec(memory_space=pltpu.SMEM)
VMEM = pl.BlockSpec(memory_space=pltpu.VMEM)

T_ROUTE, T_BACK, T_ODD = 0, 8, 16


def call(kernel, outs, ints, arrays):
    single = not isinstance(outs, (list, tuple))
    specs = jax.tree.map(lambda _: VMEM, outs)
    return pl.pallas_call(
        kernel,
        out_shape=outs,
        in_specs=[SMEM] * len(ints) + [VMEM] * len(arrays),
        out_specs=VMEM if single else specs,
        compiler_params=pltpu.CompilerParams(vmem_limit_bytes=48 * 1024 * 1024),
        cost_estimate=pl.CostEstimate(flops=0, bytes_accessed=0, transcendentals=0),
    )(*ints, *arrays)


def shaped(*shape, dtype=BF):
    return jax.ShapeDtypeStruct(shape, dtype)


def along(x, axis, distance):
    n = lax.axis_size(axis)
    return lax.ppermute(x, axis, [(i, (i + distance) % n) for i in range(n)])


def along_by_parity(x):
    return lax.ppermute(x, "z", [(i, (i + (-2 if i % 2 else 2)) % NZ) for i in range(NZ)])


def across(x, flip_xh, flip_xl):
    pairs = [
        (2 * i + j, 2 * (i ^ flip_xh) + (j ^ flip_xl)) for i in range(2) for j in range(2)
    ]
    return lax.ppermute(x, ("xh", "xl"), pairs)


def ranks(dest):
    ids = jnp.arange(dest.shape[0], dtype=jnp.int32)
    before = (ids[None, :] < ids[:, None]) & (dest[None, :] == dest[:, None])
    return jnp.sum(before.astype(jnp.int32), axis=1)


def table(dest, xh, z, c):
    ids = jnp.arange(dest.shape[0], dtype=jnp.int32)
    eight = jnp.arange(8, dtype=jnp.int32)
    cr, xr, slot = eight // 4, (eight // 2) % 2, eight % 2
    rank = ranks(dest)
    holders = ((xh ^ xr) * NZ + z) * 2 + (c ^ cr)
    in_ring = (ids // (2 * NZ) == xh) & (ids % 2 == c)
    match = (dest[None, :] == holders[:, None]) & (rank[None, :] == slot[:, None]) & in_ring[None, :]
    distance = (z - ids // 2) % NZ
    route = jnp.sum(jnp.where(match, distance[None, :] + 1, 0), axis=1) - 1
    roots = (xh * NZ + (z + eight) % NZ) * 2 + c
    root = roots[:, None] == ids[None, :]
    h = jnp.sum(jnp.where(root, dest[None], 0), axis=1)
    r = jnp.sum(jnp.where(root, rank[None], 0), axis=1)
    place = ((h % 2) ^ c) * 4 + ((h // (2 * NZ)) ^ xh) * 2 + r
    back = jnp.where((h // 2) % NZ == z, place, -1)
    return jnp.concatenate([route, back, (z % 2)[None]]).astype(jnp.int32)


def old_row(n):
    return (n // 32) % 2 * HEADS + n % 32 * 2 + n // HEADS


def pack_kernel(lat, rot, out):
    shape = (ROWS, ROWS)
    new, old = (lax.broadcasted_iota(jnp.int32, shape, d) for d in (0, 1))
    order = jnp.where(old == old_row(new), 1.0, 0.0).astype(BF)
    rows = jnp.dot(order, lat[...], preferred_element_type=F32).astype(BF)
    for j in range(COLS):
        out[j * ROWS : (j + 1) * ROWS] = rows[:, j * WIDE : (j + 1) * WIDE]
    flat = rot[...].astype(F32)
    pairs = [
        flat[s : s + 1, j * WIDE : (j + 1) * WIDE] for s in range(2) for j in range(HEADS // 2)
    ]
    out[LAT_ROWS:] = jnp.concatenate(pairs, axis=0).astype(BF)


def route_kernel(t, own, two_up, two_down, one_up, one_down, three_up, three_down, four, keep, send):
    whole = [own, one_up, two_up, three_up, four, three_down, two_down, one_down]
    for slot in range(8):
        out = (keep if slot < 4 else send).at[slot % 4]
        source = t[T_ROUTE + slot]
        for d in range(NZ):

            @pl.when(source == d)
            def _():
                out[...] = whole[d][...]

        @pl.when(source < 0)
        def _():
            out[...] = jnp.zeros(out.shape, BF)


def merge_c_kernel(keep, got, near, far):
    for r in range(2):
        near[r] = keep[r] + got[r]
        far[r] = keep[2 + r] + got[2 + r]


def add_kernel(a, b, out):
    out[...] = a[...] + b[...]


def queries_of(units):
    lat, rot = [], []
    lanes = lax.broadcasted_iota(jnp.int32, (HEADS, WIDE), 1)
    for u in units:
        lat.append(jnp.concatenate([u[ROWS * j : ROWS * (j + 1)] for j in range(COLS)], axis=1))
        pair = u[LAT_ROWS:]
        zero = jnp.zeros_like(pair)
        rot += [jnp.where(lanes < ROPE, pair, zero), jnp.where(lanes < ROPE, zero, pair)]
    return jnp.concatenate(lat, axis=0), jnp.concatenate(rot, axis=0)


def prefix_kernel(q, keys, rope2, o):
    lat, rot = queries_of([q[0], q[1]])
    half = keys.shape[0] // 2
    spans = [slice(i * half, (i + 1) * half) for i in range(2)]
    scores = []
    for at in spans:
        s = lax.dot_general(lat, keys[at], NT, preferred_element_type=F32)
        scores.append(s + jnp.dot(rot, rope2[:, at], preferred_element_type=F32))
    tops, totals, outs = [], [], []
    for s, at in zip(scores, spans):
        tops.append(jnp.max(s, axis=1, keepdims=True))
        w = jnp.exp2((s - tops[-1]) * (SCALE * LOG2E))
        totals.append(jnp.sum(w, axis=1, keepdims=True))
        outs.append(jnp.dot(w.astype(BF), keys[at], preferred_element_type=F32))
    top = jnp.maximum(*tops)
    shares = [jnp.exp2((x - top) * (SCALE * LOG2E)) for x in tops]
    total = shares[0] * totals[0] + shares[1] * totals[1]
    out = ((shares[0] * outs[0] + shares[1] * outs[1]) / total).astype(BF)
    lse = top * SCALE + jnp.log(total)
    flat = jnp.transpose(jnp.broadcast_to(lse, (2 * ROWS, WIDE)))
    for u in range(2):
        for j in range(COLS):
            o[u, j * ROWS : (j + 1) * ROWS] = out[
                u * ROWS : (u + 1) * ROWS, j * WIDE : (j + 1) * WIDE
            ]
        o[u, LAT_ROWS:] = in_thirds(flat[0:1, u * ROWS : (u + 1) * ROWS])


def in_thirds(row):
    high = row.astype(BF).astype(F32)
    mid = (row - high).astype(BF).astype(F32)
    low = row - high - mid
    place = lax.broadcasted_iota(jnp.int32, (16, WIDE), 0)
    block = jnp.where(place == 0, high, jnp.where(place == 1, mid, jnp.where(place == 2, low, 0.0)))
    return block.astype(BF)


def from_thirds(block):
    block = block.astype(F32)
    return block[0:1] + block[1:2] + block[2:3]


def down(row):
    return jnp.transpose(jnp.broadcast_to(row, (WIDE, WIDE)))


def merge_parts(parts, out):
    lses = [from_thirds(p[LAT_ROWS:]) for p in parts]
    top = functools.reduce(jnp.maximum, lses)
    shares = [jnp.exp(x - top) for x in lses]
    total = functools.reduce(jnp.add, shares)
    weights = [down(x / total) for x in shares]
    for j in range(COLS):
        at = slice(j * ROWS, (j + 1) * ROWS)
        mixed = [w * p[at].astype(F32) for w, p in zip(weights, parts)]
        out[at] = functools.reduce(jnp.add, mixed).astype(BF)
    out[LAT_ROWS:] = in_thirds(top + jnp.log(total))


def merge_kernel(*refs):
    parts, out = refs[:-1], refs[-1]
    for k in range(out.shape[0]):
        merge_parts([p.at[k] for p in parts], out.at[k])


def merge_xl_kernel(near, from_xl, from_xh, from_both, out):
    for r in range(2):
        merge_parts([near.at[r], from_xl.at[r]], out.at[r])
        merge_parts([from_xh.at[r], from_both.at[r]], out.at[2 + r])


def back_kernel(t, own, got, here, o1, o2, o3, o4, o5, o6, o7):
    for d, out in enumerate([here, o1, o2, o3, o4, o5, o6, o7]):
        place = t[T_BACK + d]

        @pl.when((place >= 0) & (place < 4))
        def _():
            out[...] = own[place]

        @pl.when(place >= 4)
        def _():
            out[...] = got[place - 4]

        @pl.when(place < 0)
        def _():
            out[...] = jnp.zeros((OUT_ROWS, WIDE), BF)


def relay_kernel(t, o2, o6, r3, r5, four, up, down):
    up[...] = o2[...] + r3[...]
    down[...] = o6[...] + r5[...]

    @pl.when(t[T_ODD] == 0)
    def _():
        up[...] += four[...]

    @pl.when(t[T_ODD] == 1)
    def _():
        down[...] += four[...]


def suffix_kernel(length, unit, keys, rope2, out, out_lse):
    lat, rot = queries_of([unit[...]])
    s = lax.dot_general(lat, keys[...], NT, preferred_element_type=F32)
    s = (s + jnp.dot(rot, rope2[...], preferred_element_type=F32)) * SCALE
    position = lax.broadcasted_iota(jnp.int32, s.shape, 1)
    step = lax.broadcasted_iota(jnp.int32, s.shape, 0) // (HEADS // 2) % 2
    s = jnp.where(position < length[0] + step + 1, s, -1e30)
    top = jnp.max(s, axis=1, keepdims=True)
    w = jnp.exp(s - top)
    total = jnp.sum(w, axis=1, keepdims=True)
    out[...] = jnp.dot(w.astype(BF), keys[...], preferred_element_type=F32) / total
    out_lse[...] = jnp.broadcast_to(top + jnp.log(total), out_lse.shape)


def final_kernel(here, from1, from7, from2, from6, suffix, suf, out):
    held = here[...] + from1[...] + from7[...] + from2[...] + from6[...]
    pre = down(from_thirds(held[LAT_ROWS:]))
    top = jnp.maximum(pre, suf[...])
    w_pre, w_suf = jnp.exp(pre - top), jnp.exp(suf[...] - top)
    total = w_pre + w_suf
    shape = (ROWS, ROWS)
    old, new = (lax.broadcasted_iota(jnp.int32, shape, d) for d in (0, 1))
    order = jnp.where(old == old_row(new), 1.0, 0.0).astype(BF)
    for j in range(COLS):
        got = held[j * ROWS : (j + 1) * ROWS].astype(F32)
        cols = slice(j * WIDE, (j + 1) * WIDE)
        mixed = ((w_pre * got + w_suf * suffix[:, cols]) / total).astype(BF)
        out[:, cols] = jnp.dot(order, mixed, preferred_element_type=F32).astype(BF)


def body(
    q_latent, q_rope, prefix_latent, prefix_rope, suffix_latent, suffix_rope, prefix_of, suffix_len
):
    rows, latent = q_latent.shape[1] * q_latent.shape[2], q_latent.shape[3]
    xh, z, c = (lax.axis_index(a) for a in ("xh", "z", "c"))
    unit = shaped(Q_ROWS, WIDE)
    own = call(pack_kernel, unit, [], [q_latent[0].reshape(rows, latent), q_rope[0]])

    two_up, two_down = along(own, "z", 2), along(own, "z", -2)
    one_up, one_down = along(own, "z", 1), along(own, "z", -1)
    three_up, three_down = along(two_up, "z", 1), along(two_down, "z", -1)
    four = along_by_parity(jnp.where(z % 2 == 0, two_up, two_down))

    t = table(prefix_of[0, :, 0], xh, z, c)
    keys, rope = prefix_latent[0], prefix_rope[0]
    rope2 = jnp.concatenate([rope, rope])
    suffix_rope2 = jnp.concatenate([suffix_rope[0], suffix_rope[0]])
    attend = functools.partial(
        pl.pallas_call,
        compiler_params=pltpu.CompilerParams(vmem_limit_bytes=48 * 1024 * 1024),
    )
    suffix, suffix_lse = attend(
        suffix_kernel,
        out_shape=[shaped(rows, LATENT, dtype=F32), shaped(rows, WIDE, dtype=F32)],
        in_specs=[SMEM, VMEM, VMEM, VMEM],
        out_specs=[VMEM, VMEM],
        cost_estimate=pl.CostEstimate(
            flops=rows * 2048 * 64, bytes_accessed=0, transcendentals=0
        ),
    )(suffix_len, own, suffix_latent[0], suffix_rope2)

    quad, two = shaped(4, Q_ROWS, WIDE), shaped(2, Q_ROWS, WIDE)
    keep, send = call(
        route_kernel,
        [quad, quad],
        [t],
        [own, two_up, two_down, one_up, one_down, three_up, three_down, four])
    near, far = call(
        merge_c_kernel, [two, two], [], [keep, along(send, "c", 1)])
    out2 = shaped(2, OUT_ROWS, WIDE)

    def attention(queries):
        return attend(
            prefix_kernel,
            out_shape=out2,
            in_specs=[VMEM] * 3,
            out_specs=VMEM,
            cost_estimate=pl.CostEstimate(
                flops=2 * 256 * 2048 * 1152, bytes_accessed=3 << 20, transcendentals=256 * 2048
            ),
        )(queries, keys, rope2)

    def merged(*parts):
        return call(merge_kernel, out2, [], parts)

    wait = lax.optimization_barrier
    from_xl, from_both = across(near, 0, 1), across(far, 1, 1)
    q, p = {}, {}
    q[0, 1] = call(add_kernel, two, [], [from_xl, from_both])
    q[1, 1], q[3, 1] = along(q[0, 1], "y", 1), along(q[0, 1], "y", -1)
    far, q[0, 1] = wait((far, q[0, 1]))
    from_xh = across(far, 1, 0)
    p[0, 1] = attention(q[0, 1])
    from_xh, p[0, 1] = wait((from_xh, p[0, 1]))
    q[0, 0] = call(add_kernel, two, [], [near, from_xh])
    q[3, 0] = along(q[0, 0], "y", -1)
    p[0, 0] = attention(q[0, 0])
    q[1, 1], q[3, 1], p[0, 1] = wait((q[1, 1], q[3, 1], p[0, 1]))
    q[2, 1] = along(q[1, 1], "y", 1)
    p[1, 1] = attention(q[1, 1])
    plain_far = along(p[1, 1], "y", -1)
    q[3, 0], q[3, 1], p[0, 0], p[1, 1] = wait((q[3, 0], q[3, 1], p[0, 0], p[1, 1]))
    q[2, 0] = along(q[3, 0], "y", -1)
    p[3, 1] = attention(q[3, 1])
    q[2, 1], p[0, 0], p[3, 1] = wait((q[2, 1], p[0, 0], p[3, 1]))
    p[2, 1] = attention(q[2, 1])
    sum_far = along(p[2, 1], "y", 1)
    q[3, 0], p[2, 1] = wait((q[3, 0], p[2, 1]))
    p[3, 0] = attention(q[3, 0])
    plain_near = along(p[3, 0], "y", 1)
    q[0, 0], p[2, 1] = wait((q[0, 0], p[2, 1]))
    q[2, 0], p[3, 0] = wait((q[2, 0], p[3, 0]))
    p[2, 0] = attention(q[2, 0])
    sum_near = along(p[2, 0], "y", -1)
    q[1, 0] = along(q[0, 0], "y", 1)
    q[1, 0], p[2, 0] = wait((q[1, 0], p[2, 0]))
    p[1, 0] = attention(q[1, 0])
    sum_far, plain_far = wait((sum_far, plain_far))
    sum_far = along(merged(p[3, 1], sum_far), "y", 1)
    sum_near, plain_near = wait((sum_near, plain_near))
    sum_near = along(merged(p[1, 0], sum_near), "y", -1)
    p_far = merged(p[0, 1], plain_far, sum_far)
    p_near = merged(p[0, 0], plain_near, sum_near)
    both = call(
        merge_xl_kernel,
        shaped(4, OUT_ROWS, WIDE),
        [],
        [p_near, across(p_far, 0, 1), across(p_near, 1, 0), across(p_far, 1, 1)])

    one = shaped(OUT_ROWS, WIDE)
    here, o1, o2, o3, o4, o5, o6, o7 = call(
        back_kernel, [one] * 8, [t], [both, along(both, "c", 1)]
    )
    r3, r5 = along(o3, "z", 1), along(o5, "z", -1)
    four = along_by_parity(o4)
    from1, from7 = along(o1, "z", 1), along(o7, "z", -1)
    o2, o6 = call(relay_kernel, [one] * 2, [t], [o2, o6, r3, r5, four])
    arrived = [from1, from7, along(o2, "z", 2), along(o6, "z", -2)]
    out = call(
        final_kernel,
        shaped(rows, LATENT),
        [],
        [here, *arrived, suffix, suffix_lse])
    return out.reshape(q_latent.shape)


def solution(mesh):
    fine = Mesh(mesh.devices.reshape(2, NZ, 2, NY, 2), AXES)
    grp, blk = ("xh", "z", "c"), ("y", "xl")
    in_specs = (
        P(AXES, None, None, None),
        P(AXES, None, None),
        P(grp, blk, None),
        P(grp, None, blk),
        P(AXES, None, None),
        P(AXES, None, None),
        P(blk, None, None),
        P(AXES),
    )
    return jax.shard_map(
        body, mesh=fine, in_specs=in_specs, out_specs=P(AXES, None, None, None), check_vma=False
    )
```

```python
import functools
import math

import jax
import jax.numpy as jnp
from jax import lax
from jax.experimental import pallas as pl
from jax.experimental.pallas import tpu as pltpu
from jax.sharding import Mesh, PartitionSpec as P

QK_DIM = 192
SCALE = QK_DIM**-0.5
LOG2E = math.log2(math.e)
BF = jnp.bfloat16
F32 = jnp.float32
AXES = ("xh", "z", "c", "y", "xl")
NZ, NY = 8, 4
HEADS, LATENT, ROPE = 64, 512, 64
WIDE = 128
COLS = LATENT // WIDE
ROWS = 2 * HEADS
LAT_ROWS = COLS * ROWS
Q_ROWS = LAT_ROWS + HEADS
OUT_ROWS = LAT_ROWS + 16
NT = (((1,), (1,)), ((), ()))

SMEM = pl.BlockSpec(memory_space=pltpu.SMEM)
VMEM = pl.BlockSpec(memory_space=pltpu.VMEM)

T_ROUTE, T_BACK = 0, 8


def call(kernel, outs, ints, arrays):
    single = not isinstance(outs, (list, tuple))
    specs = jax.tree.map(lambda _: VMEM, outs)
    return pl.pallas_call(
        kernel,
        out_shape=outs,
        in_specs=[SMEM] * len(ints) + [VMEM] * len(arrays),
        out_specs=VMEM if single else specs,
        compiler_params=pltpu.CompilerParams(vmem_limit_bytes=48 * 1024 * 1024),
        cost_estimate=pl.CostEstimate(flops=0, bytes_accessed=0, transcendentals=0),
    )(*ints, *arrays)


def shaped(*shape, dtype=BF):
    return jax.ShapeDtypeStruct(shape, dtype)


def along(x, axis, distance):
    n = lax.axis_size(axis)
    return lax.ppermute(x, axis, [(i, (i + distance) % n) for i in range(n)])


def along_by_parity(x):
    return lax.ppermute(x, "z", [(i, (i + (-2 if i % 2 else 2)) % NZ) for i in range(NZ)])


def across(x, flip_xh, flip_xl):
    pairs = [
        (2 * i + j, 2 * (i ^ flip_xh) + (j ^ flip_xl)) for i in range(2) for j in range(2)
    ]
    return lax.ppermute(x, ("xh", "xl"), pairs)


def ranks(dest):
    ids = jnp.arange(dest.shape[0], dtype=jnp.int32)
    before = (ids[None, :] < ids[:, None]) & (dest[None, :] == dest[:, None])
    return jnp.sum(before.astype(jnp.int32), axis=1)


def table(dest, xh, z, c):
    ids = jnp.arange(dest.shape[0], dtype=jnp.int32)
    eight = jnp.arange(8, dtype=jnp.int32)
    cr, xr, slot = eight // 4, (eight // 2) % 2, eight % 2
    rank = ranks(dest)
    holders = ((xh ^ xr) * NZ + z) * 2 + (c ^ cr)
    in_ring = (ids // (2 * NZ) == xh) & (ids % 2 == c)
    match = (dest[None, :] == holders[:, None]) & (rank[None, :] == slot[:, None]) & in_ring[None, :]
    distance = (z - ids // 2) % NZ
    route = jnp.sum(jnp.where(match, distance[None, :] + 1, 0), axis=1) - 1
    roots = (xh * NZ + (z + eight) % NZ) * 2 + c
    root = roots[:, None] == ids[None, :]
    h = jnp.sum(jnp.where(root, dest[None], 0), axis=1)
    r = jnp.sum(jnp.where(root, rank[None], 0), axis=1)
    place = ((h % 2) ^ c) * 4 + ((h // (2 * NZ)) ^ xh) * 2 + r
    back = jnp.where((h // 2) % NZ == z, place, -1)
    return jnp.concatenate([route, back]).astype(jnp.int32)


def old_row(n):
    return (n // 32) % 2 * HEADS + n % 32 * 2 + n // HEADS


def pack_kernel(lat, rot, out):
    shape = (ROWS, ROWS)
    new, old = (lax.broadcasted_iota(jnp.int32, shape, d) for d in (0, 1))
    order = jnp.where(old == old_row(new), 1.0, 0.0).astype(BF)
    rows = jnp.dot(order, lat[...], preferred_element_type=F32).astype(BF)
    for j in range(COLS):
        out[j * ROWS : (j + 1) * ROWS] = rows[:, j * WIDE : (j + 1) * WIDE]
    flat = rot[...].astype(F32)
    pairs = [
        flat[s : s + 1, j * WIDE : (j + 1) * WIDE] for s in range(2) for j in range(HEADS // 2)
    ]
    out[LAT_ROWS:] = jnp.concatenate(pairs, axis=0).astype(BF)


def route_kernel(t, own, two_up, two_down, one_up, one_down, three_up, three_down, four, keep, send):
    whole = [own, one_up, two_up, three_up, four, three_down, two_down, one_down]
    for slot in range(8):
        out = (keep if slot < 4 else send).at[slot % 4]
        source = t[T_ROUTE + slot]
        for d in range(NZ):

            @pl.when(source == d)
            def _():
                out[...] = whole[d][...]

        @pl.when(source < 0)
        def _():
            out[...] = jnp.zeros(out.shape, BF)


def merge_c_kernel(keep, got, near, far):
    for r in range(2):
        near[r] = keep[r] + got[r]
        far[r] = keep[2 + r] + got[2 + r]


def add_kernel(a, b, out):
    out[...] = a[...] + b[...]


def queries_of(units):
    lat, rot = [], []
    lanes = lax.broadcasted_iota(jnp.int32, (HEADS, WIDE), 1)
    for u in units:
        lat.append(jnp.concatenate([u[ROWS * j : ROWS * (j + 1)] for j in range(COLS)], axis=1))
        pair = u[LAT_ROWS:]
        zero = jnp.zeros_like(pair)
        rot += [jnp.where(lanes < ROPE, pair, zero), jnp.where(lanes < ROPE, zero, pair)]
    return jnp.concatenate(lat, axis=0), jnp.concatenate(rot, axis=0)


def prefix_kernel(q, keys, rope2, o):
    lat, rot = queries_of([q[0], q[1]])
    half = keys.shape[0] // 2
    spans = [slice(i * half, (i + 1) * half) for i in range(2)]
    scores = []
    for at in spans:
        s = lax.dot_general(lat, keys[at], NT, preferred_element_type=F32)
        scores.append(s + jnp.dot(rot, rope2[:, at], preferred_element_type=F32))
    tops, totals, outs = [], [], []
    for s, at in zip(scores, spans):
        tops.append(jnp.max(s, axis=1, keepdims=True))
        w = jnp.exp2((s - tops[-1]) * (SCALE * LOG2E))
        totals.append(jnp.sum(w, axis=1, keepdims=True))
        outs.append(jnp.dot(w.astype(BF), keys[at], preferred_element_type=F32))
    top = jnp.maximum(*tops)
    shares = [jnp.exp2((x - top) * (SCALE * LOG2E)) for x in tops]
    total = shares[0] * totals[0] + shares[1] * totals[1]
    out = ((shares[0] * outs[0] + shares[1] * outs[1]) / total).astype(BF)
    lse = top * SCALE + jnp.log(total)
    flat = jnp.transpose(jnp.broadcast_to(lse, (2 * ROWS, WIDE)))
    for u in range(2):
        for j in range(COLS):
            o[u, j * ROWS : (j + 1) * ROWS] = out[
                u * ROWS : (u + 1) * ROWS, j * WIDE : (j + 1) * WIDE
            ]
        o[u, LAT_ROWS:] = in_thirds(flat[0:1, u * ROWS : (u + 1) * ROWS])


def in_thirds(row):
    high = row.astype(BF).astype(F32)
    mid = (row - high).astype(BF).astype(F32)
    low = row - high - mid
    place = lax.broadcasted_iota(jnp.int32, (16, WIDE), 0)
    block = jnp.where(place == 0, high, jnp.where(place == 1, mid, jnp.where(place == 2, low, 0.0)))
    return block.astype(BF)


def from_thirds(block):
    block = block.astype(F32)
    return block[0:1] + block[1:2] + block[2:3]


def down(row):
    return jnp.transpose(jnp.broadcast_to(row, (WIDE, WIDE)))


def merge_parts(parts, out):
    lses = [from_thirds(p[LAT_ROWS:]) for p in parts]
    top = functools.reduce(jnp.maximum, lses)
    shares = [jnp.exp(x - top) for x in lses]
    total = functools.reduce(jnp.add, shares)
    weights = [down(x / total) for x in shares]
    for j in range(COLS):
        at = slice(j * ROWS, (j + 1) * ROWS)
        mixed = [w * p[at].astype(F32) for w, p in zip(weights, parts)]
        out[at] = functools.reduce(jnp.add, mixed).astype(BF)
    out[LAT_ROWS:] = in_thirds(top + jnp.log(total))


def merge_kernel(*refs):
    parts, out = refs[:-1], refs[-1]
    for k in range(out.shape[0]):
        merge_parts([p.at[k] for p in parts], out.at[k])


def merge_xl_kernel(near, from_xl, from_xh, from_both, out):
    for r in range(2):
        merge_parts([near.at[r], from_xl.at[r]], out.at[r])
        merge_parts([from_xh.at[r], from_both.at[r]], out.at[2 + r])


def back_kernel(t, own, got, here, o1, o2, o3, o4, o5, o6, o7):
    for d, out in enumerate([here, o1, o2, o3, o4, o5, o6, o7]):
        place = t[T_BACK + d]

        @pl.when((place >= 0) & (place < 4))
        def _():
            out[...] = own[place]

        @pl.when(place >= 4)
        def _():
            out[...] = got[place - 4]

        @pl.when(place < 0)
        def _():
            out[...] = jnp.zeros((OUT_ROWS, WIDE), BF)


def relay_kernel(o2, o6, r3, r5, four, up, down):
    up[...] = o2[...] + r3[...]
    down[...] = o6[...] + r5[...]
    odd = lax.rem(lax.axis_index("z"), 2)

    @pl.when(odd == 0)
    def _():
        up[...] += four[...]

    @pl.when(odd == 1)
    def _():
        down[...] += four[...]


def suffix_kernel(length, unit, keys, rope2, out, out_lse):
    lat, rot = queries_of([unit[...]])
    s = lax.dot_general(lat, keys[...], NT, preferred_element_type=F32)
    s = (s + jnp.dot(rot, rope2[...], preferred_element_type=F32)) * SCALE
    position = lax.broadcasted_iota(jnp.int32, s.shape, 1)
    step = lax.broadcasted_iota(jnp.int32, s.shape, 0) // (HEADS // 2) % 2
    s = jnp.where(position < length[0] + step + 1, s, -1e30)
    top = jnp.max(s, axis=1, keepdims=True)
    w = jnp.exp(s - top)
    total = jnp.sum(w, axis=1, keepdims=True)
    out[...] = jnp.dot(w.astype(BF), keys[...], preferred_element_type=F32) / total
    out_lse[...] = jnp.broadcast_to(top + jnp.log(total), out_lse.shape)


def final_kernel(here, from1, from7, from2, from6, suffix, suf, out):
    held = here[...] + from1[...] + from7[...] + from2[...] + from6[...]
    pre = down(from_thirds(held[LAT_ROWS:]))
    top = jnp.maximum(pre, suf[...])
    w_pre, w_suf = jnp.exp(pre - top), jnp.exp(suf[...] - top)
    total = w_pre + w_suf
    shape = (ROWS, ROWS)
    old, new = (lax.broadcasted_iota(jnp.int32, shape, d) for d in (0, 1))
    order = jnp.where(old == old_row(new), 1.0, 0.0).astype(BF)
    for j in range(COLS):
        got = held[j * ROWS : (j + 1) * ROWS].astype(F32)
        cols = slice(j * WIDE, (j + 1) * WIDE)
        mixed = ((w_pre * got + w_suf * suffix[:, cols]) / total).astype(BF)
        out[:, cols] = jnp.dot(order, mixed, preferred_element_type=F32).astype(BF)


def body(
    q_latent, q_rope, prefix_latent, prefix_rope, suffix_latent, suffix_rope, prefix_of, suffix_len
):
    rows, latent = q_latent.shape[1] * q_latent.shape[2], q_latent.shape[3]
    xh, z, c = (lax.axis_index(a) for a in ("xh", "z", "c"))
    unit = shaped(Q_ROWS, WIDE)
    own = call(pack_kernel, unit, [], [q_latent[0].reshape(rows, latent), q_rope[0]])
    wait = lax.optimization_barrier
    t = table(prefix_of[0, :, 0], xh, z, c)

    two_up, two_down = along(own, "z", 2), along(own, "z", -2)
    own, t = wait((own, t))
    one_up, one_down = along(own, "z", 1), along(own, "z", -1)
    three_up, three_down = along(two_up, "z", 1), along(two_down, "z", -1)
    four = along_by_parity(jnp.where(z % 2 == 0, two_up, two_down))

    keys, rope = prefix_latent[0], prefix_rope[0]
    rope2 = jnp.concatenate([rope, rope])
    suffix_rope2 = jnp.concatenate([suffix_rope[0], suffix_rope[0]])
    attend = functools.partial(
        pl.pallas_call,
        compiler_params=pltpu.CompilerParams(vmem_limit_bytes=48 * 1024 * 1024),
    )
    suffix, suffix_lse = attend(
        suffix_kernel,
        out_shape=[shaped(rows, LATENT, dtype=F32), shaped(rows, WIDE, dtype=F32)],
        in_specs=[SMEM, VMEM, VMEM, VMEM],
        out_specs=[VMEM, VMEM],
        cost_estimate=pl.CostEstimate(
            flops=rows * 2048 * 64, bytes_accessed=0, transcendentals=0
        ),
    )(suffix_len, own, suffix_latent[0], suffix_rope2)

    quad, two = shaped(4, Q_ROWS, WIDE), shaped(2, Q_ROWS, WIDE)
    keep, send = call(
        route_kernel,
        [quad, quad],
        [t],
        [own, two_up, two_down, one_up, one_down, three_up, three_down, four])
    near, far = call(
        merge_c_kernel, [two, two], [], [keep, along(send, "c", 1)])
    out2 = shaped(2, OUT_ROWS, WIDE)

    def attention(queries):
        return attend(
            prefix_kernel,
            out_shape=out2,
            in_specs=[VMEM] * 3,
            out_specs=VMEM,
            cost_estimate=pl.CostEstimate(
                flops=2 * 256 * 2048 * 1152, bytes_accessed=3 << 20, transcendentals=256 * 2048
            ),
        )(queries, keys, rope2)

    def merged(*parts):
        return call(merge_kernel, out2, [], parts)

    q, p = {}, {}
    q[0, 0] = call(add_kernel, two, [], [near, across(far, 1, 0)])
    q[1, 0] = along(q[0, 0], "y", 1)
    near, far, q[0, 0] = wait((near, far, q[0, 0]))
    from_xl, from_both = across(near, 0, 1), across(far, 1, 1)
    p[0, 0] = attention(q[0, 0])
    q[0, 0], p[0, 0] = wait((q[0, 0], p[0, 0]))
    q[3, 0] = along(q[0, 0], "y", -1)
    from_xl, from_both, p[0, 0] = wait((from_xl, from_both, p[0, 0]))
    q[0, 1] = call(add_kernel, two, [], [from_xl, from_both])
    q[3, 1] = along(q[0, 1], "y", -1)
    p[0, 1] = attention(q[0, 1])
    q[1, 0], q[3, 0], p[0, 0] = wait((q[1, 0], q[3, 0], p[0, 0]))
    q[2, 0] = along(q[1, 0], "y", 1)
    p[1, 0] = attention(q[1, 0])
    q[3, 1], q[3, 0], p[0, 1], p[1, 0] = wait((q[3, 1], q[3, 0], p[0, 1], p[1, 0]))
    q[2, 1] = along(q[3, 1], "y", -1)
    p[3, 0] = attention(q[3, 0])
    q[0, 1], p[1, 0] = wait((q[0, 1], p[1, 0]))
    q[1, 1] = along(q[0, 1], "y", 1)
    q[2, 0], p[0, 1], p[3, 0] = wait((q[2, 0], p[0, 1], p[3, 0]))
    p[2, 0] = attention(q[2, 0])
    sum_near = along(p[2, 0], "y", 1)
    p[1, 0], q[3, 1], p[2, 0] = wait((p[1, 0], q[3, 1], p[2, 0]))
    plain_near = along(p[1, 0], "y", -1)
    p[3, 1] = attention(q[3, 1])
    plain_far = along(p[3, 1], "y", 1)
    q[2, 1], p[3, 1] = wait((q[2, 1], p[3, 1]))
    p[2, 1] = attention(q[2, 1])
    sum_far = along(p[2, 1], "y", -1)
    q[1, 1], p[2, 1] = wait((q[1, 1], p[2, 1]))
    p[1, 1] = attention(q[1, 1])
    sum_near, plain_near = wait((sum_near, plain_near))
    sum_near = along(merged(p[3, 0], sum_near), "y", 1)
    sum_far, plain_far = wait((sum_far, plain_far))
    sum_far = along(merged(p[1, 1], sum_far), "y", -1)
    p_near = merged(p[0, 0], plain_near, sum_near)
    p_far = merged(p[0, 1], plain_far, sum_far)
    both = call(
        merge_xl_kernel,
        shaped(4, OUT_ROWS, WIDE),
        [],
        [p_near, across(p_far, 0, 1), across(p_near, 1, 0), across(p_far, 1, 1)])

    one = shaped(OUT_ROWS, WIDE)
    here, o1, o2, o3, o4, o5, o6, o7 = call(
        back_kernel, [one] * 8, [t], [both, along(both, "c", 1)]
    )
    r3, r5 = along(o3, "z", 1), along(o5, "z", -1)
    four = along_by_parity(o4)
    o1, o7, suffix, suffix_lse = wait((o1, o7, suffix, suffix_lse))
    from1, from7 = along(o1, "z", 1), along(o7, "z", -1)
    o2, o6 = call(relay_kernel, [one] * 2, [], [o2, o6, r3, r5, four])
    arrived = [from1, from7, along(o2, "z", 2), along(o6, "z", -2)]
    out = call(
        final_kernel,
        shaped(rows, LATENT),
        [],
        [here, *arrived, suffix, suffix_lse])
    return out.reshape(q_latent.shape)


def solution(mesh):
    fine = Mesh(mesh.devices.reshape(2, NZ, 2, NY, 2), AXES)
    grp, blk = ("xh", "z", "c"), ("y", "xl")
    in_specs = (
        P(AXES, None, None, None),
        P(AXES, None, None),
        P(grp, blk, None),
        P(grp, None, blk),
        P(AXES, None, None),
        P(AXES, None, None),
        P(blk, None, None),
        P(AXES),
    )
    return jax.shard_map(
        body, mesh=fine, in_specs=in_specs, out_specs=P(AXES, None, None, None), check_vma=False
    )
```

```python
import functools
import math

import jax
import jax.numpy as jnp
from jax import lax
from jax.experimental import pallas as pl
from jax.experimental.pallas import tpu as pltpu
from jax.sharding import Mesh, PartitionSpec as P

QK_DIM = 192
SCALE = QK_DIM**-0.5
LOG2E = math.log2(math.e)
BF = jnp.bfloat16
F32 = jnp.float32
AXES = ("xh", "z", "c", "y", "xl")
NZ, NY = 8, 4
HEADS, LATENT, ROPE = 64, 512, 64
WIDE = 128
COLS = LATENT // WIDE
ROWS = 2 * HEADS
LAT_ROWS = COLS * ROWS
Q_ROWS = LAT_ROWS + HEADS
OUT_ROWS = LAT_ROWS + 16
NT = (((1,), (1,)), ((), ()))

SMEM = pl.BlockSpec(memory_space=pltpu.SMEM)
VMEM = pl.BlockSpec(memory_space=pltpu.VMEM)

T_ROUTE, T_BACK = 0, 8


def call(kernel, outs, ints, arrays):
    single = not isinstance(outs, (list, tuple))
    specs = jax.tree.map(lambda _: VMEM, outs)
    return pl.pallas_call(
        kernel,
        out_shape=outs,
        in_specs=[SMEM] * len(ints) + [VMEM] * len(arrays),
        out_specs=VMEM if single else specs,
        compiler_params=pltpu.CompilerParams(vmem_limit_bytes=48 * 1024 * 1024),
        cost_estimate=pl.CostEstimate(flops=0, bytes_accessed=0, transcendentals=0),
    )(*ints, *arrays)


def shaped(*shape, dtype=BF):
    return jax.ShapeDtypeStruct(shape, dtype)


def along(x, axis, distance):
    n = lax.axis_size(axis)
    return lax.ppermute(x, axis, [(i, (i + distance) % n) for i in range(n)])


def along_by_parity(x):
    return lax.ppermute(x, "z", [(i, (i + (-2 if i % 2 else 2)) % NZ) for i in range(NZ)])


def across(x, flip_xh, flip_xl):
    pairs = [
        (2 * i + j, 2 * (i ^ flip_xh) + (j ^ flip_xl)) for i in range(2) for j in range(2)
    ]
    return lax.ppermute(x, ("xh", "xl"), pairs)


def ranks(dest):
    ids = jnp.arange(dest.shape[0], dtype=jnp.int32)
    before = (ids[None, :] < ids[:, None]) & (dest[None, :] == dest[:, None])
    return jnp.sum(before.astype(jnp.int32), axis=1)


def table(dest, xh, z, c):
    ids = jnp.arange(dest.shape[0], dtype=jnp.int32)
    eight = jnp.arange(8, dtype=jnp.int32)
    cr, xr, slot = eight // 4, (eight // 2) % 2, eight % 2
    rank = ranks(dest)
    holders = ((xh ^ xr) * NZ + z) * 2 + (c ^ cr)
    in_ring = (ids // (2 * NZ) == xh) & (ids % 2 == c)
    match = (dest[None, :] == holders[:, None]) & (rank[None, :] == slot[:, None]) & in_ring[None, :]
    distance = (z - ids // 2) % NZ
    route = jnp.sum(jnp.where(match, distance[None, :] + 1, 0), axis=1) - 1
    roots = (xh * NZ + (z + eight) % NZ) * 2 + c
    root = roots[:, None] == ids[None, :]
    h = jnp.sum(jnp.where(root, dest[None], 0), axis=1)
    r = jnp.sum(jnp.where(root, rank[None], 0), axis=1)
    place = ((h % 2) ^ c) * 4 + ((h // (2 * NZ)) ^ xh) * 2 + r
    back = jnp.where((h // 2) % NZ == z, place, -1)
    return jnp.concatenate([route, back]).astype(jnp.int32)


def old_row(n):
    return (n // 32) % 2 * HEADS + n % 32 * 2 + n // HEADS


def pack_kernel(lat, rot, out):
    shape = (ROWS, ROWS)
    new, old = (lax.broadcasted_iota(jnp.int32, shape, d) for d in (0, 1))
    order = jnp.where(old == old_row(new), 1.0, 0.0).astype(BF)
    rows = jnp.dot(order, lat[...], preferred_element_type=F32).astype(BF)
    for j in range(COLS):
        out[j * ROWS : (j + 1) * ROWS] = rows[:, j * WIDE : (j + 1) * WIDE]
    flat = rot[...].astype(F32)
    pairs = [
        flat[s : s + 1, j * WIDE : (j + 1) * WIDE] for s in range(2) for j in range(HEADS // 2)
    ]
    out[LAT_ROWS:] = jnp.concatenate(pairs, axis=0).astype(BF)


def route_kernel(t, own, two_up, two_down, one_up, one_down, three_up, three_down, four, keep, send):
    whole = [own, one_up, two_up, three_up, four, three_down, two_down, one_down]
    for slot in range(8):
        out = (keep if slot < 4 else send).at[slot % 4]
        source = t[T_ROUTE + slot]
        for d in range(NZ):

            @pl.when(source == d)
            def _():
                out[...] = whole[d][...]

        @pl.when(source < 0)
        def _():
            out[...] = jnp.zeros(out.shape, BF)


def merge_c_kernel(keep, got, near, far):
    for r in range(2):
        near[r] = keep[r] + got[r]
        far[r] = keep[2 + r] + got[2 + r]


def add_kernel(a, b, out):
    out[...] = a[...] + b[...]


def queries_of(units):
    lat, rot = [], []
    lanes = lax.broadcasted_iota(jnp.int32, (HEADS, WIDE), 1)
    for u in units:
        lat.append(jnp.concatenate([u[ROWS * j : ROWS * (j + 1)] for j in range(COLS)], axis=1))
        pair = u[LAT_ROWS:]
        zero = jnp.zeros_like(pair)
        rot += [jnp.where(lanes < ROPE, pair, zero), jnp.where(lanes < ROPE, zero, pair)]
    return jnp.concatenate(lat, axis=0), jnp.concatenate(rot, axis=0)


def prefix_kernel(q, keys, rope2, o):
    lat, rot = queries_of([q[0], q[1]])
    half = keys.shape[0] // 2
    spans = [slice(i * half, (i + 1) * half) for i in range(2)]
    scores = []
    for at in spans:
        s = lax.dot_general(lat, keys[at], NT, preferred_element_type=F32)
        scores.append(s + jnp.dot(rot, rope2[:, at], preferred_element_type=F32))
    tops, totals, outs = [], [], []
    for s, at in zip(scores, spans):
        tops.append(jnp.max(s, axis=1, keepdims=True))
        w = jnp.exp2((s - tops[-1]) * (SCALE * LOG2E))
        totals.append(jnp.sum(w, axis=1, keepdims=True))
        outs.append(jnp.dot(w.astype(BF), keys[at], preferred_element_type=F32))
    top = jnp.maximum(*tops)
    shares = [jnp.exp2((x - top) * (SCALE * LOG2E)) for x in tops]
    total = shares[0] * totals[0] + shares[1] * totals[1]
    out = ((shares[0] * outs[0] + shares[1] * outs[1]) / total).astype(BF)
    lse = top * SCALE + jnp.log(total)
    flat = jnp.transpose(jnp.broadcast_to(lse, (2 * ROWS, WIDE)))
    for u in range(2):
        for j in range(COLS):
            o[u, j * ROWS : (j + 1) * ROWS] = out[
                u * ROWS : (u + 1) * ROWS, j * WIDE : (j + 1) * WIDE
            ]
        o[u, LAT_ROWS:] = in_thirds(flat[0:1, u * ROWS : (u + 1) * ROWS])


def in_thirds(row):
    high = row.astype(BF).astype(F32)
    mid = (row - high).astype(BF).astype(F32)
    low = row - high - mid
    place = lax.broadcasted_iota(jnp.int32, (16, WIDE), 0)
    block = jnp.where(place == 0, high, jnp.where(place == 1, mid, jnp.where(place == 2, low, 0.0)))
    return block.astype(BF)


def from_thirds(block):
    block = block.astype(F32)
    return block[0:1] + block[1:2] + block[2:3]


def down(row):
    return jnp.transpose(jnp.broadcast_to(row, (WIDE, WIDE)))


def merge_parts(parts, out):
    lses = [from_thirds(p[LAT_ROWS:]) for p in parts]
    top = functools.reduce(jnp.maximum, lses)
    shares = [jnp.exp(x - top) for x in lses]
    total = functools.reduce(jnp.add, shares)
    weights = [down(x / total) for x in shares]
    for j in range(COLS):
        at = slice(j * ROWS, (j + 1) * ROWS)
        mixed = [w * p[at].astype(F32) for w, p in zip(weights, parts)]
        out[at] = functools.reduce(jnp.add, mixed).astype(BF)
    out[LAT_ROWS:] = in_thirds(top + jnp.log(total))


def merge_kernel(*refs):
    parts, out = refs[:-1], refs[-1]
    for k in range(out.shape[0]):
        merge_parts([p.at[k] for p in parts], out.at[k])


def merge_xl_kernel(near, from_xl, from_xh, from_both, out):
    for r in range(2):
        merge_parts([near.at[r], from_xl.at[r]], out.at[r])
        merge_parts([from_xh.at[r], from_both.at[r]], out.at[2 + r])


def back_kernel(t, own, got, here, o1, o2, o3, o4, o5, o6, o7):
    for d, out in enumerate([here, o1, o2, o3, o4, o5, o6, o7]):
        place = t[T_BACK + d]

        @pl.when((place >= 0) & (place < 4))
        def _():
            out[...] = own[place]

        @pl.when(place >= 4)
        def _():
            out[...] = got[place - 4]

        @pl.when(place < 0)
        def _():
            out[...] = jnp.zeros((OUT_ROWS, WIDE), BF)


def relay_kernel(o2, o6, r3, r5, four, up, down):
    up[...] = o2[...] + r3[...]
    down[...] = o6[...] + r5[...]
    odd = lax.rem(lax.axis_index("z"), 2)

    @pl.when(odd == 0)
    def _():
        up[...] += four[...]

    @pl.when(odd == 1)
    def _():
        down[...] += four[...]


def suffix_kernel(length, unit, keys, rope2, out, out_lse):
    lat, rot = queries_of([unit[...]])
    s = lax.dot_general(lat, keys[...], NT, preferred_element_type=F32)
    s = (s + jnp.dot(rot, rope2[...], preferred_element_type=F32)) * SCALE
    position = lax.broadcasted_iota(jnp.int32, s.shape, 1)
    step = lax.broadcasted_iota(jnp.int32, s.shape, 0) // (HEADS // 2) % 2
    s = jnp.where(position < length[0] + step + 1, s, -1e30)
    top = jnp.max(s, axis=1, keepdims=True)
    w = jnp.exp(s - top)
    total = jnp.sum(w, axis=1, keepdims=True)
    out[...] = jnp.dot(w.astype(BF), keys[...], preferred_element_type=F32) / total
    out_lse[...] = jnp.broadcast_to(top + jnp.log(total), out_lse.shape)


def final_kernel(here, from1, from7, from2, from6, suffix, suf, out):
    held = here[...] + from1[...] + from7[...] + from2[...] + from6[...]
    pre = down(from_thirds(held[LAT_ROWS:]))
    top = jnp.maximum(pre, suf[...])
    w_pre, w_suf = jnp.exp(pre - top), jnp.exp(suf[...] - top)
    total = w_pre + w_suf
    shape = (ROWS, ROWS)
    old, new = (lax.broadcasted_iota(jnp.int32, shape, d) for d in (0, 1))
    order = jnp.where(old == old_row(new), 1.0, 0.0).astype(BF)
    for j in range(COLS):
        got = held[j * ROWS : (j + 1) * ROWS].astype(F32)
        cols = slice(j * WIDE, (j + 1) * WIDE)
        mixed = ((w_pre * got + w_suf * suffix[:, cols]) / total).astype(BF)
        out[:, cols] = jnp.dot(order, mixed, preferred_element_type=F32).astype(BF)


def body(
    q_latent, q_rope, prefix_latent, prefix_rope, suffix_latent, suffix_rope, prefix_of, suffix_len
):
    rows, latent = q_latent.shape[1] * q_latent.shape[2], q_latent.shape[3]
    xh, z, c = (lax.axis_index(a) for a in ("xh", "z", "c"))
    unit = shaped(Q_ROWS, WIDE)
    own = call(pack_kernel, unit, [], [q_latent[0].reshape(rows, latent), q_rope[0]])
    wait = lax.optimization_barrier
    t = table(prefix_of[0, :, 0], xh, z, c)

    two_up, two_down = along(own, "z", 2), along(own, "z", -2)
    own, t = wait((own, t))
    one_up, one_down = along(own, "z", 1), along(own, "z", -1)
    three_up, three_down = along(two_up, "z", 1), along(two_down, "z", -1)
    four = along_by_parity(jnp.where(z % 2 == 0, two_up, two_down))

    keys, rope = prefix_latent[0], prefix_rope[0]
    rope2 = jnp.concatenate([rope, rope])
    suffix_rope2 = jnp.concatenate([suffix_rope[0], suffix_rope[0]])
    attend = functools.partial(
        pl.pallas_call,
        compiler_params=pltpu.CompilerParams(vmem_limit_bytes=48 * 1024 * 1024),
    )
    suffix, suffix_lse = attend(
        suffix_kernel,
        out_shape=[shaped(rows, LATENT, dtype=F32), shaped(rows, WIDE, dtype=F32)],
        in_specs=[SMEM, VMEM, VMEM, VMEM],
        out_specs=[VMEM, VMEM],
        cost_estimate=pl.CostEstimate(
            flops=rows * 2048 * 64, bytes_accessed=0, transcendentals=0
        ),
    )(suffix_len, own, suffix_latent[0], suffix_rope2)

    quad, two = shaped(4, Q_ROWS, WIDE), shaped(2, Q_ROWS, WIDE)
    keep, send = call(
        route_kernel,
        [quad, quad],
        [t],
        [own, two_up, two_down, one_up, one_down, three_up, three_down, four])
    near, far = call(
        merge_c_kernel, [two, two], [], [keep, along(send, "c", 1)])
    out2 = shaped(2, OUT_ROWS, WIDE)

    def attention(queries):
        return attend(
            prefix_kernel,
            out_shape=out2,
            in_specs=[VMEM] * 3,
            out_specs=VMEM,
            cost_estimate=pl.CostEstimate(
                flops=2 * 256 * 2048 * 1152, bytes_accessed=3 << 20, transcendentals=256 * 2048
            ),
        )(queries, keys, rope2)

    def merged(*parts):
        return call(merge_kernel, out2, [], parts)

    q, p = {}, {}
    q[0, 0] = call(add_kernel, two, [], [near, across(far, 1, 0)])
    q[1, 0] = along(q[0, 0], "y", 1)
    near, far, q[0, 0] = wait((near, far, q[0, 0]))
    from_xl, from_both = across(near, 0, 1), across(far, 1, 1)
    p[0, 0] = attention(q[0, 0])
    q[0, 0], p[0, 0] = wait((q[0, 0], p[0, 0]))
    q[3, 0] = along(q[0, 0], "y", -1)
    from_xl, from_both, p[0, 0] = wait((from_xl, from_both, p[0, 0]))
    q[0, 1] = call(add_kernel, two, [], [from_xl, from_both])
    q[3, 1] = along(q[0, 1], "y", -1)
    p[0, 1] = attention(q[0, 1])
    q[1, 0], q[3, 0], p[0, 0], again = wait((q[1, 0], q[3, 0], p[0, 0], q[0, 1]))
    q[2, 0] = along(q[1, 0], "y", 1)
    p[1, 0] = attention(q[1, 0])
    q[3, 1], q[3, 0], p[0, 1], p[1, 0] = wait((q[3, 1], q[3, 0], p[0, 1], p[1, 0]))
    q[2, 1] = along(q[3, 1], "y", -1)
    p[3, 0] = attention(q[3, 0])
    q[1, 1] = along(again, "y", 1)
    q[2, 0], p[0, 1], p[3, 0] = wait((q[2, 0], p[0, 1], p[3, 0]))
    p[2, 0] = attention(q[2, 0])
    sum_near = along(p[2, 0], "y", 1)
    p[1, 0], q[3, 1], p[2, 0] = wait((p[1, 0], q[3, 1], p[2, 0]))
    plain_near = along(p[1, 0], "y", -1)
    p[3, 1] = attention(q[3, 1])
    plain_far = along(p[3, 1], "y", 1)
    q[2, 1], p[3, 1] = wait((q[2, 1], p[3, 1]))
    p[2, 1] = attention(q[2, 1])
    sum_far = along(p[2, 1], "y", -1)
    q[1, 1], p[2, 1] = wait((q[1, 1], p[2, 1]))
    p[1, 1] = attention(q[1, 1])
    sum_near, plain_near = wait((sum_near, plain_near))
    sum_near = along(merged(p[3, 0], sum_near), "y", 1)
    sum_far = along(merged(p[1, 1], sum_far), "y", -1)
    p_near = merged(p[0, 0], plain_near, sum_near)
    p_far = merged(p[0, 1], plain_far, sum_far)
    both = call(
        merge_xl_kernel,
        shaped(4, OUT_ROWS, WIDE),
        [],
        [p_near, across(p_far, 0, 1), across(p_near, 1, 0), across(p_far, 1, 1)])

    one = shaped(OUT_ROWS, WIDE)
    here, o1, o2, o3, o4, o5, o6, o7 = call(
        back_kernel, [one] * 8, [t], [both, along(both, "c", 1)]
    )
    r3, r5 = along(o3, "z", 1), along(o5, "z", -1)
    four = along_by_parity(o4)
    o1, o7, suffix, suffix_lse = wait((o1, o7, suffix, suffix_lse))
    from1, from7 = along(o1, "z", 1), along(o7, "z", -1)
    o2, o6 = call(relay_kernel, [one] * 2, [], [o2, o6, r3, r5, four])
    arrived = [from1, from7, along(o2, "z", 2), along(o6, "z", -2)]
    out = call(
        final_kernel,
        shaped(rows, LATENT),
        [],
        [here, *arrived, suffix, suffix_lse])
    return out.reshape(q_latent.shape)


def solution(mesh):
    fine = Mesh(mesh.devices.reshape(2, NZ, 2, NY, 2), AXES)
    grp, blk = ("xh", "z", "c"), ("y", "xl")
    in_specs = (
        P(AXES, None, None, None),
        P(AXES, None, None),
        P(grp, blk, None),
        P(grp, None, blk),
        P(AXES, None, None),
        P(AXES, None, None),
        P(blk, None, None),
        P(AXES),
    )
    return jax.shard_map(
        body, mesh=fine, in_specs=in_specs, out_specs=P(AXES, None, None, None), check_vma=False
    )
```

```python
import functools
import math

import jax
import jax.numpy as jnp
from jax import lax
from jax.experimental import pallas as pl
from jax.experimental.pallas import tpu as pltpu
from jax.sharding import Mesh, PartitionSpec as P

QK_DIM = 192
SCALE = QK_DIM**-0.5
LOG2E = math.log2(math.e)
BF = jnp.bfloat16
F32 = jnp.float32
AXES = ("xh", "z", "c", "y", "xl")
NZ, NY = 8, 4
HEADS, LATENT, ROPE = 64, 512, 64
WIDE = 128
COLS = LATENT // WIDE
ROWS = 2 * HEADS
LAT_ROWS = COLS * ROWS
Q_ROWS = LAT_ROWS + HEADS
OUT_ROWS = LAT_ROWS + 16
NT = (((1,), (1,)), ((), ()))

SMEM = pl.BlockSpec(memory_space=pltpu.SMEM)
VMEM = pl.BlockSpec(memory_space=pltpu.VMEM)

T_ROUTE, T_BACK = 0, 8


def call(kernel, outs, ints, arrays):
    single = not isinstance(outs, (list, tuple))
    specs = jax.tree.map(lambda _: VMEM, outs)
    return pl.pallas_call(
        kernel,
        out_shape=outs,
        in_specs=[SMEM] * len(ints) + [VMEM] * len(arrays),
        out_specs=VMEM if single else specs,
        compiler_params=pltpu.CompilerParams(vmem_limit_bytes=48 * 1024 * 1024),
        cost_estimate=pl.CostEstimate(flops=0, bytes_accessed=0, transcendentals=0),
    )(*ints, *arrays)


def shaped(*shape, dtype=BF):
    return jax.ShapeDtypeStruct(shape, dtype)


def along(x, axis, distance):
    n = lax.axis_size(axis)
    return lax.ppermute(x, axis, [(i, (i + distance) % n) for i in range(n)])


def along_by_parity(x):
    return lax.ppermute(x, "z", [(i, (i + (-2 if i % 2 else 2)) % NZ) for i in range(NZ)])


def across(x, flip_xh, flip_xl):
    pairs = [
        (2 * i + j, 2 * (i ^ flip_xh) + (j ^ flip_xl)) for i in range(2) for j in range(2)
    ]
    return lax.ppermute(x, ("xh", "xl"), pairs)


def ranks(dest):
    ids = jnp.arange(dest.shape[0], dtype=jnp.int32)
    before = (ids[None, :] < ids[:, None]) & (dest[None, :] == dest[:, None])
    return jnp.sum(before.astype(jnp.int32), axis=1)


def table(dest, xh, z, c):
    ids = jnp.arange(dest.shape[0], dtype=jnp.int32)
    eight = jnp.arange(8, dtype=jnp.int32)
    cr, xr, slot = eight // 4, (eight // 2) % 2, eight % 2
    rank = ranks(dest)
    holders = ((xh ^ xr) * NZ + z) * 2 + (c ^ cr)
    in_ring = (ids // (2 * NZ) == xh) & (ids % 2 == c)
    match = (dest[None, :] == holders[:, None]) & (rank[None, :] == slot[:, None]) & in_ring[None, :]
    distance = (z - ids // 2) % NZ
    route = jnp.sum(jnp.where(match, distance[None, :] + 1, 0), axis=1) - 1
    roots = (xh * NZ + (z + eight) % NZ) * 2 + c
    root = roots[:, None] == ids[None, :]
    h = jnp.sum(jnp.where(root, dest[None], 0), axis=1)
    r = jnp.sum(jnp.where(root, rank[None], 0), axis=1)
    place = ((h % 2) ^ c) * 4 + ((h // (2 * NZ)) ^ xh) * 2 + r
    back = jnp.where((h // 2) % NZ == z, place, -1)
    return jnp.concatenate([route, back]).astype(jnp.int32)


def old_row(n):
    return (n // 32) % 2 * HEADS + n % 32 * 2 + n // HEADS


def pack_kernel(lat, rot, out):
    shape = (ROWS, ROWS)
    new, old = (lax.broadcasted_iota(jnp.int32, shape, d) for d in (0, 1))
    order = jnp.where(old == old_row(new), 1.0, 0.0).astype(BF)
    rows = jnp.dot(order, lat[...], preferred_element_type=F32).astype(BF)
    for j in range(COLS):
        out[j * ROWS : (j + 1) * ROWS] = rows[:, j * WIDE : (j + 1) * WIDE]
    flat = rot[...].astype(F32)
    pairs = [
        flat[s : s + 1, j * WIDE : (j + 1) * WIDE] for s in range(2) for j in range(HEADS // 2)
    ]
    out[LAT_ROWS:] = jnp.concatenate(pairs, axis=0).astype(BF)


def route_kernel(t, own, two_up, two_down, one_up, one_down, three_up, three_down, four, keep, send):
    whole = [own, one_up, two_up, three_up, four, three_down, two_down, one_down]
    for slot in range(8):
        out = (keep if slot < 4 else send).at[slot % 4]
        source = t[T_ROUTE + slot]
        for d in range(NZ):

            @pl.when(source == d)
            def _():
                out[...] = whole[d][...]

        @pl.when(source < 0)
        def _():
            out[...] = jnp.zeros(out.shape, BF)


def merge_c_kernel(keep, got, near, far):
    for r in range(2):
        near[r] = keep[r] + got[r]
        far[r] = keep[2 + r] + got[2 + r]


def add_kernel(a, b, out):
    out[...] = a[...] + b[...]


def queries_of(units):
    lat, rot = [], []
    lanes = lax.broadcasted_iota(jnp.int32, (HEADS, WIDE), 1)
    for u in units:
        lat.append(jnp.concatenate([u[ROWS * j : ROWS * (j + 1)] for j in range(COLS)], axis=1))
        pair = u[LAT_ROWS:]
        zero = jnp.zeros_like(pair)
        rot += [jnp.where(lanes < ROPE, pair, zero), jnp.where(lanes < ROPE, zero, pair)]
    return jnp.concatenate(lat, axis=0), jnp.concatenate(rot, axis=0)


def prefix_kernel(q, keys, rope2, o):
    lat, rot = queries_of([q[0], q[1]])
    half = keys.shape[0] // 2
    spans = [slice(i * half, (i + 1) * half) for i in range(2)]
    scores = []
    for at in spans:
        s = lax.dot_general(lat, keys[at], NT, preferred_element_type=F32)
        scores.append(s + jnp.dot(rot, rope2[:, at], preferred_element_type=F32))
    tops, totals, outs = [], [], []
    for s, at in zip(scores, spans):
        tops.append(jnp.max(s, axis=1, keepdims=True))
        w = jnp.exp2((s - tops[-1]) * (SCALE * LOG2E))
        totals.append(jnp.sum(w, axis=1, keepdims=True))
        outs.append(jnp.dot(w.astype(BF), keys[at], preferred_element_type=F32))
    top = jnp.maximum(*tops)
    shares = [jnp.exp2((x - top) * (SCALE * LOG2E)) for x in tops]
    total = shares[0] * totals[0] + shares[1] * totals[1]
    out = ((shares[0] * outs[0] + shares[1] * outs[1]) / total).astype(BF)
    lse = top * SCALE + jnp.log(total)
    flat = jnp.transpose(jnp.broadcast_to(lse, (2 * ROWS, WIDE)))
    for u in range(2):
        for j in range(COLS):
            o[u, j * ROWS : (j + 1) * ROWS] = out[
                u * ROWS : (u + 1) * ROWS, j * WIDE : (j + 1) * WIDE
            ]
        o[u, LAT_ROWS:] = in_thirds(flat[0:1, u * ROWS : (u + 1) * ROWS])


def in_thirds(row):
    high = row.astype(BF).astype(F32)
    mid = (row - high).astype(BF).astype(F32)
    low = row - high - mid
    place = lax.broadcasted_iota(jnp.int32, (16, WIDE), 0)
    block = jnp.where(place == 0, high, jnp.where(place == 1, mid, jnp.where(place == 2, low, 0.0)))
    return block.astype(BF)


def from_thirds(block):
    block = block.astype(F32)
    return block[0:1] + block[1:2] + block[2:3]


def down(row):
    return jnp.transpose(jnp.broadcast_to(row, (WIDE, WIDE)))


def merge_parts(parts, out):
    lses = [from_thirds(p[LAT_ROWS:]) for p in parts]
    top = functools.reduce(jnp.maximum, lses)
    shares = [jnp.exp(x - top) for x in lses]
    total = functools.reduce(jnp.add, shares)
    weights = [down(x / total) for x in shares]
    for j in range(COLS):
        at = slice(j * ROWS, (j + 1) * ROWS)
        mixed = [w * p[at].astype(F32) for w, p in zip(weights, parts)]
        out[at] = functools.reduce(jnp.add, mixed).astype(BF)
    out[LAT_ROWS:] = in_thirds(top + jnp.log(total))


def merge_kernel(*refs):
    parts, out = refs[:-1], refs[-1]
    for k in range(out.shape[0]):
        merge_parts([p.at[k] for p in parts], out.at[k])


def merge_xl_kernel(near, from_xl, from_xh, from_both, out):
    for r in range(2):
        merge_parts([near.at[r], from_xl.at[r]], out.at[r])
        merge_parts([from_xh.at[r], from_both.at[r]], out.at[2 + r])


def back_kernel(t, own, got, here, o1, o2, o3, o4, o5, o6, o7):
    for d, out in enumerate([here, o1, o2, o3, o4, o5, o6, o7]):
        place = t[T_BACK + d]

        @pl.when((place >= 0) & (place < 4))
        def _():
            out[...] = own[place]

        @pl.when(place >= 4)
        def _():
            out[...] = got[place - 4]

        @pl.when(place < 0)
        def _():
            out[...] = jnp.zeros((OUT_ROWS, WIDE), BF)


def relay_kernel(o2, o6, four, r3, r5, up, down):
    up[...] = o2[...] + r3[...]
    down[...] = o6[...] + r5[...]
    odd = lax.rem(lax.axis_index("z"), 2)

    @pl.when(odd == 0)
    def _():
        up[...] += four[...]

    @pl.when(odd == 1)
    def _():
        down[...] += four[...]


def suffix_kernel(length, unit, keys, rope2, out, out_lse):
    lat, rot = queries_of([unit[...]])
    s = lax.dot_general(lat, keys[...], NT, preferred_element_type=F32)
    s = (s + jnp.dot(rot, rope2[...], preferred_element_type=F32)) * SCALE
    position = lax.broadcasted_iota(jnp.int32, s.shape, 1)
    step = lax.broadcasted_iota(jnp.int32, s.shape, 0) // (HEADS // 2) % 2
    s = jnp.where(position < length[0] + step + 1, s, -1e30)
    top = jnp.max(s, axis=1, keepdims=True)
    w = jnp.exp(s - top)
    total = jnp.sum(w, axis=1, keepdims=True)
    out[...] = jnp.dot(w.astype(BF), keys[...], preferred_element_type=F32) / total
    out_lse[...] = jnp.broadcast_to(top + jnp.log(total), out_lse.shape)


def final_kernel(here, from1, from7, from2, from6, suffix, suf, out):
    held = here[...] + from1[...] + from7[...] + from2[...] + from6[...]
    pre = down(from_thirds(held[LAT_ROWS:]))
    top = jnp.maximum(pre, suf[...])
    w_pre, w_suf = jnp.exp(pre - top), jnp.exp(suf[...] - top)
    total = w_pre + w_suf
    shape = (ROWS, ROWS)
    old, new = (lax.broadcasted_iota(jnp.int32, shape, d) for d in (0, 1))
    order = jnp.where(old == old_row(new), 1.0, 0.0).astype(BF)
    for j in range(COLS):
        got = held[j * ROWS : (j + 1) * ROWS].astype(F32)
        cols = slice(j * WIDE, (j + 1) * WIDE)
        mixed = ((w_pre * got + w_suf * suffix[:, cols]) / total).astype(BF)
        out[:, cols] = jnp.dot(order, mixed, preferred_element_type=F32).astype(BF)


def body(
    q_latent, q_rope, prefix_latent, prefix_rope, suffix_latent, suffix_rope, prefix_of, suffix_len
):
    rows, latent = q_latent.shape[1] * q_latent.shape[2], q_latent.shape[3]
    xh, z, c = (lax.axis_index(a) for a in ("xh", "z", "c"))
    unit = shaped(Q_ROWS, WIDE)
    own = call(pack_kernel, unit, [], [q_latent[0].reshape(rows, latent), q_rope[0]])
    wait = lax.optimization_barrier
    t = table(prefix_of[0, :, 0], xh, z, c)

    two_up, two_down = along(own, "z", 2), along(own, "z", -2)
    own, t = wait((own, t))
    one_up, one_down = along(own, "z", 1), along(own, "z", -1)
    three_up, three_down = along(two_up, "z", 1), along(two_down, "z", -1)
    four = along_by_parity(jnp.where(z % 2 == 0, two_up, two_down))

    keys, rope = prefix_latent[0], prefix_rope[0]
    rope2 = jnp.concatenate([rope, rope])
    suffix_rope2 = jnp.concatenate([suffix_rope[0], suffix_rope[0]])
    attend = functools.partial(
        pl.pallas_call,
        compiler_params=pltpu.CompilerParams(vmem_limit_bytes=48 * 1024 * 1024),
    )
    suffix, suffix_lse = attend(
        suffix_kernel,
        out_shape=[shaped(rows, LATENT, dtype=F32), shaped(rows, WIDE, dtype=F32)],
        in_specs=[SMEM, VMEM, VMEM, VMEM],
        out_specs=[VMEM, VMEM],
        cost_estimate=pl.CostEstimate(
            flops=rows * 2048 * 64, bytes_accessed=0, transcendentals=0
        ),
    )(suffix_len, own, suffix_latent[0], suffix_rope2)

    quad, two = shaped(4, Q_ROWS, WIDE), shaped(2, Q_ROWS, WIDE)
    keep, send = call(
        route_kernel,
        [quad, quad],
        [t],
        [own, two_up, two_down, one_up, one_down, three_up, three_down, four])
    near, far = call(
        merge_c_kernel, [two, two], [], [keep, along(send, "c", 1)])
    out2 = shaped(2, OUT_ROWS, WIDE)

    def attention(queries):
        return attend(
            prefix_kernel,
            out_shape=out2,
            in_specs=[VMEM] * 3,
            out_specs=VMEM,
            cost_estimate=pl.CostEstimate(
                flops=2 * 256 * 2048 * 1152, bytes_accessed=3 << 20, transcendentals=256 * 2048
            ),
        )(queries, keys, rope2)

    def merged(*parts):
        return call(merge_kernel, out2, [], parts)

    q, p = {}, {}
    q[0, 0] = call(add_kernel, two, [], [near, across(far, 1, 0)])
    q[1, 0] = along(q[0, 0], "y", 1)
    near, far, q[0, 0] = wait((near, far, q[0, 0]))
    from_xl, from_both = across(near, 0, 1), across(far, 1, 1)
    p[0, 0] = attention(q[0, 0])
    q[0, 0], p[0, 0] = wait((q[0, 0], p[0, 0]))
    q[3, 0] = along(q[0, 0], "y", -1)
    from_xl, from_both, p[0, 0], q[1, 0] = wait((from_xl, from_both, p[0, 0], q[1, 0]))
    q[2, 0] = along(q[1, 0], "y", 1)
    q[0, 1] = call(add_kernel, two, [], [from_xl, from_both])
    q[3, 1] = along(q[0, 1], "y", -1)
    p[0, 1] = attention(q[0, 1])
    q[1, 0], q[3, 0], p[0, 0], again = wait((q[1, 0], q[3, 0], p[0, 0], q[0, 1]))
    p[1, 0] = attention(q[1, 0])
    q[3, 1], q[3, 0], p[0, 1], p[1, 0] = wait((q[3, 1], q[3, 0], p[0, 1], p[1, 0]))
    q[2, 1] = along(q[3, 1], "y", -1)
    p[3, 0] = attention(q[3, 0])
    q[1, 1] = along(again, "y", 1)
    q[2, 0], p[0, 1], p[3, 0] = wait((q[2, 0], p[0, 1], p[3, 0]))
    p[2, 0] = attention(q[2, 0])
    sum_near = along(p[2, 0], "y", 1)
    p[1, 0], q[3, 1], p[2, 0] = wait((p[1, 0], q[3, 1], p[2, 0]))
    plain_near = along(p[1, 0], "y", -1)
    p[3, 1] = attention(q[3, 1])
    q[2, 1], p[3, 1] = wait((q[2, 1], p[3, 1]))
    p[2, 1] = attention(q[2, 1])
    sum_far = along(p[2, 1], "y", -1)
    q[1, 1], p[2, 1], plain_near = wait((q[1, 1], p[2, 1], plain_near))
    p[1, 1] = attention(q[1, 1])
    part = merged(p[3, 0], sum_near)
    sum_near = along(part, "y", 1)
    p[3, 1], part = wait((p[3, 1], part))
    plain_far = along(p[3, 1], "y", 1)
    sum_far = along(merged(p[1, 1], sum_far), "y", -1)
    p_near = merged(p[0, 0], plain_near, sum_near)
    p_far = merged(p[0, 1], plain_far, sum_far)
    both = call(
        merge_xl_kernel,
        shaped(4, OUT_ROWS, WIDE),
        [],
        [p_near, across(p_far, 0, 1), across(p_near, 1, 0), across(p_far, 1, 1)])

    one = shaped(OUT_ROWS, WIDE)
    here, o1, o2, o3, o4, o5, o6, o7 = call(
        back_kernel, [one] * 8, [t], [both, along(both, "c", 1)]
    )
    four = along_by_parity(o4)
    r3, r5 = along(o3, "z", 1), along(o5, "z", -1)
    o1, o7, suffix, suffix_lse = wait((o1, o7, suffix, suffix_lse))
    from1, from7 = along(o1, "z", 1), along(o7, "z", -1)
    o2, o6 = call(relay_kernel, [one] * 2, [], [o2, o6, four, r3, r5])
    arrived = [from1, from7, along(o2, "z", 2), along(o6, "z", -2)]
    out = call(
        final_kernel,
        shaped(rows, LATENT),
        [],
        [here, *arrived, suffix, suffix_lse])
    return out.reshape(q_latent.shape)


def solution(mesh):
    fine = Mesh(mesh.devices.reshape(2, NZ, 2, NY, 2), AXES)
    grp, blk = ("xh", "z", "c"), ("y", "xl")
    in_specs = (
        P(AXES, None, None, None),
        P(AXES, None, None),
        P(grp, blk, None),
        P(grp, None, blk),
        P(AXES, None, None),
        P(AXES, None, None),
        P(blk, None, None),
        P(AXES),
    )
    return jax.shard_map(
        body, mesh=fine, in_specs=in_specs, out_specs=P(AXES, None, None, None), check_vma=False
    )
```

```python
import functools
import math

import jax
import jax.numpy as jnp
from jax import lax
from jax.experimental import pallas as pl
from jax.experimental.pallas import tpu as pltpu
from jax.sharding import Mesh, PartitionSpec as P

QK_DIM = 192
SCALE = QK_DIM**-0.5
LOG2E = math.log2(math.e)
BF = jnp.bfloat16
F32 = jnp.float32
AXES = ("xh", "z", "c", "y", "xl")
NZ, NY = 8, 4
HEADS, LATENT, ROPE = 64, 512, 64
WIDE = 128
COLS = LATENT // WIDE
ROWS = 2 * HEADS
LAT_ROWS = COLS * ROWS
Q_ROWS = LAT_ROWS + HEADS
OUT_ROWS = LAT_ROWS + 16
NT = (((1,), (1,)), ((), ()))

SMEM = pl.BlockSpec(memory_space=pltpu.SMEM)
VMEM = pl.BlockSpec(memory_space=pltpu.VMEM)

T_ROUTE, T_BACK = 0, 8


def call(kernel, outs, ints, arrays):
    single = not isinstance(outs, (list, tuple))
    specs = jax.tree.map(lambda _: VMEM, outs)
    return pl.pallas_call(
        kernel,
        out_shape=outs,
        in_specs=[SMEM] * len(ints) + [VMEM] * len(arrays),
        out_specs=VMEM if single else specs,
        compiler_params=pltpu.CompilerParams(vmem_limit_bytes=48 * 1024 * 1024),
        cost_estimate=pl.CostEstimate(flops=0, bytes_accessed=0, transcendentals=0),
    )(*ints, *arrays)


def shaped(*shape, dtype=BF):
    return jax.ShapeDtypeStruct(shape, dtype)


def along(x, axis, distance):
    n = lax.axis_size(axis)
    return lax.ppermute(x, axis, [(i, (i + distance) % n) for i in range(n)])


def along_by_parity(x):
    return lax.ppermute(x, "z", [(i, (i + (-2 if i % 2 else 2)) % NZ) for i in range(NZ)])


def across(x, flip_xh, flip_xl):
    pairs = [
        (2 * i + j, 2 * (i ^ flip_xh) + (j ^ flip_xl)) for i in range(2) for j in range(2)
    ]
    return lax.ppermute(x, ("xh", "xl"), pairs)


def ranks(dest):
    ids = jnp.arange(dest.shape[0], dtype=jnp.int32)
    before = (ids[None, :] < ids[:, None]) & (dest[None, :] == dest[:, None])
    return jnp.sum(before.astype(jnp.int32), axis=1)


def table(dest, xh, z, c):
    ids = jnp.arange(dest.shape[0], dtype=jnp.int32)
    eight = jnp.arange(8, dtype=jnp.int32)
    cr, xr, slot = eight // 4, (eight // 2) % 2, eight % 2
    rank = ranks(dest)
    holders = ((xh ^ xr) * NZ + z) * 2 + (c ^ cr)
    in_ring = (ids // (2 * NZ) == xh) & (ids % 2 == c)
    match = (dest[None, :] == holders[:, None]) & (rank[None, :] == slot[:, None]) & in_ring[None, :]
    distance = (z - ids // 2) % NZ
    route = jnp.sum(jnp.where(match, distance[None, :] + 1, 0), axis=1) - 1
    roots = (xh * NZ + (z + eight) % NZ) * 2 + c
    root = roots[:, None] == ids[None, :]
    h = jnp.sum(jnp.where(root, dest[None], 0), axis=1)
    r = jnp.sum(jnp.where(root, rank[None], 0), axis=1)
    place = ((h % 2) ^ c) * 4 + ((h // (2 * NZ)) ^ xh) * 2 + r
    back = jnp.where((h // 2) % NZ == z, place, -1)
    return jnp.concatenate([route, back]).astype(jnp.int32)


def old_row(n):
    return (n // 32) % 2 * HEADS + n % 32 * 2 + n // HEADS


def pack_kernel(lat, rot, out):
    shape = (ROWS, ROWS)
    new, old = (lax.broadcasted_iota(jnp.int32, shape, d) for d in (0, 1))
    order = jnp.where(old == old_row(new), 1.0, 0.0).astype(BF)
    rows = jnp.dot(order, lat[...], preferred_element_type=F32).astype(BF)
    for j in range(COLS):
        out[j * ROWS : (j + 1) * ROWS] = rows[:, j * WIDE : (j + 1) * WIDE]
    flat = rot[...].astype(F32)
    pairs = [
        flat[s : s + 1, j * WIDE : (j + 1) * WIDE] for s in range(2) for j in range(HEADS // 2)
    ]
    out[LAT_ROWS:] = jnp.concatenate(pairs, axis=0).astype(BF)


def route_kernel(t, own, two_up, two_down, one_up, one_down, three_up, three_down, four, keep, send):
    whole = [own, one_up, two_up, three_up, four, three_down, two_down, one_down]
    for slot in range(8):
        out = (keep if slot < 4 else send).at[slot % 4]
        source = t[T_ROUTE + slot]
        for d in range(NZ):

            @pl.when(source == d)
            def _():
                out[...] = whole[d][...]

        @pl.when(source < 0)
        def _():
            out[...] = jnp.zeros(out.shape, BF)


def merge_c_kernel(keep, got, near, far):
    for r in range(2):
        near[r] = keep[r] + got[r]
        far[r] = keep[2 + r] + got[2 + r]


def add_kernel(a, b, out):
    out[...] = a[...] + b[...]


def queries_of(units):
    lat, rot = [], []
    lanes = lax.broadcasted_iota(jnp.int32, (HEADS, WIDE), 1)
    for u in units:
        lat.append(jnp.concatenate([u[ROWS * j : ROWS * (j + 1)] for j in range(COLS)], axis=1))
        pair = u[LAT_ROWS:]
        zero = jnp.zeros_like(pair)
        rot += [jnp.where(lanes < ROPE, pair, zero), jnp.where(lanes < ROPE, zero, pair)]
    return jnp.concatenate(lat, axis=0), jnp.concatenate(rot, axis=0)


def prefix_kernel(q, keys, rope2, o):
    lat, rot = queries_of([q[0], q[1]])
    half = keys.shape[0] // 2
    spans = [slice(i * half, (i + 1) * half) for i in range(2)]
    scores = []
    for at in spans:
        s = lax.dot_general(lat, keys[at], NT, preferred_element_type=F32)
        scores.append(s + jnp.dot(rot, rope2[:, at], preferred_element_type=F32))
    tops, totals, outs = [], [], []
    for s, at in zip(scores, spans):
        tops.append(jnp.max(s, axis=1, keepdims=True))
        w = jnp.exp2((s - tops[-1]) * (SCALE * LOG2E))
        totals.append(jnp.sum(w, axis=1, keepdims=True))
        outs.append(jnp.dot(w.astype(BF), keys[at], preferred_element_type=F32))
    top = jnp.maximum(*tops)
    shares = [jnp.exp2((x - top) * (SCALE * LOG2E)) for x in tops]
    total = shares[0] * totals[0] + shares[1] * totals[1]
    out = ((shares[0] * outs[0] + shares[1] * outs[1]) / total).astype(BF)
    lse = top * SCALE + jnp.log(total)
    flat = jnp.transpose(jnp.broadcast_to(lse, (2 * ROWS, WIDE)))
    for u in range(2):
        for j in range(COLS):
            o[u, j * ROWS : (j + 1) * ROWS] = out[
                u * ROWS : (u + 1) * ROWS, j * WIDE : (j + 1) * WIDE
            ]
        o[u, LAT_ROWS:] = in_thirds(flat[0:1, u * ROWS : (u + 1) * ROWS])


def in_thirds(row):
    high = row.astype(BF).astype(F32)
    mid = (row - high).astype(BF).astype(F32)
    low = row - high - mid
    place = lax.broadcasted_iota(jnp.int32, (16, WIDE), 0)
    block = jnp.where(place == 0, high, jnp.where(place == 1, mid, jnp.where(place == 2, low, 0.0)))
    return block.astype(BF)


def from_thirds(block):
    block = block.astype(F32)
    return block[0:1] + block[1:2] + block[2:3]


def down(row):
    return jnp.transpose(jnp.broadcast_to(row, (WIDE, WIDE)))


def merge_parts(parts, out):
    lses = [from_thirds(p[LAT_ROWS:]) for p in parts]
    top = functools.reduce(jnp.maximum, lses)
    shares = [jnp.exp(x - top) for x in lses]
    total = functools.reduce(jnp.add, shares)
    weights = [down(x / total) for x in shares]
    for j in range(COLS):
        at = slice(j * ROWS, (j + 1) * ROWS)
        mixed = [w * p[at].astype(F32) for w, p in zip(weights, parts)]
        out[at] = functools.reduce(jnp.add, mixed).astype(BF)
    out[LAT_ROWS:] = in_thirds(top + jnp.log(total))


def merge_kernel(*refs):
    parts, out = refs[:-1], refs[-1]
    for k in range(out.shape[0]):
        merge_parts([p.at[k] for p in parts], out.at[k])


def merge_xl_kernel(near, from_xl, from_xh, from_both, out):
    for r in range(2):
        merge_parts([near.at[r], from_xl.at[r]], out.at[r])
        merge_parts([from_xh.at[r], from_both.at[r]], out.at[2 + r])


def back_kernel(t, own, got, here, o1, o2, o3, o4, o5, o6, o7):
    for d, out in enumerate([here, o1, o2, o3, o4, o5, o6, o7]):
        place = t[T_BACK + d]

        @pl.when((place >= 0) & (place < 4))
        def _():
            out[...] = own[place]

        @pl.when(place >= 4)
        def _():
            out[...] = got[place - 4]

        @pl.when(place < 0)
        def _():
            out[...] = jnp.zeros((OUT_ROWS, WIDE), BF)


def relay_kernel(o2, o6, r3, r5, four, up, down):
    up[...] = o2[...] + r3[...]
    down[...] = o6[...] + r5[...]
    odd = lax.rem(lax.axis_index("z"), 2)

    @pl.when(odd == 0)
    def _():
        up[...] += four[...]

    @pl.when(odd == 1)
    def _():
        down[...] += four[...]


def suffix_kernel(length, unit, keys, rope2, out, out_lse):
    lat, rot = queries_of([unit[...]])
    s = lax.dot_general(lat, keys[...], NT, preferred_element_type=F32)
    s = (s + jnp.dot(rot, rope2[...], preferred_element_type=F32)) * SCALE
    position = lax.broadcasted_iota(jnp.int32, s.shape, 1)
    step = lax.broadcasted_iota(jnp.int32, s.shape, 0) // (HEADS // 2) % 2
    s = jnp.where(position < length[0] + step + 1, s, -1e30)
    top = jnp.max(s, axis=1, keepdims=True)
    w = jnp.exp(s - top)
    total = jnp.sum(w, axis=1, keepdims=True)
    out[...] = jnp.dot(w.astype(BF), keys[...], preferred_element_type=F32) / total
    out_lse[...] = jnp.broadcast_to(top + jnp.log(total), out_lse.shape)


def final_kernel(here, from1, from7, from2, from6, suffix, suf, out):
    held = here[...] + from1[...] + from7[...] + from2[...] + from6[...]
    pre = down(from_thirds(held[LAT_ROWS:]))
    top = jnp.maximum(pre, suf[...])
    w_pre, w_suf = jnp.exp(pre - top), jnp.exp(suf[...] - top)
    total = w_pre + w_suf
    shape = (ROWS, ROWS)
    old, new = (lax.broadcasted_iota(jnp.int32, shape, d) for d in (0, 1))
    order = jnp.where(old == old_row(new), 1.0, 0.0).astype(BF)
    for j in range(COLS):
        got = held[j * ROWS : (j + 1) * ROWS].astype(F32)
        cols = slice(j * WIDE, (j + 1) * WIDE)
        mixed = ((w_pre * got + w_suf * suffix[:, cols]) / total).astype(BF)
        out[:, cols] = jnp.dot(order, mixed, preferred_element_type=F32).astype(BF)


def body(
    q_latent, q_rope, prefix_latent, prefix_rope, suffix_latent, suffix_rope, prefix_of, suffix_len
):
    rows, latent = q_latent.shape[1] * q_latent.shape[2], q_latent.shape[3]
    xh, z, c = (lax.axis_index(a) for a in ("xh", "z", "c"))
    unit = shaped(Q_ROWS, WIDE)
    own = call(pack_kernel, unit, [], [q_latent[0].reshape(rows, latent), q_rope[0]])
    wait = lax.optimization_barrier
    t = table(prefix_of[0, :, 0], xh, z, c)

    two_up, two_down = along(own, "z", 2), along(own, "z", -2)
    own, t = wait((own, t))
    one_up, one_down = along(own, "z", 1), along(own, "z", -1)
    three_up, three_down = along(two_up, "z", 1), along(two_down, "z", -1)
    four = along_by_parity(jnp.where(z % 2 == 0, two_up, two_down))

    keys, rope = prefix_latent[0], prefix_rope[0]
    rope2 = jnp.concatenate([rope, rope])
    suffix_rope2 = jnp.concatenate([suffix_rope[0], suffix_rope[0]])
    attend = functools.partial(
        pl.pallas_call,
        compiler_params=pltpu.CompilerParams(vmem_limit_bytes=48 * 1024 * 1024),
    )
    suffix, suffix_lse = attend(
        suffix_kernel,
        out_shape=[shaped(rows, LATENT, dtype=F32), shaped(rows, WIDE, dtype=F32)],
        in_specs=[SMEM, VMEM, VMEM, VMEM],
        out_specs=[VMEM, VMEM],
        cost_estimate=pl.CostEstimate(
            flops=rows * 2048 * 64, bytes_accessed=0, transcendentals=0
        ),
    )(suffix_len, own, suffix_latent[0], suffix_rope2)

    quad, two = shaped(4, Q_ROWS, WIDE), shaped(2, Q_ROWS, WIDE)
    keep, send = call(
        route_kernel,
        [quad, quad],
        [t],
        [own, two_up, two_down, one_up, one_down, three_up, three_down, four])
    near, far = call(
        merge_c_kernel, [two, two], [], [keep, along(send, "c", 1)])
    out2 = shaped(2, OUT_ROWS, WIDE)

    def attention(queries):
        return attend(
            prefix_kernel,
            out_shape=out2,
            in_specs=[VMEM] * 3,
            out_specs=VMEM,
            cost_estimate=pl.CostEstimate(
                flops=2 * 256 * 2048 * 1152, bytes_accessed=3 << 20, transcendentals=256 * 2048
            ),
        )(queries, keys, rope2)

    def merged(*parts):
        return call(merge_kernel, out2, [], parts)

    q, p = {}, {}
    q[0, 0] = call(add_kernel, two, [], [near, across(far, 1, 0)])
    q[1, 0] = along(q[0, 0], "y", 1)
    near, far, q[0, 0] = wait((near, far, q[0, 0]))
    from_xl, from_both = across(near, 0, 1), across(far, 1, 1)
    p[0, 0] = attention(q[0, 0])
    q[0, 0], p[0, 0] = wait((q[0, 0], p[0, 0]))
    q[3, 0] = along(q[0, 0], "y", -1)
    from_xl, from_both, p[0, 0], q[1, 0] = wait((from_xl, from_both, p[0, 0], q[1, 0]))
    q[2, 0] = along(q[1, 0], "y", 1)
    q[0, 1] = call(add_kernel, two, [], [from_xl, from_both])
    q[3, 1] = along(q[0, 1], "y", -1)
    p[0, 1] = attention(q[0, 1])
    q[1, 0], q[3, 0], p[0, 0], again = wait((q[1, 0], q[3, 0], p[0, 0], q[0, 1]))
    p[1, 0] = attention(q[1, 0])
    q[3, 1], q[3, 0], p[0, 1], p[1, 0] = wait((q[3, 1], q[3, 0], p[0, 1], p[1, 0]))
    q[2, 1] = along(q[3, 1], "y", -1)
    p[3, 0] = attention(q[3, 0])
    q[1, 1] = along(again, "y", 1)
    q[2, 0], p[0, 1], p[3, 0] = wait((q[2, 0], p[0, 1], p[3, 0]))
    p[2, 0] = attention(q[2, 0])
    sum_near = along(p[2, 0], "y", 1)
    p[1, 0], q[3, 1], p[2, 0] = wait((p[1, 0], q[3, 1], p[2, 0]))
    plain_near = along(p[1, 0], "y", -1)
    p[3, 1] = attention(q[3, 1])
    q[2, 1], p[3, 1] = wait((q[2, 1], p[3, 1]))
    p[2, 1] = attention(q[2, 1])
    sum_far = along(p[2, 1], "y", -1)
    q[1, 1], p[2, 1] = wait((q[1, 1], p[2, 1]))
    p[1, 1] = attention(q[1, 1])
    sum_near, plain_near = wait((sum_near, plain_near))
    part = merged(p[3, 0], sum_near)
    sum_near = along(part, "y", 1)
    p[3, 1], part = wait((p[3, 1], part))
    plain_far = along(p[3, 1], "y", 1)
    sum_far = along(merged(p[1, 1], sum_far), "y", -1)
    p_near = merged(p[0, 0], plain_near, sum_near)
    p_far = merged(p[0, 1], plain_far, sum_far)
    both = call(
        merge_xl_kernel,
        shaped(4, OUT_ROWS, WIDE),
        [],
        [p_near, across(p_far, 0, 1), across(p_near, 1, 0), across(p_far, 1, 1)])

    one = shaped(OUT_ROWS, WIDE)
    here, o1, o2, o3, o4, o5, o6, o7 = call(
        back_kernel, [one] * 8, [t], [both, along(both, "c", 1)]
    )
    four = along_by_parity(o4)
    r3, r5 = along(o3, "z", 1), along(o5, "z", -1)
    o1, o7, suffix, suffix_lse = wait((o1, o7, suffix, suffix_lse))
    from1, from7 = along(o1, "z", 1), along(o7, "z", -1)
    o2, o6 = call(relay_kernel, [one] * 2, [], [o2, o6, r3, r5, four])
    arrived = [from1, from7, along(o2, "z", 2), along(o6, "z", -2)]
    out = call(
        final_kernel,
        shaped(rows, LATENT),
        [],
        [here, *arrived, suffix, suffix_lse])
    return out.reshape(q_latent.shape)


def solution(mesh):
    fine = Mesh(mesh.devices.reshape(2, NZ, 2, NY, 2), AXES)
    grp, blk = ("xh", "z", "c"), ("y", "xl")
    in_specs = (
        P(AXES, None, None, None),
        P(AXES, None, None),
        P(grp, blk, None),
        P(grp, None, blk),
        P(AXES, None, None),
        P(AXES, None, None),
        P(blk, None, None),
        P(AXES),
    )
    return jax.shard_map(
        body, mesh=fine, in_specs=in_specs, out_specs=P(AXES, None, None, None), check_vma=False
    )
```

```python
import functools
import math

import jax
import jax.numpy as jnp
from jax import lax
from jax.experimental import pallas as pl
from jax.experimental.pallas import tpu as pltpu
from jax.sharding import Mesh, PartitionSpec as P

QK_DIM = 192
SCALE = QK_DIM**-0.5
LOG2E = math.log2(math.e)
BF = jnp.bfloat16
F32 = jnp.float32
AXES = ("xh", "z", "c", "y", "xl")
NZ, NY = 8, 4
HEADS, LATENT, ROPE = 64, 512, 64
WIDE = 128
COLS = LATENT // WIDE
ROWS = 2 * HEADS
LAT_ROWS = COLS * ROWS
Q_ROWS = LAT_ROWS + HEADS
OUT_ROWS = LAT_ROWS + 16
NT = (((1,), (1,)), ((), ()))

SMEM = pl.BlockSpec(memory_space=pltpu.SMEM)
VMEM = pl.BlockSpec(memory_space=pltpu.VMEM)

T_ROUTE, T_BACK = 0, 8


def call(kernel, outs, ints, arrays):
    single = not isinstance(outs, (list, tuple))
    specs = jax.tree.map(lambda _: VMEM, outs)
    return pl.pallas_call(
        kernel,
        out_shape=outs,
        in_specs=[SMEM] * len(ints) + [VMEM] * len(arrays),
        out_specs=VMEM if single else specs,
        compiler_params=pltpu.CompilerParams(vmem_limit_bytes=48 * 1024 * 1024),
        cost_estimate=pl.CostEstimate(flops=0, bytes_accessed=0, transcendentals=0),
    )(*ints, *arrays)


def shaped(*shape, dtype=BF):
    return jax.ShapeDtypeStruct(shape, dtype)


def along(x, axis, distance):
    n = lax.axis_size(axis)
    return lax.ppermute(x, axis, [(i, (i + distance) % n) for i in range(n)])


def along_by_parity(x):
    return lax.ppermute(x, "z", [(i, (i + (-2 if i % 2 else 2)) % NZ) for i in range(NZ)])


def across(x, flip_xh, flip_xl):
    pairs = [
        (2 * i + j, 2 * (i ^ flip_xh) + (j ^ flip_xl)) for i in range(2) for j in range(2)
    ]
    return lax.ppermute(x, ("xh", "xl"), pairs)


def ranks(dest):
    ids = jnp.arange(dest.shape[0], dtype=jnp.int32)
    before = (ids[None, :] < ids[:, None]) & (dest[None, :] == dest[:, None])
    return jnp.sum(before.astype(jnp.int32), axis=1)


def table(dest, xh, z, c):
    ids = jnp.arange(dest.shape[0], dtype=jnp.int32)
    eight = jnp.arange(8, dtype=jnp.int32)
    cr, xr, slot = eight // 4, (eight // 2) % 2, eight % 2
    rank = ranks(dest)
    holders = ((xh ^ xr) * NZ + z) * 2 + (c ^ cr)
    in_ring = (ids // (2 * NZ) == xh) & (ids % 2 == c)
    match = (dest[None, :] == holders[:, None]) & (rank[None, :] == slot[:, None]) & in_ring[None, :]
    distance = (z - ids // 2) % NZ
    route = jnp.sum(jnp.where(match, distance[None, :] + 1, 0), axis=1) - 1
    roots = (xh * NZ + (z + eight) % NZ) * 2 + c
    root = roots[:, None] == ids[None, :]
    h = jnp.sum(jnp.where(root, dest[None], 0), axis=1)
    r = jnp.sum(jnp.where(root, rank[None], 0), axis=1)
    place = ((h % 2) ^ c) * 4 + ((h // (2 * NZ)) ^ xh) * 2 + r
    back = jnp.where((h // 2) % NZ == z, place, -1)
    return jnp.concatenate([route, back]).astype(jnp.int32)


def old_row(n):
    return (n // 32) % 2 * HEADS + n % 32 * 2 + n // HEADS


def pack_kernel(lat, rot, out):
    shape = (ROWS, ROWS)
    new, old = (lax.broadcasted_iota(jnp.int32, shape, d) for d in (0, 1))
    order = jnp.where(old == old_row(new), 1.0, 0.0).astype(BF)
    rows = jnp.dot(order, lat[...], preferred_element_type=F32).astype(BF)
    for j in range(COLS):
        out[j * ROWS : (j + 1) * ROWS] = rows[:, j * WIDE : (j + 1) * WIDE]
    flat = rot[...].astype(F32)
    pairs = [
        flat[s : s + 1, j * WIDE : (j + 1) * WIDE] for s in range(2) for j in range(HEADS // 2)
    ]
    out[LAT_ROWS:] = jnp.concatenate(pairs, axis=0).astype(BF)


def route_kernel(t, own, two_up, two_down, one_up, one_down, three_up, three_down, four, keep, send):
    whole = [own, one_up, two_up, three_up, four, three_down, two_down, one_down]
    for slot in range(8):
        out = (keep if slot < 4 else send).at[slot % 4]
        source = t[T_ROUTE + slot]
        for d in range(NZ):

            @pl.when(source == d)
            def _():
                out[...] = whole[d][...]

        @pl.when(source < 0)
        def _():
            out[...] = jnp.zeros(out.shape, BF)


def merge_c_kernel(keep, got, near, far):
    for r in range(2):
        near[r] = keep[r] + got[r]
        far[r] = keep[2 + r] + got[2 + r]


def add_kernel(a, b, out):
    out[...] = a[...] + b[...]


def queries_of(units):
    lat, rot = [], []
    lanes = lax.broadcasted_iota(jnp.int32, (HEADS, WIDE), 1)
    for u in units:
        lat.append(jnp.concatenate([u[ROWS * j : ROWS * (j + 1)] for j in range(COLS)], axis=1))
        pair = u[LAT_ROWS:]
        zero = jnp.zeros_like(pair)
        rot += [jnp.where(lanes < ROPE, pair, zero), jnp.where(lanes < ROPE, zero, pair)]
    return jnp.concatenate(lat, axis=0), jnp.concatenate(rot, axis=0)


def prefix_kernel(q, keys, rope2, o):
    lat, rot = queries_of([q[0], q[1]])
    half = keys.shape[0] // 2
    spans = [slice(i * half, (i + 1) * half) for i in range(2)]
    scores = []
    for at in spans:
        s = lax.dot_general(lat, keys[at], NT, preferred_element_type=F32)
        scores.append(s + jnp.dot(rot, rope2[:, at], preferred_element_type=F32))
    tops, totals, outs = [], [], []
    for s, at in zip(scores, spans):
        tops.append(jnp.max(s, axis=1, keepdims=True))
        w = jnp.exp2((s - tops[-1]) * (SCALE * LOG2E))
        totals.append(jnp.sum(w, axis=1, keepdims=True))
        outs.append(jnp.dot(w.astype(BF), keys[at], preferred_element_type=F32))
    top = jnp.maximum(*tops)
    shares = [jnp.exp2((x - top) * (SCALE * LOG2E)) for x in tops]
    total = shares[0] * totals[0] + shares[1] * totals[1]
    out = ((shares[0] * outs[0] + shares[1] * outs[1]) / total).astype(BF)
    lse = top * SCALE + jnp.log(total)
    flat = jnp.transpose(jnp.broadcast_to(lse, (2 * ROWS, WIDE)))
    for u in range(2):
        for j in range(COLS):
            o[u, j * ROWS : (j + 1) * ROWS] = out[
                u * ROWS : (u + 1) * ROWS, j * WIDE : (j + 1) * WIDE
            ]
        o[u, LAT_ROWS:] = in_thirds(flat[0:1, u * ROWS : (u + 1) * ROWS])


def in_thirds(row):
    high = row.astype(BF).astype(F32)
    mid = (row - high).astype(BF).astype(F32)
    low = row - high - mid
    place = lax.broadcasted_iota(jnp.int32, (16, WIDE), 0)
    block = jnp.where(place == 0, high, jnp.where(place == 1, mid, jnp.where(place == 2, low, 0.0)))
    return block.astype(BF)


def from_thirds(block):
    block = block.astype(F32)
    return block[0:1] + block[1:2] + block[2:3]


def down(row):
    return jnp.transpose(jnp.broadcast_to(row, (WIDE, WIDE)))


def merge_parts(parts, out):
    lses = [from_thirds(p[LAT_ROWS:]) for p in parts]
    top = functools.reduce(jnp.maximum, lses)
    shares = [jnp.exp(x - top) for x in lses]
    total = functools.reduce(jnp.add, shares)
    weights = [down(x / total) for x in shares]
    for j in range(COLS):
        at = slice(j * ROWS, (j + 1) * ROWS)
        mixed = [w * p[at].astype(F32) for w, p in zip(weights, parts)]
        out[at] = functools.reduce(jnp.add, mixed).astype(BF)
    out[LAT_ROWS:] = in_thirds(top + jnp.log(total))


def merge_kernel(*refs):
    parts, out = refs[:-1], refs[-1]
    for k in range(out.shape[0]):
        merge_parts([p.at[k] for p in parts], out.at[k])


def merge_xl_kernel(near, from_xl, from_xh, from_both, out):
    for r in range(2):
        merge_parts([near.at[r], from_xl.at[r]], out.at[r])
        merge_parts([from_xh.at[r], from_both.at[r]], out.at[2 + r])


def back_kernel(t, own, got, here, o1, o2, o3, o4, o5, o6, o7):
    for d, out in enumerate([here, o1, o2, o3, o4, o5, o6, o7]):
        place = t[T_BACK + d]

        @pl.when((place >= 0) & (place < 4))
        def _():
            out[...] = own[place]

        @pl.when(place >= 4)
        def _():
            out[...] = got[place - 4]

        @pl.when(place < 0)
        def _():
            out[...] = jnp.zeros((OUT_ROWS, WIDE), BF)


def relay_kernel(o2, o6, r3, r5, four, up, down):
    up[...] = o2[...] + r3[...]
    down[...] = o6[...] + r5[...]
    odd = lax.rem(lax.axis_index("z"), 2)

    @pl.when(odd == 0)
    def _():
        up[...] += four[...]

    @pl.when(odd == 1)
    def _():
        down[...] += four[...]


def suffix_kernel(length, unit, keys, rope2, out, out_lse):
    lat, rot = queries_of([unit[...]])
    s = lax.dot_general(lat, keys[...], NT, preferred_element_type=F32)
    s = (s + jnp.dot(rot, rope2[...], preferred_element_type=F32)) * SCALE
    position = lax.broadcasted_iota(jnp.int32, s.shape, 1)
    step = lax.broadcasted_iota(jnp.int32, s.shape, 0) // (HEADS // 2) % 2
    s = jnp.where(position < length[0] + step + 1, s, -1e30)
    top = jnp.max(s, axis=1, keepdims=True)
    w = jnp.exp(s - top)
    total = jnp.sum(w, axis=1, keepdims=True)
    out[...] = jnp.dot(w.astype(BF), keys[...], preferred_element_type=F32) / total
    out_lse[...] = jnp.broadcast_to(top + jnp.log(total), out_lse.shape)


def final_kernel(here, from1, from7, from2, from6, suffix, suf, out):
    held = here[...] + from1[...] + from7[...] + from2[...] + from6[...]
    pre = down(from_thirds(held[LAT_ROWS:]))
    top = jnp.maximum(pre, suf[...])
    w_pre, w_suf = jnp.exp(pre - top), jnp.exp(suf[...] - top)
    total = w_pre + w_suf
    shape = (ROWS, ROWS)
    old, new = (lax.broadcasted_iota(jnp.int32, shape, d) for d in (0, 1))
    order = jnp.where(old == old_row(new), 1.0, 0.0).astype(BF)
    for j in range(COLS):
        got = held[j * ROWS : (j + 1) * ROWS].astype(F32)
        cols = slice(j * WIDE, (j + 1) * WIDE)
        mixed = ((w_pre * got + w_suf * suffix[:, cols]) / total).astype(BF)
        out[:, cols] = jnp.dot(order, mixed, preferred_element_type=F32).astype(BF)


def body(
    q_latent, q_rope, prefix_latent, prefix_rope, suffix_latent, suffix_rope, prefix_of, suffix_len
):
    rows, latent = q_latent.shape[1] * q_latent.shape[2], q_latent.shape[3]
    xh, z, c = (lax.axis_index(a) for a in ("xh", "z", "c"))
    unit = shaped(Q_ROWS, WIDE)
    own = call(pack_kernel, unit, [], [q_latent[0].reshape(rows, latent), q_rope[0]])
    wait = lax.optimization_barrier
    t = table(prefix_of[0, :, 0], xh, z, c)

    two_up, two_down = along(own, "z", 2), along(own, "z", -2)
    own, t = wait((own, t))
    one_up, one_down = along(own, "z", 1), along(own, "z", -1)
    three_up, three_down = along(two_up, "z", 1), along(two_down, "z", -1)
    four = along_by_parity(jnp.where(z % 2 == 0, two_up, two_down))

    keys, rope = prefix_latent[0], prefix_rope[0]
    rope2 = jnp.concatenate([rope, rope])
    suffix_rope2 = jnp.concatenate([suffix_rope[0], suffix_rope[0]])
    attend = functools.partial(
        pl.pallas_call,
        compiler_params=pltpu.CompilerParams(vmem_limit_bytes=48 * 1024 * 1024),
    )
    suffix, suffix_lse = attend(
        suffix_kernel,
        out_shape=[shaped(rows, LATENT, dtype=F32), shaped(rows, WIDE, dtype=F32)],
        in_specs=[SMEM, VMEM, VMEM, VMEM],
        out_specs=[VMEM, VMEM],
        cost_estimate=pl.CostEstimate(
            flops=rows * 2048 * 64, bytes_accessed=0, transcendentals=0
        ),
    )(suffix_len, own, suffix_latent[0], suffix_rope2)

    quad, two = shaped(4, Q_ROWS, WIDE), shaped(2, Q_ROWS, WIDE)
    keep, send = call(
        route_kernel,
        [quad, quad],
        [t],
        [own, two_up, two_down, one_up, one_down, three_up, three_down, four])
    near, far = call(
        merge_c_kernel, [two, two], [], [keep, along(send, "c", 1)])
    out2 = shaped(2, OUT_ROWS, WIDE)

    def attention(queries):
        return attend(
            prefix_kernel,
            out_shape=out2,
            in_specs=[VMEM] * 3,
            out_specs=VMEM,
            cost_estimate=pl.CostEstimate(
                flops=2 * 256 * 2048 * 1152, bytes_accessed=3 << 20, transcendentals=256 * 2048
            ),
        )(queries, keys, rope2)

    def merged(*parts):
        return call(merge_kernel, out2, [], parts)

    q, p = {}, {}
    q[0, 0] = call(add_kernel, two, [], [near, across(far, 1, 0)])
    q[1, 0] = along(q[0, 0], "y", 1)
    near, far, q[0, 0] = wait((near, far, q[0, 0]))
    from_xl, from_both = across(near, 0, 1), across(far, 1, 1)
    p[0, 0] = attention(q[0, 0])
    q[0, 0], p[0, 0] = wait((q[0, 0], p[0, 0]))
    q[3, 0] = along(q[0, 0], "y", -1)
    from_xl, from_both, p[0, 0], q[1, 0] = wait((from_xl, from_both, p[0, 0], q[1, 0]))
    q[2, 0] = along(q[1, 0], "y", 1)
    q[0, 1] = call(add_kernel, two, [], [from_xl, from_both])
    q[3, 1] = along(q[0, 1], "y", -1)
    p[0, 1] = attention(q[0, 1])
    q[1, 0], q[3, 0], p[0, 0], again = wait((q[1, 0], q[3, 0], p[0, 0], q[0, 1]))
    p[1, 0] = attention(q[1, 0])
    q[3, 1], q[3, 0], p[0, 1], p[1, 0] = wait((q[3, 1], q[3, 0], p[0, 1], p[1, 0]))
    q[2, 1] = along(again, "y", 2)
    p[3, 0] = attention(q[3, 0])
    again, p[3, 0] = wait((again, p[3, 0]))
    q[1, 1] = along(again, "y", 1)
    q[2, 0], p[0, 1], p[3, 0] = wait((q[2, 0], p[0, 1], p[3, 0]))
    p[2, 0] = attention(q[2, 0])
    sum_near = along(p[2, 0], "y", 1)
    p[1, 0], q[2, 1], p[2, 0] = wait((p[1, 0], q[2, 1], p[2, 0]))
    plain_near = along(p[1, 0], "y", -1)
    p[2, 1] = attention(q[2, 1])
    sum_far = along(p[2, 1], "y", -1)
    q[3, 1], p[2, 1] = wait((q[3, 1], p[2, 1]))
    p[3, 1] = attention(q[3, 1])
    q[1, 1], p[3, 1], plain_near = wait((q[1, 1], p[3, 1], plain_near))
    p[1, 1] = attention(q[1, 1])
    part = merged(p[3, 0], sum_near)
    sum_near = along(part, "y", 1)
    plain_far = along(p[3, 1], "y", 1)
    sum_far, plain_far = wait((sum_far, plain_far))
    sum_far = along(merged(p[1, 1], sum_far), "y", -1)
    p_near = merged(p[0, 0], plain_near, sum_near)
    p_far = merged(p[0, 1], plain_far, sum_far)
    both = call(
        merge_xl_kernel,
        shaped(4, OUT_ROWS, WIDE),
        [],
        [p_near, across(p_far, 0, 1), across(p_near, 1, 0), across(p_far, 1, 1)])

    one = shaped(OUT_ROWS, WIDE)
    here, o1, o2, o3, o4, o5, o6, o7 = call(
        back_kernel, [one] * 8, [t], [both, along(both, "c", 1)]
    )
    four = along_by_parity(o4)
    r3, r5 = along(o3, "z", 1), along(o5, "z", -1)
    o1, o7, suffix, suffix_lse = wait((o1, o7, suffix, suffix_lse))
    from1, from7 = along(o1, "z", 1), along(o7, "z", -1)
    o2, o6 = call(relay_kernel, [one] * 2, [], [o2, o6, r3, r5, four])
    arrived = [from1, from7, along(o2, "z", 2), along(o6, "z", -2)]
    out = call(
        final_kernel,
        shaped(rows, LATENT),
        [],
        [here, *arrived, suffix, suffix_lse])
    return out.reshape(q_latent.shape)


def solution(mesh):
    fine = Mesh(mesh.devices.reshape(2, NZ, 2, NY, 2), AXES)
    grp, blk = ("xh", "z", "c"), ("y", "xl")
    in_specs = (
        P(AXES, None, None, None),
        P(AXES, None, None),
        P(grp, blk, None),
        P(grp, None, blk),
        P(AXES, None, None),
        P(AXES, None, None),
        P(blk, None, None),
        P(AXES),
    )
    return jax.shard_map(
        body, mesh=fine, in_specs=in_specs, out_specs=P(AXES, None, None, None), check_vma=False
    )
```
